32 devices in a mesh: groups: 2 (over y), ctx: 4 (over z), exp: 4 (over x, core), rep: 1.
Axes of the slice: x: 2, y: 2, z: 4, core: 2. Of those that a mesh axis runs over, the one named last changes fastest.
Arguments:
- queries: bfloat16 [2, 256, 4096], P('groups', 'ctx', ('exp', 'rep')), parts along dimension 0, may hold values from -16.25 to 16.25
- pages: bfloat16 [2, 2304, 2, 512], P('groups', 'ctx', None, 'exp'), parts along dimension 0, may hold values from -5.2 to 5.2
- cached_lengths: int32 [2, 4], P('groups'), parts along dimension 0, may hold values from 128 to 512
- residual_in: bfloat16 [2, 256, 2048], P('groups', ('ctx', 'exp')), parts along dimension 0, may hold values from -2.390625 to 2.390625
- out_weight: bfloat16 [4096, 2048], P(('exp', 'rep')), may hold values from -0.09375 to 0.09375
- norm_gain: float32 [2048], replicated, may hold values from 0.1 to 1.9
- expert_ids: int32 [2, 256, 8], P('groups', ('ctx', 'exp')), parts along dimension 0, may hold values from 0 to 15, all different within a row; in each aligned block of 16 rows (0 to 15, 16 to 31, ..., all dimensions but the last counted through in order) at most 8 rows name the same one
- route_scores: float32 [2, 256, 8], P('groups', ('ctx', 'exp')), parts along dimension 0, may hold values from 0.05 to 1
- expert_input: bfloat16 [16, 2048, 2, 384], P(('ctx', 'exp'), None, None, 'rep'), may hold values from -0.125 to 0.125
- expert_output: bfloat16 [16, 384, 2048], P(('ctx', 'exp'), 'rep'), may hold values from -0.3125 to 0.3125
Outputs:
- context: bfloat16 [2, 256, 4096], P('groups', 'ctx', ('exp', 'rep')), parts along dimension 0
- layer_out: bfloat16 [2, 256, 2048], P('groups', ('ctx', 'exp', 'rep')), parts along dimension 0
The draws below stay inside these ranges and needn't reach their ends.
There are 2 independent parts, one for each index of `groups`. The reference program is written for one: setup_inputs(seed, part) draws one part's arguments, and reference() takes and returns one part's arrays. A program takes and returns all parts, laid end to end along the dimension named above; an argument that names none is the same for every part. Nothing has to cross between parts.
Inputs may be any that keep to these rules, and one draw needn't show every extreme that they name: `expert_ids`: in every aligned block of 16 positions of one request, no expert is named by more than 8 of the block's rows, and in some blocks one expert by exactly 8; the 8 experts of a row differ.
All inputs are finite; a program needn't handle non-finite values.
Results may differ from the reference program's by a relative error of at most 0.015.
Values may be sent and summed in bfloat16 or wider, within the bound.
No kernel may reach another device: no remote copies, remote signals or barrier semaphores. Data moves between devices by JAX's collectives and lax.ppermute only.
A program may use at most 128 MiB of HBM per device.

```python
import math
import jax
import jax.numpy as jnp
import numpy as np
from jax import lax

D = 2048
HEADS = 32
KV_HEADS = 4
HEAD = 128
TOPK = 8
EXPERT_FF = 384
REQS = 1
FRESH_DEV = 64
SLAB = 512
FRESH = 256
PAGE = 576
PAGE_COUNT = 4
PAGES_LEN = 2304
EXPERTS = 16
TOK_BLK = 16
MOST = 8
SPLITS = 1


def draw_queries(key, part):
    values = 2.0 * jax.random.normal(jax.random.fold_in(key, 11), (REQS, FRESH, HEADS * HEAD), jnp.float32)
    values = jnp.clip(values, -8.0, 8.0)
    return values.astype(jnp.bfloat16)


def draw_pages(key, part):
    values = 1.3 * jax.random.normal(jax.random.fold_in(key, 12), (REQS, PAGES_LEN, 2, KV_HEADS * HEAD), jnp.float32)
    values = jnp.clip(values, -5.2, 5.2)
    return values.astype(jnp.bfloat16)


def draw_cached_lengths(key, part):
    slab_count = PAGES_LEN // PAGE
    lowest = max(2, SLAB // 4)
    drawn_lengths = jax.random.randint(jax.random.fold_in(key, 13), (REQS, slab_count), lowest, SLAB + 1)
    full_pick = jax.random.randint(jax.random.fold_in(key, 14), (REQS, 1), 0, slab_count)
    filled = jnp.where(jnp.arange(slab_count, dtype=jnp.int32)[None, :] == full_pick, SLAB, drawn_lengths)
    return filled.astype(jnp.int32)


def level_of(stream_key, shape, pieces, least, top_value):
    loudness, own = 1.0, jax.random.fold_in(stream_key, 6)
    for position, parts in pieces:
        steps = jnp.exp(jax.random.uniform(jax.random.fold_in(own, position), (parts,), jnp.float32, least / len(pieces), top_value / len(pieces)))
        loudness = loudness * jnp.repeat(steps, shape[position] // parts).reshape([-1 if axis == position else 1 for axis in range(len(shape))])
    return loudness


def routed_block(rng, own, number, rows, count, top, bound, lean):
    ranking = jax.random.permutation(rng, count)
    heavy_load, ordinary = shares(count, rows * top, bound, lean, True), shares(count, rows * top, bound, lean, False)
    places = jnp.arange(count)

    def named(tallies, turn):
        used = int((tallies > 0).sum())
        fixed = max(1, used // 4)
        shifted = fixed + (places - fixed + turn * (used - fixed)) % max(1, count - fixed)
        return jnp.zeros((count,), jnp.int32).at[ranking[jnp.where(places < fixed, places, shifted)]].set(jnp.asarray(tallies, jnp.int32))

    tallies = jnp.where(number % 4 == 0, named(heavy_load, number // 4), named(ordinary, number - number // 4 - 1))
    mixed = jax.random.permutation(jax.random.fold_in(own, 3), count)
    donor, taker = mixed[0:count // 2 * 2:2], mixed[1:count // 2 * 2:2]
    room = jnp.minimum(tallies[donor] - 1, bound - tallies[taker]) // 2
    room = jnp.where((donor == ranking[0]) | (taker == ranking[0]) | (tallies[taker] == 0), 0, jnp.maximum(room, 0))
    shifted = jax.random.randint(jax.random.fold_in(own, 4), (count // 2,), 0, 1 << 20) % (room + 1)
    tallies = tallies.at[donor].add(-shifted).at[taker].add(shifted)
    labels = jnp.searchsorted(jnp.cumsum(tallies), jnp.arange(rows * top), side="right").astype(jnp.int32)
    listing = labels.reshape(top, rows).T
    listing = listing[jax.random.permutation(jax.random.fold_in(own, 1), rows)]
    turn = jax.random.randint(jax.random.fold_in(own, 2), (rows, 1), 0, top)
    return jnp.take_along_axis(listing, (jnp.arange(top)[None, :] + turn) % top, axis=1)


def shares(number_of, total, reach, skew, full):
    weights = [(1 << 20) // math.isqrt(standing ** skew) + 1 for standing in range(1, number_of + 1)]
    largest = reach if full else min(reach, max(-(-total // number_of), total * weights[0] // sum(weights)))
    least = 1 if total - largest >= number_of - 1 else 0
    given, surplus = [largest] + [least] * (number_of - 1), total - largest - least * (number_of - 1)
    while surplus > 0:
        free = [i for i in range(1, number_of) if given[i] < largest] or [i for i in range(1, number_of) if given[i] < reach]
        pool, left = sum([weights[i] for i in free]), surplus
        for i in free:
            more = min(reach - given[i], max(1, left * weights[i] // pool), surplus)
            given[i] = given[i] + more
            surplus = surplus - more
    return np.array(given)


def bell_draw(rng, dims, scale, limit, pieces=(), kind=jnp.bfloat16):
    drawn = jax.random.normal(rng, dims, jnp.float32) * scale
    if len(pieces) > 0:
        drawn = level_of(rng, dims, pieces, -0.22, 0.18) * drawn
    return jnp.clip(drawn, min=-limit, max=limit).astype(kind)


def setup_inputs(seed: int = 0, part: int = 0) -> dict:
    key_list = jax.random.split(jax.random.key(seed), 11)
    own_keys = jax.random.split(jax.random.fold_in(key_list[10], part), 11)
    queries = draw_queries(jax.random.fold_in(jax.random.fold_in(key_list[10], part), 71), part)
    pages = draw_pages(jax.random.fold_in(jax.random.fold_in(key_list[10], part), 71), part)
    cached_lengths = draw_cached_lengths(jax.random.fold_in(jax.random.fold_in(key_list[10], part), 71), part)
    residual_in = bell_draw(own_keys[3], (REQS, FRESH, D), 0.4, 2.390625, ((1, 16),))
    out_weight = bell_draw(key_list[4], (HEADS * HEAD, D), (HEADS * HEAD) ** -0.5, 0.09375, ((0, 4),))
    norm_gain = jnp.clip(1.0 + 0.18 * jax.random.normal(key_list[5], (D,), jnp.float32), 0.1, 1.9)
    expert_ids_keys = jax.random.split(jax.random.fold_in(own_keys[6], 1), REQS * FRESH // TOK_BLK)
    expert_ids_turns = jax.random.permutation(jax.random.fold_in(own_keys[6], 3), REQS * FRESH // TOK_BLK)
    expert_ids = jax.vmap(lambda own, number: routed_block(jax.random.fold_in(own_keys[6], 2), own, number, TOK_BLK, EXPERTS, TOPK, MOST, 2))(expert_ids_keys, expert_ids_turns).reshape((REQS, FRESH, TOPK))
    route_scores = jnp.clip(jnp.exp(math.log(1.0) - 2.9957323 * jax.random.uniform(own_keys[7], (REQS, FRESH, TOPK), jnp.float32) ** level_of(own_keys[7], (REQS, FRESH, TOPK), ((1, 16),), -0.2, 0.2)), 0.05, 1.0)
    expert_input = bell_draw(key_list[8], (EXPERTS, D, 2, EXPERT_FF), D ** -0.5, 0.125, ((0, 16),))
    expert_output = bell_draw(key_list[9], (EXPERTS, EXPERT_FF, D), EXPERT_FF ** -0.5, 0.3125, ((0, 16),))
    return dict(queries=queries, pages=pages, cached_lengths=cached_lengths, residual_in=residual_in, out_weight=out_weight, norm_gain=norm_gain, expert_ids=expert_ids, route_scores=route_scores, expert_input=expert_input, expert_output=expert_output)


floor_value = -1e+30
norm_epsilon = 1e-06

def normalize(hidden, norm_gain):
    widened = hidden.astype(jnp.float32)
    mean_square = lax.optimization_barrier(jnp.mean(widened * widened, axis=-1, keepdims=True))
    return (widened * lax.rsqrt(mean_square + norm_epsilon) * norm_gain).astype(jnp.bfloat16)

def expert_apply(normed_rows, weight_in, weight_out):
    inner_rows = jnp.einsum('nd,dgh->ngh', normed_rows.astype(jnp.float32), weight_in.astype(jnp.float32))
    activated = (jax.nn.silu(inner_rows[:, 0]) * inner_rows[:, 1]).astype(jnp.bfloat16)
    part_width = EXPERT_FF // SPLITS
    result = jnp.zeros((normed_rows.shape[0], D), jnp.float32)
    for portion in range(SPLITS):
        lower = portion * part_width
        partial_value = jnp.dot(activated[:, lower:lower + part_width], weight_out[lower:lower + part_width], preferred_element_type=jnp.float32)
        rounded_part = lax.optimization_barrier(partial_value.astype(jnp.bfloat16))
        result = result + rounded_part.astype(jnp.float32)
    return result

def reference(queries, pages, cached_lengths, residual_in, out_weight, norm_gain, expert_ids, route_scores, expert_input, expert_output):
    group_size = HEADS // KV_HEADS
    scaling = HEAD ** (-0.5)
    zero_index = jnp.int32(0)
    row_index = jnp.arange(PAGES_LEN, dtype=jnp.int32)
    page_number = row_index // PAGE
    offset = row_index - page_number * PAGE
    query_positions = jnp.arange(FRESH, dtype=jnp.int32)

    def one_head(flat_index):
        flat_index = flat_index.astype(jnp.int32)
        request = (flat_index // HEADS).astype(jnp.int32)
        head_number = (flat_index - request * HEADS).astype(jnp.int32)
        pair_head = (head_number // group_size).astype(jnp.int32)
        query_rows = lax.dynamic_slice(queries, (request, zero_index, (head_number * HEAD).astype(jnp.int32)), (1, FRESH, HEAD))[0]
        page_rows = lax.dynamic_slice(pages, (request, zero_index, zero_index, (pair_head * HEAD).astype(jnp.int32)), (1, PAGES_LEN, 2, HEAD))[0]
        lengths_row = lax.dynamic_slice(cached_lengths, (request, zero_index), (1, PAGE_COUNT))[0]
        live_length = lengths_row[page_number]
        in_cache = (offset < SLAB) & (offset < live_length)
        fresh_position = page_number * FRESH_DEV + offset - SLAB
        in_fresh = (offset >= SLAB)[None, :] & (fresh_position[None, :] <= query_positions[:, None])
        allowed = in_cache[None, :] | in_fresh
        scores = jnp.dot(query_rows, page_rows[:, 0].T, preferred_element_type=jnp.float32) * scaling
        masked = jnp.where(allowed, scores, floor_value)
        peaks = lax.optimization_barrier(jnp.max(masked, axis=1, keepdims=True))
        weights = jnp.where(allowed, jnp.exp(masked - peaks), 0.0)
        totals = lax.optimization_barrier(jnp.sum(weights, axis=1, keepdims=True))
        summed = jnp.dot(weights.astype(jnp.bfloat16), page_rows[:, 1], preferred_element_type=jnp.float32)
        return (summed / totals).astype(jnp.bfloat16)
    heads_out = lax.map(one_head, jnp.arange(REQS * HEADS, dtype=jnp.int32))
    context = heads_out.reshape(REQS, HEADS, FRESH, HEAD).transpose(0, 2, 1, 3).reshape(REQS, FRESH, HEADS * HEAD)
    projected = jnp.dot(context.reshape(REQS * FRESH, HEADS * HEAD), out_weight, preferred_element_type=jnp.float32).reshape(REQS, FRESH, D)
    hidden = (residual_in.astype(jnp.float32) + projected).astype(jnp.bfloat16)
    normed = normalize(hidden, norm_gain)
    token_count = REQS * FRESH
    flat_normed = normed.reshape(token_count, D)
    flat_ids = expert_ids.reshape(-1).astype(jnp.int32)
    combine = (route_scores / lax.optimization_barrier(jnp.sum(route_scores, axis=2, keepdims=True))).astype(jnp.bfloat16)
    combine = lax.optimization_barrier(combine).astype(jnp.float32).reshape(-1)
    sorted_rows = jnp.argsort(flat_ids, stable=True).astype(jnp.int32)
    counts = lax.optimization_barrier(jnp.sum((flat_ids[:, None] == jnp.arange(EXPERTS, dtype=jnp.int32)[None, :]).astype(jnp.int32), axis=0))
    starts = (jnp.cumsum(counts) - counts).astype(jnp.int32)
    row_limit = min(token_count * TOPK, token_count // TOK_BLK * MOST)
    padded = jnp.concatenate([sorted_rows, jnp.zeros((row_limit,), jnp.int32)])

    def add_expert(expert, mixture):
        picked = lax.dynamic_slice(padded, (starts[expert].astype(jnp.int32),), (row_limit,))
        alive_rows = jnp.arange(row_limit, dtype=jnp.int32) < counts[expert]
        tokens = picked // TOPK
        outputs = expert_apply(flat_normed[tokens], expert_input[expert], expert_output[expert])
        scaled = outputs * jnp.where(alive_rows, combine[picked], 0.0)[:, None]
        return mixture.at[tokens].add(scaled)
    mixture = lax.fori_loop(0, EXPERTS, add_expert, jnp.zeros((token_count, D), jnp.float32))
    layer_out = (hidden.astype(jnp.float32).reshape(token_count, D) + mixture).astype(jnp.bfloat16).reshape(REQS, FRESH, D)
    return (context, layer_out)
```

```python
import functools

import jax
import jax.numpy as jnp
from jax import lax
from jax.experimental import pallas as pl
from jax.experimental.pallas import tpu as pltpu
from jax.sharding import PartitionSpec as P

HEAD = 128

floor_value = -1e30
norm_epsilon = 1e-06


def normalize(hidden, norm_gain):
    widened = hidden.astype(jnp.float32)
    mean_square = jnp.mean(widened * widened, axis=-1, keepdims=True)
    return (widened * lax.rsqrt(mean_square + norm_epsilon) * norm_gain).astype(jnp.bfloat16)


def partner(index, step, count):
    if count & (count - 1) == 0:
        return index ^ step
    return lax.rem(index + step, count)


def swap(value, axis, step):
    count = lax.axis_size(axis)
    pow2 = count & (count - 1) == 0
    pairs = [(i, (i ^ step) if pow2 else (i + step) % count) for i in range(count)]
    return lax.ppermute(value, axis, pairs)


def shift(value, axis, step):
    count = lax.axis_size(axis)
    return lax.ppermute(value, axis, [(i, (i + step) % count) for i in range(count)])


def stack_heads(queries):
    heads = queries.shape[1] // HEAD
    return jnp.concatenate(
        [queries[:, h * HEAD : (h + 1) * HEAD] for h in range(heads)], axis=0
    )


def page_partial(stacked, keys, values, page, length, place, fresh_block):
    rows, page_size = stacked.shape[0], keys.shape[0]
    slab_size = page_size - fresh_block
    scores = lax.dot_general(
        stacked, keys, (((1,), (1,)), ((), ())), preferred_element_type=jnp.float32
    )
    offset = lax.broadcasted_iota(jnp.int32, (fresh_block, page_size), 1)
    position = place * fresh_block + lax.broadcasted_iota(
        jnp.int32, (fresh_block, page_size), 0
    )
    in_cache = (offset < slab_size) & (offset < length)
    in_fresh = (offset >= slab_size) & (page * fresh_block + offset - slab_size <= position)
    bias = jnp.where(in_cache | in_fresh, 0.0, floor_value)
    masked = scores + jnp.concatenate([bias] * (rows // fresh_block), axis=0)
    peak = jnp.max(masked, axis=1, keepdims=True)
    weights = jnp.exp((masked - peak) * (HEAD**-0.5))
    total = jnp.sum(weights, axis=1, keepdims=True)
    summed = jnp.dot(weights.astype(jnp.bfloat16), values, preferred_element_type=jnp.float32)
    return peak, total, summed


def merge(first, second):
    peak = jnp.maximum(first[0], second[0])
    scale_first = jnp.exp((first[0] - peak) * (HEAD**-0.5))
    scale_second = jnp.exp((second[0] - peak) * (HEAD**-0.5))
    return (
        peak,
        first[1] * scale_first + second[1] * scale_second,
        first[2] * scale_first + second[2] * scale_second,
    )


def early_kernel(count, fresh_block, info, queries, *refs):
    pages, (peak_out, total_out, summed_out) = refs[: 2 * count], refs[2 * count :]
    stacked = stack_heads(queries[...])
    state = None
    for number in range(count):
        part = page_partial(
            stacked,
            pages[2 * number][...],
            pages[2 * number + 1][...],
            info[1 + 2 * number],
            info[2 + 2 * number],
            info[0],
            fresh_block,
        )
        state = part if state is None else merge(state, part)
    peak_out[...] = state[0]
    total_out[...] = state[1]
    summed_out[...] = state[2]


def late_kernel(fresh_block, info, queries, keys, values, peak, total, summed, context_out):
    stacked = stack_heads(queries[...])
    part = page_partial(
        stacked, keys[...], values[...], info[1], info[2], info[0], fresh_block
    )
    state = merge((peak[...], total[...], summed[...]), part)
    result = (state[2] / state[1]).astype(jnp.bfloat16)
    for h in range(result.shape[0] // fresh_block):
        context_out[:, h * HEAD : (h + 1) * HEAD] = result[
            h * fresh_block : (h + 1) * fresh_block
        ]


def whole_specs(count):
    return [pl.BlockSpec(memory_space=pltpu.VMEM)] * count


def attention(queries, pages, lengths):
    fresh_block, width = queries.shape
    heads = width // HEAD
    stacked_rows = heads * fresh_block
    place = lax.axis_index("ctx")
    count = lax.axis_size("ctx")
    own_keys, own_values = pages[:, 0], pages[:, 1]
    held = [(place, own_keys, own_values)]
    from_left, from_right = (own_keys, own_values), (own_keys, own_values)
    for step in range(1, (count - 1) // 2 + 1):
        from_left = tuple(shift(part, "ctx", 1) for part in from_left)
        from_right = tuple(shift(part, "ctx", -1) for part in reversed(from_right))[::-1]
        held.append((lax.rem(place - step + count, count), *from_left))
        held.append((lax.rem(place + step, count), *from_right))
    if count % 2 == 0:
        last = (
            lax.rem(place + count // 2, count),
            shift(from_left[0], "ctx", 1),
            shift(from_right[1], "ctx", -1),
        )
    else:
        last = held.pop()

    def info_of(parts):
        numbers = [place]
        for page, _, _ in parts:
            numbers += [page, lax.dynamic_index_in_dim(lengths, page, 0, keepdims=False)]
        return jnp.stack(numbers).astype(jnp.int32)

    smem = pl.BlockSpec(memory_space=pltpu.SMEM)
    column = jax.ShapeDtypeStruct((stacked_rows, 1), jnp.float32)
    limit = pltpu.CompilerParams(vmem_limit_bytes=32 * 1024 * 1024)
    page_flops = 4 * stacked_rows * pages.shape[0] * HEAD

    state = None
    for start in range(0, len(held), 3):
        group = held[start : start + 3]
        operands = [part for _, keys, values in group for part in (keys, values)]
        partial_state = pl.pallas_call(
            functools.partial(early_kernel, len(group), fresh_block),
            out_shape=(column, column, jax.ShapeDtypeStruct((stacked_rows, HEAD), jnp.float32)),
            in_specs=[smem] + whole_specs(1 + len(operands)),
            out_specs=tuple(whole_specs(3)),
            compiler_params=limit,
            cost_estimate=pl.CostEstimate(
                flops=len(group) * page_flops, bytes_accessed=2 << 20, transcendentals=0
            ),
        )(info_of(group), queries, *operands)
        state = partial_state if state is None else merge(state, partial_state)
    return pl.pallas_call(
        functools.partial(late_kernel, fresh_block),
        out_shape=jax.ShapeDtypeStruct(queries.shape, jnp.bfloat16),
        in_specs=[smem] + whole_specs(6),
        out_specs=whole_specs(1)[0],
        compiler_params=limit,
        cost_estimate=pl.CostEstimate(
            flops=page_flops, bytes_accessed=1 << 20, transcendentals=0
        ),
    )(info_of([last]), queries, last[1], last[2], *state)


def scatter_sum(blocks):
    count = lax.axis_size("exp")
    place = lax.axis_index("exp")
    pick = lambda index: lax.dynamic_index_in_dim(blocks, index, 0, keepdims=False)
    arrived = [
        swap(pick(partner(place, step, count)), "exp", step) for step in reversed(range(1, count))
    ]
    total = pick(place).astype(jnp.float32)
    for part in arrived:
        total = total + part.astype(jnp.float32)
    return total


def exp_strides():
    count = lax.axis_size("exp")
    if count & (count - 1) == 0:
        return [1 << bit for bit in range(count.bit_length() - 1)]
    return None


def gather_rows(rows):
    count = lax.axis_size("ctx")
    column = jnp.stack([rows] + [shift(rows, "ctx", step) for step in range(1, count)])
    strides = exp_strides()
    if strides is None:
        parts = [column] + [swap(column, "exp", step) for step in range(1, lax.axis_size("exp"))]
        return jnp.concatenate(parts)
    held = [column]
    for stride in reversed(strides):
        held = held + [swap(part, "exp", stride) for part in held]
    return jnp.concatenate(held)


def give_back(blocks):
    count = lax.axis_size("ctx")
    strides = exp_strides()
    groups = blocks.shape[0] // count
    held = [blocks[i * count : (i + 1) * count] for i in range(groups)]
    if strides is None:
        size = lax.axis_size("exp")
        total = held[0].astype(jnp.float32)
        for step in range(1, size):
            total = total + swap(held[step], "exp", size - step).astype(jnp.float32)
        column = total
    else:
        for stride in strides:
            half = len(held) // 2
            arrived = [swap(part.astype(jnp.bfloat16), "exp", stride) for part in held[half:]]
            held = [
                keep.astype(jnp.float32) + new.astype(jnp.float32)
                for keep, new in zip(held[:half], arrived)
            ]
        column = held[0].astype(jnp.float32)
    sent = column.astype(jnp.bfloat16)
    total = column[0]
    for step in range(1, count):
        total = total + shift(sent[step], "ctx", -step).astype(jnp.float32)
    return total


def per_device(
    queries,
    pages,
    cached_lengths,
    residual_in,
    out_weight,
    norm_gain,
    expert_ids,
    route_scores,
    expert_input,
    expert_output,
):
    requests, fresh_block, query_width = queries.shape
    core_place = lax.axis_index("rep")
    rep_count = lax.axis_size("rep")
    exp_count = lax.axis_size("exp")
    expert_count = lax.axis_size("ctx") * exp_count
    token_block, model_width = residual_in.shape[1:]
    token_count = requests * token_block
    expert = lax.axis_index("ctx") * exp_count + lax.axis_index("exp")

    combine = (route_scores / jnp.sum(route_scores, axis=2, keepdims=True)).astype(jnp.bfloat16)
    named = expert_ids[..., None] == jnp.arange(expert_count, dtype=jnp.int32)
    dense = jnp.sum(jnp.where(named, combine[..., None], 0).astype(jnp.float32), axis=2)
    dense = dense.astype(jnp.bfloat16).reshape(token_count, expert_count)
    all_dense = gather_rows(dense).reshape(-1, expert_count)
    own_column = jnp.arange(expert_count, dtype=jnp.int32) == expert
    own_weight = jnp.sum(jnp.where(own_column, all_dense.astype(jnp.float32), 0.0), axis=1)

    context = jnp.stack(
        [attention(queries[r], pages[r], cached_lengths[r]) for r in range(requests)]
    )
    projected = jnp.dot(
        context.reshape(requests * fresh_block, query_width),
        out_weight,
        preferred_element_type=jnp.float32,
    ).astype(jnp.bfloat16)
    blocks = projected.reshape(requests, exp_count, token_block, model_width)
    blocks = blocks.transpose(1, 0, 2, 3)
    share = scatter_sum(blocks)
    share_size = token_block // rep_count
    if rep_count > 1:
        share = lax.psum_scatter(
            share.astype(jnp.bfloat16), "rep", scatter_dimension=1, tiled=True
        ).astype(jnp.float32)
    own_residual = lax.dynamic_slice_in_dim(residual_in, core_place * share_size, share_size, 1)
    own_hidden = (own_residual.astype(jnp.float32) + share).astype(jnp.bfloat16)
    normed = normalize(own_hidden, norm_gain)
    if rep_count > 1:
        normed = lax.all_gather(normed, "rep", axis=1, tiled=True)

    arrived = gather_rows(normed.reshape(token_count, model_width))
    inner = jnp.einsum(
        "nd,dgh->ngh",
        arrived.reshape(-1, model_width),
        expert_input[0],
        preferred_element_type=jnp.float32,
    )
    activated = (jax.nn.silu(inner[:, 0]) * inner[:, 1]).astype(jnp.bfloat16)
    piece = jnp.dot(activated, expert_output[0], preferred_element_type=jnp.float32)
    piece = piece.astype(jnp.bfloat16).astype(jnp.float32)
    scaled = (piece * own_weight[:, None]).astype(jnp.bfloat16)
    mixture = give_back(scaled.reshape(arrived.shape)).reshape(requests, token_block, model_width)
    if rep_count > 1:
        mixture = lax.psum_scatter(
            mixture.astype(jnp.bfloat16), "rep", scatter_dimension=1, tiled=True
        ).astype(jnp.float32)
    layer_out = (own_hidden.astype(jnp.float32) + mixture).astype(jnp.bfloat16)
    return (context, layer_out)


def solution(mesh):
    in_specs = (
        P("groups", "ctx", ("exp", "rep")),
        P("groups", "ctx", None, "exp"),
        P("groups", None),
        P("groups", ("ctx", "exp"), None),
        P(("exp", "rep"), None),
        P(),
        P("groups", ("ctx", "exp"), None),
        P("groups", ("ctx", "exp"), None),
        P(("ctx", "exp"), None, None, "rep"),
        P(("ctx", "exp"), "rep", None),
    )
    out_specs = (P("groups", "ctx", ("exp", "rep")), P("groups", ("ctx", "exp", "rep"), None))
    return jax.shard_map(
        per_device, mesh=mesh, in_specs=in_specs, out_specs=out_specs, check_vma=False
    )
```

```python
import functools
import math

import jax
import jax.numpy as jnp
from jax import lax
from jax.experimental import pallas as pl
from jax.experimental.pallas import tpu as pltpu
from jax.sharding import PartitionSpec as P

HEAD = 128

floor_value = -1e30
norm_epsilon = 1e-06


def normalize(hidden, norm_gain):
    widened = hidden.astype(jnp.float32)
    mean_square = jnp.mean(widened * widened, axis=-1, keepdims=True)
    return (widened * lax.rsqrt(mean_square + norm_epsilon) * norm_gain).astype(jnp.bfloat16)


def strides(count):
    assert count & (count - 1) == 0
    return [1 << bit for bit in reversed(range(count.bit_length() - 1))]


def swap(value, axis, stride):
    return lax.ppermute(value, axis, [(i, i ^ stride) for i in range(lax.axis_size(axis))])


def shift(value, axis, step):
    count = lax.axis_size(axis)
    return lax.ppermute(value, axis, [(i, (i + step) % count) for i in range(count)])


def whole_specs(count):
    return [pl.BlockSpec(memory_space=pltpu.VMEM)] * count


SMEM_SPEC = pl.BlockSpec(memory_space=pltpu.SMEM)
LIMIT = pltpu.CompilerParams(vmem_limit_bytes=16 * 1024 * 1024)


def stack_heads(queries):
    heads = queries.shape[1] // HEAD
    return jnp.concatenate(
        [queries[:, h * HEAD : (h + 1) * HEAD] for h in range(heads)], axis=0
    )


def page_partial(stacked, keys, values, page, length, place, fresh_block):
    rows, page_size = stacked.shape[0], keys.shape[0]
    slab_size = page_size - fresh_block
    scores = lax.dot_general(
        keys, stacked, (((1,), (1,)), ((), ())), preferred_element_type=jnp.float32
    )
    lanes = HEAD if HEAD % fresh_block == 0 and rows % HEAD == 0 else rows
    offset = lax.broadcasted_iota(jnp.int32, (slab_size, lanes), 0)
    fresh = page * fresh_block + lax.broadcasted_iota(jnp.int32, (fresh_block, lanes), 0)
    lane = lax.broadcasted_iota(jnp.int32, (fresh_block, lanes), 1)
    position = place * fresh_block + lax.rem(lane, fresh_block)
    bias = jnp.concatenate(
        [
            jnp.where(offset < length, 0.0, floor_value),
            jnp.where(fresh <= position, 0.0, floor_value),
        ],
        axis=0,
    )
    masked = scores + jnp.concatenate([bias] * (rows // lanes), axis=1)
    peak = jnp.max(masked, axis=0, keepdims=True)
    weights = jnp.exp((masked - peak) * (HEAD**-0.5))
    total = jnp.sum(weights, axis=0, keepdims=True)
    summed = lax.dot_general(
        values,
        weights.astype(jnp.bfloat16),
        (((0,), (0,)), ((), ())),
        preferred_element_type=jnp.float32,
    )
    return peak, total, summed


def merge(first, second):
    peak = jnp.maximum(first[0], second[0])
    scale_first = jnp.exp((first[0] - peak) * (HEAD**-0.5))
    scale_second = jnp.exp((second[0] - peak) * (HEAD**-0.5))
    return (
        peak,
        first[1] * scale_first + second[1] * scale_second,
        first[2] * scale_first + second[2] * scale_second,
    )


def page_at(offset):
    count = lax.axis_size("ctx")
    return lax.rem(lax.axis_index("ctx") + offset + count, count)


def early_kernel(offsets, fresh_block, lengths, queries, *refs):
    count = len(offsets)
    pages, (peak_out, total_out, summed_out) = refs[: 2 * count], refs[2 * count :]
    stacked = stack_heads(queries[...])
    place = lax.axis_index("ctx")
    state = None
    for number, offset in enumerate(offsets):
        page = page_at(offset)
        part = page_partial(
            stacked,
            pages[2 * number][...],
            pages[2 * number + 1][...],
            page,
            lengths[page],
            place,
            fresh_block,
        )
        state = part if state is None else merge(state, part)
    peak_out[...] = state[0]
    total_out[...] = state[1]
    summed_out[...] = state[2]


def late_kernel(
    offset,
    fresh_block,
    lengths,
    queries,
    keys,
    values,
    peak,
    total,
    summed,
    weight_hbm,
    context_out,
    own_out,
    *rest,
):
    sent_outs, (weight, blocks, sem) = rest[:-3], rest[-3:]
    copy = pltpu.make_async_copy(weight_hbm, weight, sem)
    copy.start()
    page = page_at(offset)
    part = page_partial(
        stack_heads(queries[...]),
        keys[...],
        values[...],
        page,
        lengths[page],
        lax.axis_index("ctx"),
        fresh_block,
    )
    state = merge((peak[...], total[...], summed[...]), part)
    result = jnp.transpose(state[2] / state[1])
    context = jnp.concatenate(
        [
            result[h * fresh_block : (h + 1) * fresh_block]
            for h in range(result.shape[0] // fresh_block)
        ],
        axis=1,
    ).astype(jnp.bfloat16)
    context_out[...] = context
    copy.wait()
    blocks[...] = jnp.dot(context, weight[...], preferred_element_type=jnp.float32)
    place = lax.axis_index("exp")
    size = own_out.shape[0]
    pick = lambda index: blocks[pl.ds(pl.multiple_of(index * size, size), size), :]
    own_out[...] = pick(place)
    for step, out in enumerate(sent_outs, 1):
        out[...] = pick(place ^ step).astype(jnp.bfloat16)


def attention(queries, pages, lengths, out_weight, token_block):
    fresh_block, width = queries.shape
    rows = width // HEAD * fresh_block
    count = lax.axis_size("ctx")
    exp_count = lax.axis_size("exp")
    model_width = out_weight.shape[1]
    own_keys, own_values = pages[:, 0], pages[:, 1]
    held = [(0, own_keys, own_values)]
    left_keys, left_values = own_keys, own_values
    right_keys, right_values = own_keys, own_values
    for step in range(1, (count - 1) // 2 + 1):
        left_keys = shift(left_keys, "ctx", 1)
        right_values = shift(right_values, "ctx", -1)
        left_values = shift(left_values, "ctx", 1)
        right_keys = shift(right_keys, "ctx", -1)
        held.append((-step, left_keys, left_values))
        held.append((step, right_keys, right_values))
    if count % 2 == 0:
        last = (count // 2, shift(left_keys, "ctx", 1), shift(right_values, "ctx", -1))
    else:
        last = held.pop()
    page_flops = 4 * rows * pages.shape[0] * HEAD
    line = jax.ShapeDtypeStruct((1, rows), jnp.float32)
    state = None
    for start in range(0, len(held), 3):
        group = held[start : start + 3]
        operands = [part for _, keys, values in group for part in (keys, values)]
        partial_state = pl.pallas_call(
            functools.partial(early_kernel, [offset for offset, _, _ in group], fresh_block),
            out_shape=(line, line, jax.ShapeDtypeStruct((HEAD, rows), jnp.float32)),
            in_specs=[SMEM_SPEC] + whole_specs(1 + len(operands)),
            out_specs=tuple(whole_specs(3)),
            compiler_params=LIMIT,
            cost_estimate=pl.CostEstimate(
                flops=len(group) * page_flops, bytes_accessed=2 << 20, transcendentals=0
            ),
        )(lengths, queries, *operands)
        state = partial_state if state is None else merge(state, partial_state)
    block = jax.ShapeDtypeStruct((token_block, model_width), jnp.bfloat16)
    outs = pl.pallas_call(
        functools.partial(late_kernel, last[0], fresh_block),
        out_shape=(
            jax.ShapeDtypeStruct(queries.shape, jnp.bfloat16),
            jax.ShapeDtypeStruct(block.shape, jnp.float32),
        )
        + (block,) * (exp_count - 1),
        in_specs=[SMEM_SPEC] + whole_specs(6) + [pl.BlockSpec(memory_space=pl.ANY)],
        out_specs=tuple(whole_specs(1 + exp_count)),
        scratch_shapes=[
            pltpu.VMEM(out_weight.shape, jnp.bfloat16),
            pltpu.VMEM((fresh_block, model_width), jnp.float32),
            pltpu.SemaphoreType.DMA,
        ],
        compiler_params=LIMIT,
        cost_estimate=pl.CostEstimate(
            flops=page_flops + 2 * fresh_block * width * model_width,
            bytes_accessed=6 << 20,
            transcendentals=0,
        ),
    )(lengths, queries, last[1], last[2], *state, out_weight)
    return outs[0], outs[1], outs[2:], left_keys


def split_kernel(tile, source, target):
    half = source.shape[3]

    def body(number, carry):
        rows = pl.ds(pl.multiple_of(number * tile, tile), tile)
        target[rows, :half] = source[0, rows, 0, :]
        target[rows, half:] = source[0, rows, 1, :]
        return carry

    lax.fori_loop(0, source.shape[1] // tile, body, 0)


def split_gate_up(expert_input):
    _, width, _, hidden = expert_input.shape
    return pl.pallas_call(
        functools.partial(split_kernel, math.gcd(width, 128)),
        out_shape=jax.ShapeDtypeStruct((width, 2 * hidden), jnp.bfloat16),
        in_specs=whole_specs(1),
        out_specs=whole_specs(1)[0],
        compiler_params=LIMIT,
        cost_estimate=pl.CostEstimate(flops=0, bytes_accessed=6 << 20, transcendentals=0),
    )(expert_input)


def expert_kernel(*refs):
    pieces, (gate_up, down, scale, keep_out, send_out) = refs[:-5], refs[-5:]
    rows = jnp.concatenate([piece[...] for piece in pieces], axis=0)
    inner = jnp.dot(rows, gate_up[...], preferred_element_type=jnp.float32)
    hidden = inner.shape[1] // 2
    gate, up = inner[:, :hidden], inner[:, hidden:]
    activated = (gate / (1.0 + jnp.exp(-gate)) * up).astype(jnp.bfloat16)
    result = jnp.dot(activated, down[0], preferred_element_type=jnp.float32)
    result = result.astype(jnp.bfloat16).astype(jnp.float32) * scale[...]
    half = keep_out.shape[0]
    keep_out[...] = result[:half]
    send_out[...] = result[half:].astype(jnp.bfloat16)


def expert_apply(pieces, gate_up, down, scale):
    rows = sum(piece.shape[0] for piece in pieces)
    width, hidden = down.shape[2], down.shape[1]
    half = (rows // 2, width)
    return pl.pallas_call(
        expert_kernel,
        out_shape=(
            jax.ShapeDtypeStruct(half, jnp.float32),
            jax.ShapeDtypeStruct(half, jnp.bfloat16),
        ),
        in_specs=whole_specs(len(pieces) + 3),
        out_specs=tuple(whole_specs(2)),
        compiler_params=LIMIT,
        cost_estimate=pl.CostEstimate(
            flops=6 * rows * width * hidden, bytes_accessed=6 << 20, transcendentals=0
        ),
    )(*pieces, gate_up, down, scale)


def gather_column(rows):
    for stride in strides(lax.axis_size("ctx")):
        rows = jnp.concatenate([rows, swap(rows, "ctx", stride)], axis=0)
    return rows


def gather_pieces(rows):
    pieces = [gather_column(rows)]
    for stride in strides(lax.axis_size("exp")):
        pieces = pieces + [swap(piece, "exp", stride) for piece in pieces]
    return pieces


def give_back(keep, send):
    exchanges = [("exp", stride) for stride in reversed(strides(lax.axis_size("exp")))]
    exchanges += [("ctx", stride) for stride in reversed(strides(lax.axis_size("ctx")))]
    for number, (axis, stride) in enumerate(exchanges):
        total = keep + swap(send, axis, stride).astype(jnp.float32)
        if number + 1 == len(exchanges):
            return total
        half = total.shape[0] // 2
        keep, send = total[:half], total[half:].astype(jnp.bfloat16)


def per_device(
    queries,
    pages,
    cached_lengths,
    residual_in,
    out_weight,
    norm_gain,
    expert_ids,
    route_scores,
    expert_input,
    expert_output,
):
    requests = queries.shape[0]
    core_place = lax.axis_index("rep")
    rep_count = lax.axis_size("rep")
    exp_count = lax.axis_size("exp")
    expert_count = lax.axis_size("ctx") * exp_count
    token_block, model_width = residual_in.shape[1:]
    token_count = requests * token_block
    expert = lax.axis_index("ctx") * exp_count + lax.axis_index("exp")

    contexts, owns, sents = [], [], []
    for r in range(requests):
        context, own, sent, arrived_keys = attention(
            queries[r], pages[r], cached_lengths[r], out_weight, token_block
        )
        contexts.append(context)
        owns.append(own)
        sents.append(sent)
    context = jnp.stack(contexts)

    route_scores, expert_ids, expert_input, _ = lax.optimization_barrier(
        (route_scores, expert_ids, expert_input, arrived_keys)
    )
    combine = (route_scores / jnp.sum(route_scores, axis=2, keepdims=True)).astype(jnp.bfloat16)
    named = expert_ids[..., None] == jnp.arange(expert_count, dtype=jnp.int32)
    dense = jnp.sum(jnp.where(named, combine[..., None], 0).astype(jnp.float32), axis=2)
    dense = dense.astype(jnp.bfloat16).reshape(token_count, expert_count)
    dense = gather_column(dense)
    for stride in strides(exp_count):
        dense = jnp.concatenate([dense, swap(dense, "exp", stride)], axis=0)
    own_column = jnp.arange(expert_count, dtype=jnp.int32) == expert
    own_weight = jnp.sum(jnp.where(own_column, dense.astype(jnp.float32), 0.0), axis=1)
    own_weight = own_weight.reshape(-1, token_count)
    gate_up = split_gate_up(expert_input)

    share = jnp.stack(owns)
    for step in range(1, exp_count):
        blocks = jnp.stack([sent[step - 1] for sent in sents])
        share = share + swap(blocks, "exp", step).astype(jnp.float32)
    share_size = token_block // rep_count
    if rep_count > 1:
        share = lax.psum_scatter(
            share.astype(jnp.bfloat16), "rep", scatter_dimension=1, tiled=True
        ).astype(jnp.float32)
    own_residual = lax.dynamic_slice_in_dim(residual_in, core_place * share_size, share_size, 1)
    own_hidden = (own_residual.astype(jnp.float32) + share).astype(jnp.bfloat16)
    normed = normalize(own_hidden, norm_gain)
    if rep_count > 1:
        normed = lax.all_gather(normed, "rep", axis=1, tiled=True)
    normed = normed.reshape(token_count, model_width)

    parts = 2 if token_count % 16 == 0 else 1
    size = token_count // parts
    returned = []
    for part in range(parts):
        rows = slice(part * size, (part + 1) * size)
        pieces = gather_pieces(normed[rows])
        scale = own_weight[:, rows].reshape(-1, 1)
        returned.append(give_back(*expert_apply(pieces, gate_up, expert_output, scale)))
    mixture = jnp.concatenate(returned, axis=0).reshape(requests, token_block, model_width)
    if rep_count > 1:
        mixture = lax.psum_scatter(
            mixture.astype(jnp.bfloat16), "rep", scatter_dimension=1, tiled=True
        ).astype(jnp.float32)
    layer_out = (own_hidden.astype(jnp.float32) + mixture).astype(jnp.bfloat16)
    return (context, layer_out)


def solution(mesh):
    in_specs = (
        P("groups", "ctx", ("exp", "rep")),
        P("groups", "ctx", None, "exp"),
        P("groups", None),
        P("groups", ("ctx", "exp"), None),
        P(("exp", "rep"), None),
        P(),
        P("groups", ("ctx", "exp"), None),
        P("groups", ("ctx", "exp"), None),
        P(("ctx", "exp"), None, None, "rep"),
        P(("ctx", "exp"), "rep", None),
    )
    out_specs = (P("groups", "ctx", ("exp", "rep")), P("groups", ("ctx", "exp", "rep"), None))
    return jax.shard_map(
        per_device, mesh=mesh, in_specs=in_specs, out_specs=out_specs, check_vma=False
    )
```

```python
import functools

import jax
import jax.numpy as jnp
from jax import lax
from jax.experimental import pallas as pl
from jax.experimental.pallas import tpu as pltpu
from jax.sharding import PartitionSpec as P

HEAD = 128

floor_value = -1e30
norm_epsilon = 1e-06


def normalize(hidden, norm_gain):
    widened = hidden.astype(jnp.float32)
    mean_square = jnp.mean(widened * widened, axis=-1, keepdims=True)
    return (widened * lax.rsqrt(mean_square + norm_epsilon) * norm_gain).astype(jnp.bfloat16)


def strides(count):
    assert count & (count - 1) == 0
    return [1 << bit for bit in reversed(range(count.bit_length() - 1))]


def swap(value, axis, stride):
    return lax.ppermute(value, axis, [(i, i ^ stride) for i in range(lax.axis_size(axis))])


def shift(value, axis, step):
    count = lax.axis_size(axis)
    return lax.ppermute(value, axis, [(i, (i + step) % count) for i in range(count)])


def whole_specs(count):
    return [pl.BlockSpec(memory_space=pltpu.VMEM)] * count


SMEM_SPEC = pl.BlockSpec(memory_space=pltpu.SMEM)
LIMIT = pltpu.CompilerParams(vmem_limit_bytes=16 * 1024 * 1024)


def stack_heads(queries):
    heads = queries.shape[1] // HEAD
    return jnp.concatenate(
        [queries[:, h * HEAD : (h + 1) * HEAD] for h in range(heads)], axis=0
    )


def page_partial(stacked, keys, values, page, length, place, fresh_block):
    rows, page_size = stacked.shape[0], keys.shape[0]
    slab_size = page_size - fresh_block
    scores = lax.dot_general(
        keys, stacked, (((1,), (1,)), ((), ())), preferred_element_type=jnp.float32
    )
    lanes = HEAD if HEAD % fresh_block == 0 and rows % HEAD == 0 else rows
    offset = lax.broadcasted_iota(jnp.int32, (slab_size, lanes), 0)
    fresh = page * fresh_block + lax.broadcasted_iota(jnp.int32, (fresh_block, lanes), 0)
    lane = lax.broadcasted_iota(jnp.int32, (fresh_block, lanes), 1)
    position = place * fresh_block + lax.rem(lane, fresh_block)
    bias = jnp.concatenate(
        [
            jnp.where(offset < length, 0.0, floor_value),
            jnp.where(fresh <= position, 0.0, floor_value),
        ],
        axis=0,
    )
    masked = scores + jnp.concatenate([bias] * (rows // lanes), axis=1)
    peak = jnp.max(masked, axis=0, keepdims=True)
    weights = jnp.exp((masked - peak) * (HEAD**-0.5))
    total = jnp.sum(weights, axis=0, keepdims=True)
    summed = lax.dot_general(
        values,
        weights.astype(jnp.bfloat16),
        (((0,), (0,)), ((), ())),
        preferred_element_type=jnp.float32,
    )
    return peak, total, summed


def merge(first, second):
    peak = jnp.maximum(first[0], second[0])
    scale_first = jnp.exp((first[0] - peak) * (HEAD**-0.5))
    scale_second = jnp.exp((second[0] - peak) * (HEAD**-0.5))
    return (
        peak,
        first[1] * scale_first + second[1] * scale_second,
        first[2] * scale_first + second[2] * scale_second,
    )


def page_at(offset):
    count = lax.axis_size("ctx")
    return lax.rem(lax.axis_index("ctx") + offset + count, count)


def early_kernel(offsets, last, fresh_block, lengths, queries, *refs):
    count = len(offsets)
    pages, (peak_out, total_out, summed_out, length_out) = refs[: 2 * count], refs[-4:]
    length_out[...] = jnp.full(length_out.shape, lengths[page_at(last)], jnp.int32)
    stacked = stack_heads(queries[...])
    place = lax.axis_index("ctx")
    state = None
    for number, offset in enumerate(offsets):
        page = page_at(offset)
        part = page_partial(
            stacked,
            pages[2 * number][...],
            pages[2 * number + 1][...],
            page,
            lengths[page],
            place,
            fresh_block,
        )
        state = part if state is None else merge(state, part)
    peak_out[...] = state[0]
    total_out[...] = state[1]
    summed_out[...] = state[2]


def late_kernel(
    offset,
    fresh_block,
    queries,
    keys,
    values,
    peak,
    total,
    summed,
    length,
    weight,
    context_out,
    own_out,
    *rest,
):
    sent_outs, blocks = rest[:-1], rest[-1]
    page = page_at(offset)
    part = page_partial(
        stack_heads(queries[...]),
        keys[...],
        values[...],
        page,
        length[...],
        lax.axis_index("ctx"),
        fresh_block,
    )
    state = merge((peak[...], total[...], summed[...]), part)
    result = jnp.transpose(state[2] / state[1])
    context = jnp.concatenate(
        [
            result[h * fresh_block : (h + 1) * fresh_block]
            for h in range(result.shape[0] // fresh_block)
        ],
        axis=1,
    ).astype(jnp.bfloat16)
    context_out[...] = context
    blocks[...] = jnp.dot(context, weight[...], preferred_element_type=jnp.float32)
    place = lax.axis_index("exp")
    size = own_out.shape[0]
    pick = lambda index: blocks[pl.ds(pl.multiple_of(index * size, size), size), :]
    own_out[...] = pick(place)
    for step, out in enumerate(sent_outs, 1):
        out[...] = pick(place ^ step).astype(jnp.bfloat16)


def attention(queries, pages, lengths, out_weight, token_block, later):
    fresh_block, width = queries.shape
    rows = width // HEAD * fresh_block
    count = lax.axis_size("ctx")
    exp_count = lax.axis_size("exp")
    model_width = out_weight.shape[1]
    own_keys, own_values = pages[:, 0], pages[:, 1]
    held = [(0, own_keys, own_values)]
    left_keys, left_values = own_keys, own_values
    right_keys, right_values = own_keys, own_values
    for step in range(1, (count - 1) // 2 + 1):
        left_keys = shift(left_keys, "ctx", 1)
        right_values = shift(right_values, "ctx", -1)
        left_values = shift(left_values, "ctx", 1)
        right_keys = shift(right_keys, "ctx", -1)
        held.append((-step, left_keys, left_values))
        held.append((step, right_keys, right_values))
    if count % 2 == 0:
        last = (count // 2, shift(left_keys, "ctx", 1), shift(right_values, "ctx", -1))
    else:
        last = held.pop()
    page_flops = 4 * rows * pages.shape[0] * HEAD
    line = jax.ShapeDtypeStruct((1, rows), jnp.float32)
    state = None
    for start in range(0, len(held), 3):
        group = held[start : start + 3]
        operands = [part for _, keys, values in group for part in (keys, values)]
        held_operands = () if start else (out_weight, *later)
        partial_state = pl.pallas_call(
            functools.partial(
                early_kernel, [offset for offset, _, _ in group], last[0], fresh_block
            ),
            out_shape=(
                line,
                line,
                jax.ShapeDtypeStruct((HEAD, rows), jnp.float32),
                jax.ShapeDtypeStruct((1, HEAD), jnp.int32),
            ),
            in_specs=[SMEM_SPEC]
            + whole_specs(1 + len(operands))
            + [pl.BlockSpec(memory_space=pl.ANY)] * len(held_operands),
            out_specs=tuple(whole_specs(4)),
            compiler_params=LIMIT,
            cost_estimate=pl.CostEstimate(
                flops=len(group) * page_flops, bytes_accessed=2 << 20, transcendentals=0
            ),
        )(lengths, queries, *operands, *held_operands)
        partial_state, length = partial_state[:3], partial_state[3]
        state = partial_state if state is None else merge(state, partial_state)
    block = jax.ShapeDtypeStruct((token_block, model_width), jnp.bfloat16)
    outs = pl.pallas_call(
        functools.partial(late_kernel, last[0], fresh_block),
        out_shape=(
            jax.ShapeDtypeStruct(queries.shape, jnp.bfloat16),
            jax.ShapeDtypeStruct(block.shape, jnp.float32),
        )
        + (block,) * (exp_count - 1),
        in_specs=whole_specs(8),
        out_specs=tuple(whole_specs(1 + exp_count)),
        scratch_shapes=[pltpu.VMEM((fresh_block, model_width), jnp.float32)],
        compiler_params=LIMIT,
        cost_estimate=pl.CostEstimate(
            flops=page_flops + 2 * fresh_block * width * model_width,
            bytes_accessed=6 << 20,
            transcendentals=0,
        ),
    )(queries, last[1], last[2], *state, length, out_weight)
    return outs[0], outs[1], outs[2:]


def finish_kernel(count, *refs):
    parts, (residual, gain, ids, scores, hidden_out, sent_out) = refs[:count], refs[count:]
    total = residual[...].astype(jnp.float32)
    for part in parts:
        total = total + part[...].astype(jnp.float32)
    hidden = total.astype(jnp.bfloat16)
    hidden_out[...] = hidden
    width = hidden.shape[1]
    sent_out[:, :width] = normalize(hidden, gain[...])
    chosen = scores[...]
    combine = (chosen / jnp.sum(chosen, axis=1, keepdims=True)).astype(jnp.bfloat16)
    combine = combine.astype(jnp.float32)
    tokens, choices = chosen.shape
    expert = lax.broadcasted_iota(jnp.int32, (tokens, sent_out.shape[1] - width), 1)
    dense = jnp.zeros(expert.shape, jnp.float32)
    for k in range(choices):
        dense = dense + jnp.where(ids[:, k : k + 1] == expert, combine[:, k : k + 1], 0.0)
    sent_out[:, width:] = dense.astype(jnp.bfloat16)


def finish(parts, residual, norm_gain, ids, scores, expert_count):
    tokens, width = residual.shape
    lanes = -(-expert_count // 128) * 128
    return pl.pallas_call(
        functools.partial(finish_kernel, len(parts)),
        out_shape=(
            jax.ShapeDtypeStruct((tokens, width), jnp.bfloat16),
            jax.ShapeDtypeStruct((tokens, width + lanes), jnp.bfloat16),
        ),
        in_specs=whole_specs(len(parts) + 4),
        out_specs=tuple(whole_specs(2)),
        compiler_params=LIMIT,
        cost_estimate=pl.CostEstimate(
            flops=8 * residual.size, bytes_accessed=1 << 19, transcendentals=0
        ),
    )(*parts, residual, norm_gain[None], ids, scores)


def down_kernel(inner, rows, down, out):
    expert = lax.axis_index("ctx") * lax.axis_size("exp") + lax.axis_index("exp")
    gate = inner[0]
    activated = (gate / (1.0 + jnp.exp(-gate)) * inner[1]).astype(jnp.bfloat16)
    piece = jnp.dot(activated, down[0], preferred_element_type=jnp.float32)
    dense = rows[:, out.shape[1] :].astype(jnp.float32)
    lane = lax.broadcasted_iota(jnp.int32, dense.shape, 1)
    scale = jnp.sum(jnp.where(lane == expert, dense, 0.0), axis=1, keepdims=True)
    out[...] = (piece.astype(jnp.bfloat16).astype(jnp.float32) * scale).astype(out.dtype)


def expert_apply(rows, gate_up, down, kind):
    _, hidden, width = down.shape
    inner = jnp.einsum(
        "nd,dgh->gnh", rows[:, :width], gate_up[0], preferred_element_type=jnp.float32
    )
    return pl.pallas_call(
        down_kernel,
        out_shape=jax.ShapeDtypeStruct((rows.shape[0], width), kind),
        in_specs=whole_specs(3),
        out_specs=whole_specs(1)[0],
        compiler_params=LIMIT,
        cost_estimate=pl.CostEstimate(
            flops=2 * rows.shape[0] * width * hidden, bytes_accessed=2 << 20, transcendentals=0
        ),
    )(inner, rows, down)


def gather_near(rows, near):
    pieces = [rows]
    for stride in near:
        pieces = pieces + [swap(piece, "exp", stride) for piece in pieces]
    return pieces


def return_near(values, near):
    for stride in reversed(near):
        half = len(values) // 2
        values = [
            keep.astype(jnp.float32)
            + swap(send.astype(jnp.bfloat16), "exp", stride).astype(jnp.float32)
            for keep, send in zip(values[:half], values[half:])
        ]
    return values[0].astype(jnp.float32)


def mixture_of(rows, gate_up, down):
    tokens = rows.shape[0]
    ctx_count = lax.axis_size("ctx")
    exp_strides = strides(lax.axis_size("exp"))
    far, near = exp_strides[:1], exp_strides[1:]

    blocks = {0: rows}
    for offset in reversed(range(1, ctx_count)):
        blocks[offset] = swap(rows, "ctx", offset)
    half = ctx_count // 2
    chunks = [list(range(half, ctx_count)), list(range(half))] if half else [[0]]
    sent = [jnp.concatenate([blocks[offset] for offset in chunk], axis=0) for chunk in chunks]

    def results(pieces):
        half = (len(pieces) + 1) // 2
        kinds = [jnp.float32] * half + [jnp.bfloat16] * (len(pieces) - half)
        values = [expert_apply(piece, gate_up, down, kind) for piece, kind in zip(pieces, kinds)]
        return return_near(values, near)

    crossed = [[swap(piece, "exp", stride) for stride in far] for piece in sent]
    totals = {}
    for chunk, home, away in zip(chunks, sent, crossed):
        value = results(gather_near(home, near))
        for piece in away:
            other = results(gather_near(piece, near)).astype(jnp.bfloat16)
            value = value + swap(other, "exp", far[0]).astype(jnp.float32)
        for position, offset in enumerate(chunk):
            totals[offset] = value[position * tokens : (position + 1) * tokens]
    total = totals[0]
    for offset in reversed(range(1, ctx_count)):
        total = total + swap(totals[offset].astype(jnp.bfloat16), "ctx", offset).astype(jnp.float32)
    return total


def per_device(
    queries,
    pages,
    cached_lengths,
    residual_in,
    out_weight,
    norm_gain,
    expert_ids,
    route_scores,
    expert_input,
    expert_output,
):
    requests = queries.shape[0]
    core_place = lax.axis_index("rep")
    rep_count = lax.axis_size("rep")
    exp_count = lax.axis_size("exp")
    expert_count = lax.axis_size("ctx") * exp_count
    token_block, model_width = residual_in.shape[1:]
    token_count = requests * token_block

    contexts, owns, sents = [], [], []
    for r in range(requests):
        context, own, sent = attention(
            queries[r],
            pages[r],
            cached_lengths[r],
            out_weight,
            token_block,
            (residual_in, norm_gain, expert_output, expert_ids, route_scores),
        )
        contexts.append(context)
        owns.append(own)
        sents.append(sent)
    context = jnp.stack(contexts)

    parts = [jnp.concatenate(owns, axis=0)]
    for step in range(1, exp_count):
        blocks = jnp.concatenate([sent[step - 1] for sent in sents], axis=0)
        parts.append(swap(blocks, "exp", step))
    residual, ids, scores = residual_in, expert_ids, route_scores
    if rep_count > 1:
        share_size = token_block // rep_count
        share = sum(part.astype(jnp.float32) for part in parts).astype(jnp.bfloat16)
        share = share.reshape(requests, token_block, model_width)
        share = lax.psum_scatter(share, "rep", scatter_dimension=1, tiled=True)
        parts = [share.reshape(-1, model_width)]
        residual, ids, scores = (
            lax.dynamic_slice_in_dim(whole, core_place * share_size, share_size, 1)
            for whole in (residual, ids, scores)
        )
    own_hidden, normed = finish(
        parts,
        residual.reshape(-1, model_width),
        norm_gain,
        ids.reshape(-1, ids.shape[2]),
        scores.reshape(-1, ids.shape[2]),
        expert_count,
    )
    own_hidden = own_hidden.reshape(requests, -1, model_width)
    if rep_count > 1:
        normed = normed.reshape(requests, share_size, -1)
        normed = lax.all_gather(normed, "rep", axis=1, tiled=True)
        normed = normed.reshape(token_count, -1)

    mixture = mixture_of(normed, expert_input, expert_output)
    mixture = mixture.reshape(requests, token_block, model_width)
    if rep_count > 1:
        mixture = lax.psum_scatter(
            mixture.astype(jnp.bfloat16), "rep", scatter_dimension=1, tiled=True
        ).astype(jnp.float32)
    layer_out = (own_hidden.astype(jnp.float32) + mixture).astype(jnp.bfloat16)
    return (context, layer_out)


def solution(mesh):
    in_specs = (
        P("groups", "ctx", ("exp", "rep")),
        P("groups", "ctx", None, "exp"),
        P("groups", None),
        P("groups", ("ctx", "exp"), None),
        P(("exp", "rep"), None),
        P(),
        P("groups", ("ctx", "exp"), None),
        P("groups", ("ctx", "exp"), None),
        P(("ctx", "exp"), None, None, "rep"),
        P(("ctx", "exp"), "rep", None),
    )
    out_specs = (P("groups", "ctx", ("exp", "rep")), P("groups", ("ctx", "exp", "rep"), None))
    return jax.shard_map(
        per_device, mesh=mesh, in_specs=in_specs, out_specs=out_specs, check_vma=False
    )
```

```python
import functools

import jax
import jax.numpy as jnp
from jax import lax
from jax.experimental import pallas as pl
from jax.experimental.pallas import tpu as pltpu
from jax.sharding import PartitionSpec as P

HEAD = 128

floor_value = -1e30
norm_epsilon = 1e-06


def normalize(hidden, norm_gain):
    widened = hidden.astype(jnp.float32)
    mean_square = jnp.mean(widened * widened, axis=-1, keepdims=True)
    return (widened * lax.rsqrt(mean_square + norm_epsilon) * norm_gain).astype(jnp.bfloat16)


def strides(count):
    assert count & (count - 1) == 0
    return [1 << bit for bit in reversed(range(count.bit_length() - 1))]


def swap(value, axis, stride):
    return lax.ppermute(value, axis, [(i, i ^ stride) for i in range(lax.axis_size(axis))])


def shift(value, axis, step):
    count = lax.axis_size(axis)
    return lax.ppermute(value, axis, [(i, (i + step) % count) for i in range(count)])


def whole_specs(count):
    return [pl.BlockSpec(memory_space=pltpu.VMEM)] * count


SMEM_SPEC = pl.BlockSpec(memory_space=pltpu.SMEM)
LIMIT = pltpu.CompilerParams(vmem_limit_bytes=12 * 1024 * 1024)


def stack_heads(queries):
    heads = queries.shape[1] // HEAD
    return jnp.concatenate(
        [queries[:, h * HEAD : (h + 1) * HEAD] for h in range(heads)], axis=0
    )


def page_partial(stacked, keys, values, page, length, place, fresh_block):
    rows, page_size = stacked.shape[0], keys.shape[0]
    slab_size = page_size - fresh_block
    scores = lax.dot_general(
        keys, stacked, (((1,), (1,)), ((), ())), preferred_element_type=jnp.float32
    )
    lanes = HEAD if HEAD % fresh_block == 0 and rows % HEAD == 0 else rows
    offset = lax.broadcasted_iota(jnp.int32, (slab_size, lanes), 0)
    fresh = page * fresh_block + lax.broadcasted_iota(jnp.int32, (fresh_block, lanes), 0)
    lane = lax.broadcasted_iota(jnp.int32, (fresh_block, lanes), 1)
    position = place * fresh_block + lax.rem(lane, fresh_block)
    bias = jnp.concatenate(
        [
            jnp.where(offset < length, 0.0, floor_value),
            jnp.where(fresh <= position, 0.0, floor_value),
        ],
        axis=0,
    )
    masked = scores + jnp.concatenate([bias] * (rows // lanes), axis=1)
    peak = jnp.max(masked, axis=0, keepdims=True)
    weights = jnp.exp((masked - peak) * (HEAD**-0.5))
    total = jnp.sum(weights, axis=0, keepdims=True)
    summed = lax.dot_general(
        values,
        weights.astype(jnp.bfloat16),
        (((0,), (0,)), ((), ())),
        preferred_element_type=jnp.float32,
    )
    return peak, total, summed


def merge(first, second):
    peak = jnp.maximum(first[0], second[0])
    scale_first = jnp.exp((first[0] - peak) * (HEAD**-0.5))
    scale_second = jnp.exp((second[0] - peak) * (HEAD**-0.5))
    return (
        peak,
        first[1] * scale_first + second[1] * scale_second,
        first[2] * scale_first + second[2] * scale_second,
    )


def page_at(offset):
    count = lax.axis_size("ctx")
    return lax.rem(lax.axis_index("ctx") + offset + count, count)


def first_kernel(fresh_block, count, lengths, queries, keys, values, *refs):
    peak_out, total_out, summed_out, lengths_out = refs[-4:]
    for offset in range(count):
        lengths_out[offset : offset + 1, :] = jnp.full(
            (1, lengths_out.shape[1]), lengths[page_at(offset)], jnp.int32
        )
    place = lax.axis_index("ctx")
    peak_out[...], total_out[...], summed_out[...] = page_partial(
        stack_heads(queries[...]),
        keys[...],
        values[...],
        place,
        lengths[place],
        place,
        fresh_block,
    )


def middle_kernel(offsets, fresh_block, queries, lengths, *refs):
    count = len(offsets)
    pages, (peak, total, summed) = refs[: 2 * count], refs[2 * count : 2 * count + 3]
    outs = refs[2 * count + 3 :]
    stacked = stack_heads(queries[...])
    state = (peak[...], total[...], summed[...])
    for number, offset in enumerate(offsets):
        part = page_partial(
            stacked,
            pages[2 * number][...],
            pages[2 * number + 1][...],
            page_at(offset),
            lengths[offset : offset + 1, :],
            lax.axis_index("ctx"),
            fresh_block,
        )
        state = merge(state, part)
    for out, value in zip(outs, state):
        out[...] = value


def late_kernel(
    offset,
    fresh_block,
    queries,
    keys,
    values,
    lengths,
    peak,
    total,
    summed,
    weight,
    context_out,
    own_out,
    *rest,
):
    sent_outs, blocks = rest[:-1], rest[-1]
    page = page_at(offset)
    part = page_partial(
        stack_heads(queries[...]),
        keys[...],
        values[...],
        page,
        lengths[offset : offset + 1, :],
        lax.axis_index("ctx"),
        fresh_block,
    )
    state = merge((peak[...], total[...], summed[...]), part)
    result = jnp.transpose(state[2] / state[1])
    context = jnp.concatenate(
        [
            result[h * fresh_block : (h + 1) * fresh_block]
            for h in range(result.shape[0] // fresh_block)
        ],
        axis=1,
    ).astype(jnp.bfloat16)
    context_out[...] = context
    blocks[...] = jnp.dot(context, weight[...], preferred_element_type=jnp.float32)
    place = lax.axis_index("exp")
    size = own_out.shape[0]
    pick = lambda index: blocks[pl.ds(pl.multiple_of(index * size, size), size), :]
    own_out[...] = pick(place)
    for step, out in enumerate(sent_outs, 1):
        out[...] = pick(place ^ step).astype(jnp.bfloat16)


def attention(queries, pages, lengths, out_weight, token_block, later):
    fresh_block, width = queries.shape
    rows = width // HEAD * fresh_block
    count = lax.axis_size("ctx")
    exp_count = lax.axis_size("exp")
    model_width = out_weight.shape[1]
    own_keys, own_values = pages[:, 0], pages[:, 1]
    held = []
    left_keys, left_values = own_keys, own_values
    right_keys, right_values = own_keys, own_values
    for step in range(1, (count - 1) // 2 + 1):
        left_keys = shift(left_keys, "ctx", 1)
        right_values = shift(right_values, "ctx", -1)
        left_values = shift(left_values, "ctx", 1)
        right_keys = shift(right_keys, "ctx", -1)
        held.append((count - step, left_keys, left_values))
        held.append((step, right_keys, right_values))
    if count % 2 == 0:
        last = (count // 2, shift(left_keys, "ctx", 1), shift(right_values, "ctx", -1))
    else:
        last = held.pop()
    page_flops = 4 * rows * pages.shape[0] * HEAD
    line = jax.ShapeDtypeStruct((1, rows), jnp.float32)
    partial_shape = (line, line, jax.ShapeDtypeStruct((HEAD, rows), jnp.float32))
    *state, page_lengths = pl.pallas_call(
        functools.partial(first_kernel, fresh_block, count),
        out_shape=partial_shape + (jax.ShapeDtypeStruct((count, HEAD), jnp.int32),),
        in_specs=[SMEM_SPEC]
        + whole_specs(3)
        + [pl.BlockSpec(memory_space=pl.ANY)] * (1 + len(later)),
        out_specs=tuple(whole_specs(4)),
        compiler_params=LIMIT,
        cost_estimate=pl.CostEstimate(
            flops=16 * page_flops, bytes_accessed=8 << 20, transcendentals=0
        ),
    )(lengths, queries, own_keys, own_values, out_weight, *later)
    for start in range(0, len(held), 2):
        group = held[start : start + 2]
        operands = [part for _, keys, values in group for part in (keys, values)]
        state = pl.pallas_call(
            functools.partial(middle_kernel, [offset for offset, _, _ in group], fresh_block),
            out_shape=partial_shape,
            in_specs=whole_specs(5 + len(operands)),
            out_specs=tuple(whole_specs(3)),
            compiler_params=LIMIT,
            cost_estimate=pl.CostEstimate(
                flops=len(group) * page_flops, bytes_accessed=2 << 20, transcendentals=0
            ),
        )(queries, page_lengths, *operands, *state)
    block = jax.ShapeDtypeStruct((token_block, model_width), jnp.bfloat16)
    outs = pl.pallas_call(
        functools.partial(late_kernel, last[0], fresh_block),
        out_shape=(
            jax.ShapeDtypeStruct(queries.shape, jnp.bfloat16),
            jax.ShapeDtypeStruct(block.shape, jnp.float32),
        )
        + (block,) * (exp_count - 1),
        in_specs=whole_specs(8),
        out_specs=tuple(whole_specs(1 + exp_count)),
        scratch_shapes=[pltpu.VMEM((fresh_block, model_width), jnp.float32)],
        compiler_params=LIMIT,
        cost_estimate=pl.CostEstimate(
            flops=page_flops + 2 * fresh_block * width * model_width,
            bytes_accessed=6 << 20,
            transcendentals=0,
        ),
    )(queries, last[1], last[2], page_lengths, *state, out_weight)
    return outs[0], outs[1], outs[2:]


def finish_kernel(count, *refs):
    parts, (residual, gain, ids, scores, hidden_out, sent_out) = refs[:count], refs[count:]
    total = residual[...].astype(jnp.float32)
    for part in parts:
        total = total + part[...].astype(jnp.float32)
    hidden = total.astype(jnp.bfloat16)
    hidden_out[...] = hidden
    width = hidden.shape[1]
    sent_out[:, :width] = normalize(hidden, gain[...])
    chosen = jnp.transpose(scores[...])
    ids = jnp.transpose(ids[...])
    combine = (chosen / jnp.sum(chosen, axis=1, keepdims=True)).astype(jnp.bfloat16)
    combine = combine.astype(jnp.float32)
    tokens, choices = chosen.shape
    expert = lax.broadcasted_iota(jnp.int32, (tokens, sent_out.shape[1] - width), 1)
    dense = jnp.zeros(expert.shape, jnp.float32)
    for k in range(choices):
        dense = dense + jnp.where(ids[:, k : k + 1] == expert, combine[:, k : k + 1], 0.0)
    sent_out[:, width:] = dense.astype(jnp.bfloat16)


def finish(parts, residual, norm_gain, ids, scores, expert_count):
    tokens, width = residual.shape
    lanes = -(-expert_count // 128) * 128
    return pl.pallas_call(
        functools.partial(finish_kernel, len(parts)),
        out_shape=(
            jax.ShapeDtypeStruct((tokens, width), jnp.bfloat16),
            jax.ShapeDtypeStruct((tokens, width + lanes), jnp.bfloat16),
        ),
        in_specs=whole_specs(len(parts) + 4),
        out_specs=tuple(whole_specs(2)),
        compiler_params=LIMIT,
        cost_estimate=pl.CostEstimate(
            flops=8 * residual.size, bytes_accessed=1 << 19, transcendentals=0
        ),
    )(*parts, residual, norm_gain[None], ids, scores)


def down_kernel(inner, rows, down, out):
    expert = lax.axis_index("ctx") * lax.axis_size("exp") + lax.axis_index("exp")
    gate = inner[0]
    activated = (gate / (1.0 + jnp.exp(-gate)) * inner[1]).astype(jnp.bfloat16)
    piece = jnp.dot(activated, down[0], preferred_element_type=jnp.float32)
    dense = rows[:, out.shape[1] :].astype(jnp.float32)
    lane = lax.broadcasted_iota(jnp.int32, dense.shape, 1)
    scale = jnp.sum(jnp.where(lane == expert, dense, 0.0), axis=1, keepdims=True)
    out[...] = (piece.astype(jnp.bfloat16).astype(jnp.float32) * scale).astype(out.dtype)


def expert_apply(rows, gate_up, down, kind):
    _, hidden, width = down.shape
    inner = jnp.einsum(
        "nd,dgh->gnh", rows[:, :width], gate_up[0], preferred_element_type=jnp.float32
    )
    return pl.pallas_call(
        down_kernel,
        out_shape=jax.ShapeDtypeStruct((rows.shape[0], width), kind),
        in_specs=whole_specs(3),
        out_specs=whole_specs(1)[0],
        compiler_params=LIMIT,
        cost_estimate=pl.CostEstimate(
            flops=2 * rows.shape[0] * width * hidden, bytes_accessed=2 << 20, transcendentals=0
        ),
    )(inner, rows, down)


def gather_near(rows, near):
    pieces = [rows]
    for stride in near:
        pieces = pieces + [swap(piece, "exp", stride) for piece in pieces]
    return pieces


def return_near(values, near):
    for stride in reversed(near):
        half = len(values) // 2
        values = [
            keep.astype(jnp.float32)
            + swap(send.astype(jnp.bfloat16), "exp", stride).astype(jnp.float32)
            for keep, send in zip(values[:half], values[half:])
        ]
    return values[0].astype(jnp.float32)


def mixture_of(rows, gate_up, down):
    tokens = rows.shape[0]
    ctx_count = lax.axis_size("ctx")
    exp_strides = strides(lax.axis_size("exp"))
    far, near = exp_strides[:1], exp_strides[1:]

    blocks = {0: rows}
    for offset in range(1, ctx_count):
        blocks[offset] = swap(rows, "ctx", offset)
    half = ctx_count // 2
    chunks = [list(range(half)), list(range(half, ctx_count))] if half else [[0]]
    sent = [jnp.concatenate([blocks[offset] for offset in chunk], axis=0) for chunk in chunks]

    def results(pieces):
        half = (len(pieces) + 1) // 2
        kinds = [jnp.float32] * half + [jnp.bfloat16] * (len(pieces) - half)
        values = [expert_apply(piece, gate_up, down, kind) for piece, kind in zip(pieces, kinds)]
        return return_near(values, near)

    crossed = []
    for number, piece in enumerate(sent):
        if crossed:
            piece, crossed[-1] = lax.optimization_barrier((piece, crossed[-1]))
        crossed.append([swap(piece, "exp", stride) for stride in far])
    totals = {}
    for chunk, home, away in zip(chunks, sent, crossed):
        value = results(gather_near(home, near))
        for piece in away:
            other = results(gather_near(piece, near)).astype(jnp.bfloat16)
            value = value + swap(other, "exp", far[0]).astype(jnp.float32)
        for position, offset in enumerate(chunk):
            totals[offset] = value[position * tokens : (position + 1) * tokens]
    total = totals[0]
    for offset in reversed(range(1, ctx_count)):
        total = total + swap(totals[offset].astype(jnp.bfloat16), "ctx", offset).astype(jnp.float32)
    return total


def per_device(
    queries,
    pages,
    cached_lengths,
    residual_in,
    out_weight,
    norm_gain,
    expert_ids,
    route_scores,
    expert_input,
    expert_output,
):
    requests = queries.shape[0]
    core_place = lax.axis_index("rep")
    rep_count = lax.axis_size("rep")
    exp_count = lax.axis_size("exp")
    expert_count = lax.axis_size("ctx") * exp_count
    token_block, model_width = residual_in.shape[1:]
    token_count = requests * token_block

    contexts, owns, sents = [], [], []
    for r in range(requests):
        context, own, sent = attention(
            queries[r],
            pages[r],
            cached_lengths[r],
            out_weight,
            token_block,
            (expert_output,),
        )
        contexts.append(context)
        owns.append(own)
        sents.append(sent)
    context = jnp.stack(contexts)

    parts = [jnp.concatenate(owns, axis=0)]
    for step in range(1, exp_count):
        blocks = jnp.concatenate([sent[step - 1] for sent in sents], axis=0)
        parts.append(swap(blocks, "exp", step))
    residual, ids, scores = residual_in, expert_ids, route_scores
    if rep_count > 1:
        share_size = token_block // rep_count
        share = sum(part.astype(jnp.float32) for part in parts).astype(jnp.bfloat16)
        share = share.reshape(requests, token_block, model_width)
        share = lax.psum_scatter(share, "rep", scatter_dimension=1, tiled=True)
        parts = [share.reshape(-1, model_width)]
        residual, ids, scores = (
            lax.dynamic_slice_in_dim(whole, core_place * share_size, share_size, 1)
            for whole in (residual, ids, scores)
        )
    own_hidden, normed = finish(
        parts,
        residual.reshape(-1, model_width),
        norm_gain,
        ids.reshape(-1, ids.shape[2]).T,
        scores.reshape(-1, ids.shape[2]).T,
        expert_count,
    )
    own_hidden = own_hidden.reshape(requests, -1, model_width)
    if rep_count > 1:
        normed = normed.reshape(requests, share_size, -1)
        normed = lax.all_gather(normed, "rep", axis=1, tiled=True)
        normed = normed.reshape(token_count, -1)

    mixture = mixture_of(normed, expert_input, expert_output)
    mixture = mixture.reshape(requests, token_block, model_width)
    if rep_count > 1:
        mixture = lax.psum_scatter(
            mixture.astype(jnp.bfloat16), "rep", scatter_dimension=1, tiled=True
        ).astype(jnp.float32)
    layer_out = (own_hidden.astype(jnp.float32) + mixture).astype(jnp.bfloat16)
    return (context, layer_out)


def solution(mesh):
    in_specs = (
        P("groups", "ctx", ("exp", "rep")),
        P("groups", "ctx", None, "exp"),
        P("groups", None),
        P("groups", ("ctx", "exp"), None),
        P(("exp", "rep"), None),
        P(),
        P("groups", ("ctx", "exp"), None),
        P("groups", ("ctx", "exp"), None),
        P(("ctx", "exp"), None, None, "rep"),
        P(("ctx", "exp"), "rep", None),
    )
    out_specs = (P("groups", "ctx", ("exp", "rep")), P("groups", ("ctx", "exp", "rep"), None))
    return jax.shard_map(
        per_device, mesh=mesh, in_specs=in_specs, out_specs=out_specs, check_vma=False
    )
```

```python
import functools

import jax
import jax.numpy as jnp
from jax import lax
from jax.experimental import pallas as pl
from jax.experimental.pallas import tpu as pltpu
from jax.sharding import PartitionSpec as P

HEAD = 128

floor_value = -1e30
norm_epsilon = 1e-06


def normalize(hidden, norm_gain):
    widened = hidden.astype(jnp.float32)
    mean_square = jnp.mean(widened * widened, axis=-1, keepdims=True)
    return (widened * lax.rsqrt(mean_square + norm_epsilon) * norm_gain).astype(jnp.bfloat16)


def strides(count):
    assert count & (count - 1) == 0
    return [1 << bit for bit in reversed(range(count.bit_length() - 1))]


def swap(value, axis, stride):
    return lax.ppermute(value, axis, [(i, i ^ stride) for i in range(lax.axis_size(axis))])


def shift(value, axis, step):
    count = lax.axis_size(axis)
    return lax.ppermute(value, axis, [(i, (i + step) % count) for i in range(count)])


def whole_specs(count):
    return [pl.BlockSpec(memory_space=pltpu.VMEM)] * count


SMEM_SPEC = pl.BlockSpec(memory_space=pltpu.SMEM)
LIMIT = pltpu.CompilerParams(vmem_limit_bytes=12 * 1024 * 1024)


def stack_heads(queries):
    heads = queries.shape[1] // HEAD
    return jnp.concatenate(
        [queries[:, h * HEAD : (h + 1) * HEAD] for h in range(heads)], axis=0
    )


def page_partial(stacked, keys, values, page, length, place, fresh_block):
    rows, page_size = stacked.shape[0], keys.shape[0]
    slab_size = page_size - fresh_block
    scores = lax.dot_general(
        keys, stacked, (((1,), (1,)), ((), ())), preferred_element_type=jnp.float32
    )
    lanes = HEAD if HEAD % fresh_block == 0 and rows % HEAD == 0 else rows
    offset = lax.broadcasted_iota(jnp.int32, (slab_size, lanes), 0)
    fresh = page * fresh_block + lax.broadcasted_iota(jnp.int32, (fresh_block, lanes), 0)
    lane = lax.broadcasted_iota(jnp.int32, (fresh_block, lanes), 1)
    position = place * fresh_block + lax.rem(lane, fresh_block)
    bias = jnp.concatenate(
        [
            jnp.where(offset < length, 0.0, floor_value),
            jnp.where(fresh <= position, 0.0, floor_value),
        ],
        axis=0,
    )
    masked = scores + jnp.concatenate([bias] * (rows // lanes), axis=1)
    peak = jnp.max(masked, axis=0, keepdims=True)
    weights = jnp.exp((masked - peak) * (HEAD**-0.5))
    total = jnp.sum(weights, axis=0, keepdims=True)
    summed = lax.dot_general(
        values,
        weights.astype(jnp.bfloat16),
        (((0,), (0,)), ((), ())),
        preferred_element_type=jnp.float32,
    )
    return peak, total, summed


def merge(first, second):
    peak = jnp.maximum(first[0], second[0])
    scale_first = jnp.exp((first[0] - peak) * (HEAD**-0.5))
    scale_second = jnp.exp((second[0] - peak) * (HEAD**-0.5))
    return (
        peak,
        first[1] * scale_first + second[1] * scale_second,
        first[2] * scale_first + second[2] * scale_second,
    )


def page_at(offset):
    count = lax.axis_size("ctx")
    return lax.rem(lax.axis_index("ctx") + offset + count, count)


def first_kernel(fresh_block, count, lengths, queries, keys, values, *refs):
    peak_out, total_out, summed_out, lengths_out = refs[-4:]
    for offset in range(count):
        lengths_out[offset : offset + 1, :] = jnp.full(
            (1, lengths_out.shape[1]), lengths[page_at(offset)], jnp.int32
        )
    place = lax.axis_index("ctx")
    peak_out[...], total_out[...], summed_out[...] = page_partial(
        stack_heads(queries[...]),
        keys[...],
        values[...],
        place,
        lengths[place],
        place,
        fresh_block,
    )


def middle_kernel(offsets, fresh_block, queries, lengths, *refs):
    count = len(offsets)
    pages, (peak, total, summed) = refs[: 2 * count], refs[2 * count : 2 * count + 3]
    outs = refs[2 * count + 3 :]
    stacked = stack_heads(queries[...])
    state = (peak[...], total[...], summed[...])
    for number, offset in enumerate(offsets):
        part = page_partial(
            stacked,
            pages[2 * number][...],
            pages[2 * number + 1][...],
            page_at(offset),
            lengths[offset : offset + 1, :],
            lax.axis_index("ctx"),
            fresh_block,
        )
        state = merge(state, part)
    for out, value in zip(outs, state):
        out[...] = value


def late_kernel(
    offset,
    fresh_block,
    queries,
    keys,
    values,
    lengths,
    peak,
    total,
    summed,
    weight,
    context_out,
    own_out,
    *rest,
):
    sent_outs, blocks = rest[:-1], rest[-1]
    page = page_at(offset)
    part = page_partial(
        stack_heads(queries[...]),
        keys[...],
        values[...],
        page,
        lengths[offset : offset + 1, :],
        lax.axis_index("ctx"),
        fresh_block,
    )
    state = merge((peak[...], total[...], summed[...]), part)
    result = jnp.transpose(state[2] / state[1])
    context = jnp.concatenate(
        [
            result[h * fresh_block : (h + 1) * fresh_block]
            for h in range(result.shape[0] // fresh_block)
        ],
        axis=1,
    ).astype(jnp.bfloat16)
    context_out[...] = context
    blocks[...] = jnp.dot(context, weight[...], preferred_element_type=jnp.float32)
    place = lax.axis_index("exp")
    size = own_out.shape[0]
    pick = lambda index: blocks[pl.ds(pl.multiple_of(index * size, size), size), :]
    own_out[...] = pick(place)
    for step, out in enumerate(sent_outs, 1):
        out[...] = pick(place ^ step).astype(jnp.bfloat16)


def attention(queries, pages, lengths, out_weight, token_block, later):
    fresh_block, width = queries.shape
    rows = width // HEAD * fresh_block
    count = lax.axis_size("ctx")
    exp_count = lax.axis_size("exp")
    model_width = out_weight.shape[1]
    own_keys, own_values = pages[:, 0], pages[:, 1]
    held = []
    left_keys, left_values = own_keys, own_values
    right_keys, right_values = own_keys, own_values
    for step in range(1, (count - 1) // 2 + 1):
        left_keys = shift(left_keys, "ctx", 1)
        right_values = shift(right_values, "ctx", -1)
        left_values = shift(left_values, "ctx", 1)
        right_keys = shift(right_keys, "ctx", -1)
        held.append((count - step, left_keys, left_values))
        held.append((step, right_keys, right_values))
    if count % 2 == 0:
        last = (count // 2, shift(left_keys, "ctx", 1), shift(right_values, "ctx", -1))
    else:
        last = held.pop()
    page_flops = 4 * rows * pages.shape[0] * HEAD
    line = jax.ShapeDtypeStruct((1, rows), jnp.float32)
    partial_shape = (line, line, jax.ShapeDtypeStruct((HEAD, rows), jnp.float32))
    *state, page_lengths = pl.pallas_call(
        functools.partial(first_kernel, fresh_block, count),
        out_shape=partial_shape + (jax.ShapeDtypeStruct((count, HEAD), jnp.int32),),
        in_specs=[SMEM_SPEC]
        + whole_specs(3)
        + [pl.BlockSpec(memory_space=pl.ANY)] * (1 + len(later)),
        out_specs=tuple(whole_specs(4)),
        compiler_params=LIMIT,
        cost_estimate=pl.CostEstimate(
            flops=16 * page_flops, bytes_accessed=8 << 20, transcendentals=0
        ),
    )(lengths, queries, own_keys, own_values, out_weight, *later)
    for start in range(0, len(held), 2):
        group = held[start : start + 2]
        operands = [part for _, keys, values in group for part in (keys, values)]
        state = pl.pallas_call(
            functools.partial(middle_kernel, [offset for offset, _, _ in group], fresh_block),
            out_shape=partial_shape,
            in_specs=whole_specs(5 + len(operands)),
            out_specs=tuple(whole_specs(3)),
            compiler_params=LIMIT,
            cost_estimate=pl.CostEstimate(
                flops=len(group) * page_flops, bytes_accessed=2 << 20, transcendentals=0
            ),
        )(queries, page_lengths, *operands, *state)
    block = jax.ShapeDtypeStruct((token_block, model_width), jnp.bfloat16)
    outs = pl.pallas_call(
        functools.partial(late_kernel, last[0], fresh_block),
        out_shape=(
            jax.ShapeDtypeStruct(queries.shape, jnp.bfloat16),
            jax.ShapeDtypeStruct(block.shape, jnp.float32),
        )
        + (block,) * (exp_count - 1),
        in_specs=whole_specs(8),
        out_specs=tuple(whole_specs(1 + exp_count)),
        scratch_shapes=[pltpu.VMEM((fresh_block, model_width), jnp.float32)],
        compiler_params=LIMIT,
        cost_estimate=pl.CostEstimate(
            flops=page_flops + 2 * fresh_block * width * model_width,
            bytes_accessed=6 << 20,
            transcendentals=0,
        ),
    )(queries, last[1], last[2], page_lengths, *state, out_weight)
    return outs[0], outs[1], outs[2:]


def finish_kernel(count, *refs):
    parts, (residual, gain, ids, scores, hidden_out, sent_out) = refs[:count], refs[count:]
    total = residual[...].astype(jnp.float32)
    for part in parts:
        total = total + part[...].astype(jnp.float32)
    hidden = total.astype(jnp.bfloat16)
    hidden_out[...] = hidden
    width = hidden.shape[1]
    sent_out[:, :width] = normalize(hidden, gain[...])
    chosen = jnp.transpose(scores[...])
    ids = jnp.transpose(ids[...])
    combine = (chosen / jnp.sum(chosen, axis=1, keepdims=True)).astype(jnp.bfloat16)
    combine = combine.astype(jnp.float32)
    tokens, choices = chosen.shape
    expert = lax.broadcasted_iota(jnp.int32, (tokens, sent_out.shape[1] - width), 1)
    dense = jnp.zeros(expert.shape, jnp.float32)
    for k in range(choices):
        dense = dense + jnp.where(ids[:, k : k + 1] == expert, combine[:, k : k + 1], 0.0)
    sent_out[:, width:] = dense.astype(jnp.bfloat16)


def finish(parts, residual, norm_gain, ids, scores, expert_count):
    tokens, width = residual.shape
    lanes = -(-expert_count // 128) * 128
    return pl.pallas_call(
        functools.partial(finish_kernel, len(parts)),
        out_shape=(
            jax.ShapeDtypeStruct((tokens, width), jnp.bfloat16),
            jax.ShapeDtypeStruct((tokens, width + lanes), jnp.bfloat16),
        ),
        in_specs=whole_specs(len(parts) + 4),
        out_specs=tuple(whole_specs(2)),
        compiler_params=LIMIT,
        cost_estimate=pl.CostEstimate(
            flops=8 * residual.size, bytes_accessed=1 << 19, transcendentals=0
        ),
    )(*parts, residual, norm_gain[None], ids, scores)


def down_kernel(inner, rows, down, keep_out, *send_out):
    expert = lax.axis_index("ctx") * lax.axis_size("exp") + lax.axis_index("exp")
    gate = inner[0]
    activated = (gate / (1.0 + jnp.exp(-gate)) * inner[1]).astype(jnp.bfloat16)
    piece = jnp.dot(activated, down[0], preferred_element_type=jnp.float32)
    dense = rows[:, piece.shape[1] :].astype(jnp.float32)
    lane = lax.broadcasted_iota(jnp.int32, dense.shape, 1)
    scale = jnp.sum(jnp.where(lane == expert, dense, 0.0), axis=1, keepdims=True)
    result = piece.astype(jnp.bfloat16).astype(jnp.float32) * scale
    size = keep_out.shape[0]
    keep_out[...] = result[:size]
    for out in send_out:
        out[...] = result[size:].astype(jnp.bfloat16)


def expert_apply(rows, gate_up, down, size):
    _, hidden, width = down.shape
    total = rows.shape[0]
    half = max(size, total // 2)
    inner = jnp.einsum(
        "nd,dgh->gnh", rows[:, :width], gate_up[0], preferred_element_type=jnp.float32
    )
    shapes = [jax.ShapeDtypeStruct((half, width), jnp.float32)]
    if total > half:
        shapes.append(jax.ShapeDtypeStruct((total - half, width), jnp.bfloat16))
    outs = pl.pallas_call(
        down_kernel,
        out_shape=shapes,
        in_specs=whole_specs(3),
        out_specs=whole_specs(len(shapes)),
        compiler_params=LIMIT,
        cost_estimate=pl.CostEstimate(
            flops=2 * total * width * hidden, bytes_accessed=2 << 20, transcendentals=0
        ),
    )(inner, rows, down)
    return outs[0], (outs[1] if total > half else None)


def return_near(keep, send, near):
    for stride in reversed(near):
        keep = keep + swap(send, "exp", stride).astype(jnp.float32)
        half = keep.shape[0] // 2
        if stride != near[0]:
            keep, send = keep[:half], keep[half:].astype(jnp.bfloat16)
    return keep


def mixture_of(rows, gate_up, down):
    tokens = rows.shape[0]
    ctx_strides = strides(lax.axis_size("ctx"))
    exp_strides = strides(lax.axis_size("exp"))
    far, near = exp_strides[:1], exp_strides[1:]

    offsets, chunks, sent = [0], [], rows
    for stride in ctx_strides[:-1]:
        sent = jnp.concatenate([sent, swap(sent, "ctx", stride)], axis=0)
        offsets = offsets + [offset ^ stride for offset in offsets]
    chunks = [(offsets, sent)]
    for stride in ctx_strides[-1:]:
        chunks.append(([offset ^ stride for offset in offsets], swap(sent, "ctx", stride)))

    def gather(piece):
        held = [piece]
        for stride in near:
            held = held + [swap(part, "exp", stride) for part in held]
        return jnp.concatenate(held, axis=0)

    def results(held, size):
        return return_near(*expert_apply(held, gate_up, down, size), near)

    size = sent.shape[0]
    crossed = [
        [gather(swap(piece, "exp", stride)) for stride in far] for _, piece in chunks
    ]
    everything = jnp.concatenate([piece for _, piece in chunks], axis=0)
    everything, crossed[0] = lax.optimization_barrier((everything, crossed[0]))
    home = results(gather(everything), size * len(chunks))
    homes = lax.optimization_barrier(
        [home[number * size : (number + 1) * size] for number in range(len(chunks))]
    )
    total, arrived = None, []
    for (offsets, _), value, away in zip(chunks, homes, crossed):
        for part in away:
            other = results(part, size).astype(jnp.bfloat16)
            value = value + swap(other, "exp", far[0]).astype(jnp.float32)
        value, arrived = lax.optimization_barrier((value, arrived))
        for position, offset in enumerate(offsets):
            block = value[position * tokens : (position + 1) * tokens]
            if offset == 0:
                total = block
            else:
                arrived.append(swap(block.astype(jnp.bfloat16), "ctx", offset))
    for block in arrived:
        total = total + block.astype(jnp.float32)
    return total


def per_device(
    queries,
    pages,
    cached_lengths,
    residual_in,
    out_weight,
    norm_gain,
    expert_ids,
    route_scores,
    expert_input,
    expert_output,
):
    requests = queries.shape[0]
    core_place = lax.axis_index("rep")
    rep_count = lax.axis_size("rep")
    exp_count = lax.axis_size("exp")
    expert_count = lax.axis_size("ctx") * exp_count
    token_block, model_width = residual_in.shape[1:]
    token_count = requests * token_block

    contexts, owns, sents = [], [], []
    for r in range(requests):
        context, own, sent = attention(
            queries[r],
            pages[r],
            cached_lengths[r],
            out_weight,
            token_block,
            (expert_output,),
        )
        contexts.append(context)
        owns.append(own)
        sents.append(sent)
    context = jnp.stack(contexts)

    parts = [jnp.concatenate(owns, axis=0)]
    for step in range(1, exp_count):
        blocks = jnp.concatenate([sent[step - 1] for sent in sents], axis=0)
        parts.append(swap(blocks, "exp", step))
    residual, ids, scores = residual_in, expert_ids, route_scores
    if rep_count > 1:
        share_size = token_block // rep_count
        share = sum(part.astype(jnp.float32) for part in parts).astype(jnp.bfloat16)
        share = share.reshape(requests, token_block, model_width)
        share = lax.psum_scatter(share, "rep", scatter_dimension=1, tiled=True)
        parts = [share.reshape(-1, model_width)]
        residual, ids, scores = (
            lax.dynamic_slice_in_dim(whole, core_place * share_size, share_size, 1)
            for whole in (residual, ids, scores)
        )
    own_hidden, normed = finish(
        parts,
        residual.reshape(-1, model_width),
        norm_gain,
        ids.reshape(-1, ids.shape[2]).T,
        scores.reshape(-1, ids.shape[2]).T,
        expert_count,
    )
    own_hidden = own_hidden.reshape(requests, -1, model_width)
    if rep_count > 1:
        normed = normed.reshape(requests, share_size, -1)
        normed = lax.all_gather(normed, "rep", axis=1, tiled=True)
        normed = normed.reshape(token_count, -1)

    mixture = mixture_of(normed, expert_input, expert_output)
    mixture = mixture.reshape(requests, token_block, model_width)
    if rep_count > 1:
        mixture = lax.psum_scatter(
            mixture.astype(jnp.bfloat16), "rep", scatter_dimension=1, tiled=True
        ).astype(jnp.float32)
    layer_out = (own_hidden.astype(jnp.float32) + mixture).astype(jnp.bfloat16)
    return (context, layer_out)


def solution(mesh):
    in_specs = (
        P("groups", "ctx", ("exp", "rep")),
        P("groups", "ctx", None, "exp"),
        P("groups", None),
        P("groups", ("ctx", "exp"), None),
        P(("exp", "rep"), None),
        P(),
        P("groups", ("ctx", "exp"), None),
        P("groups", ("ctx", "exp"), None),
        P(("ctx", "exp"), None, None, "rep"),
        P(("ctx", "exp"), "rep", None),
    )
    out_specs = (P("groups", "ctx", ("exp", "rep")), P("groups", ("ctx", "exp", "rep"), None))
    return jax.shard_map(
        per_device, mesh=mesh, in_specs=in_specs, out_specs=out_specs, check_vma=False
    )
```

```python
import functools

import jax
import jax.numpy as jnp
from jax import lax
from jax.experimental import pallas as pl
from jax.experimental.pallas import tpu as pltpu
from jax.sharding import PartitionSpec as P

HEAD = 128

floor_value = -1e30
norm_epsilon = 1e-06


def normalize(hidden, norm_gain):
    widened = hidden.astype(jnp.float32)
    mean_square = jnp.mean(widened * widened, axis=-1, keepdims=True)
    return (widened * lax.rsqrt(mean_square + norm_epsilon) * norm_gain).astype(jnp.bfloat16)


def strides(count):
    assert count & (count - 1) == 0
    return [1 << bit for bit in reversed(range(count.bit_length() - 1))]


def swap(value, axis, stride):
    return lax.ppermute(value, axis, [(i, i ^ stride) for i in range(lax.axis_size(axis))])


def shift(value, axis, step):
    count = lax.axis_size(axis)
    return lax.ppermute(value, axis, [(i, (i + step) % count) for i in range(count)])


def whole_specs(count):
    return [pl.BlockSpec(memory_space=pltpu.VMEM)] * count


SMEM_SPEC = pl.BlockSpec(memory_space=pltpu.SMEM)
LIMIT = pltpu.CompilerParams(vmem_limit_bytes=12 * 1024 * 1024)


def stack_heads(queries):
    heads = queries.shape[1] // HEAD
    return jnp.concatenate(
        [queries[:, h * HEAD : (h + 1) * HEAD] for h in range(heads)], axis=0
    )


def page_partial(stacked, keys, values, page, length, place, fresh_block):
    rows, page_size = stacked.shape[0], keys.shape[0]
    slab_size = page_size - fresh_block
    scores = lax.dot_general(
        keys, stacked, (((1,), (1,)), ((), ())), preferred_element_type=jnp.float32
    )
    lanes = HEAD if HEAD % fresh_block == 0 and rows % HEAD == 0 else rows
    offset = lax.broadcasted_iota(jnp.int32, (slab_size, lanes), 0)
    fresh = page * fresh_block + lax.broadcasted_iota(jnp.int32, (fresh_block, lanes), 0)
    lane = lax.broadcasted_iota(jnp.int32, (fresh_block, lanes), 1)
    position = place * fresh_block + lax.rem(lane, fresh_block)
    bias = jnp.concatenate(
        [
            jnp.where(offset < length, 0.0, floor_value),
            jnp.where(fresh <= position, 0.0, floor_value),
        ],
        axis=0,
    )
    masked = scores + jnp.concatenate([bias] * (rows // lanes), axis=1)
    peak = jnp.max(masked, axis=0, keepdims=True)
    weights = jnp.exp((masked - peak) * (HEAD**-0.5))
    total = jnp.sum(weights, axis=0, keepdims=True)
    summed = lax.dot_general(
        values,
        weights.astype(jnp.bfloat16),
        (((0,), (0,)), ((), ())),
        preferred_element_type=jnp.float32,
    )
    return peak, total, summed


def merge(first, second):
    peak = jnp.maximum(first[0], second[0])
    scale_first = jnp.exp((first[0] - peak) * (HEAD**-0.5))
    scale_second = jnp.exp((second[0] - peak) * (HEAD**-0.5))
    return (
        peak,
        first[1] * scale_first + second[1] * scale_second,
        first[2] * scale_first + second[2] * scale_second,
    )


def page_at(offset):
    count = lax.axis_size("ctx")
    return lax.rem(lax.axis_index("ctx") + offset + count, count)


def first_kernel(fresh_block, count, lengths, queries, keys, values, *refs):
    peak_out, total_out, summed_out, lengths_out = refs[-4:]
    for offset in range(count):
        lengths_out[offset : offset + 1, :] = jnp.full(
            (1, lengths_out.shape[1]), lengths[page_at(offset)], jnp.int32
        )
    place = lax.axis_index("ctx")
    peak_out[...], total_out[...], summed_out[...] = page_partial(
        stack_heads(queries[...]),
        keys[...],
        values[...],
        place,
        lengths[place],
        place,
        fresh_block,
    )


def middle_kernel(offsets, fresh_block, queries, lengths, *refs):
    count = len(offsets)
    pages, (peak, total, summed) = refs[: 2 * count], refs[2 * count : 2 * count + 3]
    outs = refs[2 * count + 3 :]
    stacked = stack_heads(queries[...])
    state = (peak[...], total[...], summed[...])
    for number, offset in enumerate(offsets):
        part = page_partial(
            stacked,
            pages[2 * number][...],
            pages[2 * number + 1][...],
            page_at(offset),
            lengths[offset : offset + 1, :],
            lax.axis_index("ctx"),
            fresh_block,
        )
        state = merge(state, part)
    for out, value in zip(outs, state):
        out[...] = value


def late_kernel(
    offset,
    fresh_block,
    queries,
    keys,
    values,
    lengths,
    peak,
    total,
    summed,
    weight,
    context_out,
    own_out,
    *rest,
):
    sent_outs, blocks = rest[:-1], rest[-1]
    page = page_at(offset)
    part = page_partial(
        stack_heads(queries[...]),
        keys[...],
        values[...],
        page,
        lengths[offset : offset + 1, :],
        lax.axis_index("ctx"),
        fresh_block,
    )
    state = merge((peak[...], total[...], summed[...]), part)
    result = jnp.transpose(state[2] / state[1])
    context = jnp.concatenate(
        [
            result[h * fresh_block : (h + 1) * fresh_block]
            for h in range(result.shape[0] // fresh_block)
        ],
        axis=1,
    ).astype(jnp.bfloat16)
    context_out[...] = context
    blocks[...] = jnp.dot(context, weight[...], preferred_element_type=jnp.float32)
    place = lax.axis_index("exp")
    size = own_out.shape[0]
    pick = lambda index: blocks[pl.ds(pl.multiple_of(index * size, size), size), :]
    own_out[...] = pick(place)
    for step, out in enumerate(sent_outs, 1):
        out[...] = pick(place ^ step).astype(jnp.bfloat16)


def attention(queries, pages, lengths, out_weight, token_block, later):
    fresh_block, width = queries.shape
    rows = width // HEAD * fresh_block
    count = lax.axis_size("ctx")
    exp_count = lax.axis_size("exp")
    model_width = out_weight.shape[1]
    own_keys, own_values = pages[:, 0], pages[:, 1]
    held = []
    left_keys, left_values = own_keys, own_values
    right_keys, right_values = own_keys, own_values
    for step in range(1, (count - 1) // 2 + 1):
        left_keys = shift(left_keys, "ctx", 1)
        right_values = shift(right_values, "ctx", -1)
        left_values = shift(left_values, "ctx", 1)
        right_keys = shift(right_keys, "ctx", -1)
        held.append((count - step, left_keys, left_values))
        held.append((step, right_keys, right_values))
    if count % 2 == 0:
        last = (count // 2, shift(left_keys, "ctx", 1), shift(right_values, "ctx", -1))
    else:
        last = held.pop()
    page_flops = 4 * rows * pages.shape[0] * HEAD
    line = jax.ShapeDtypeStruct((1, rows), jnp.float32)
    partial_shape = (line, line, jax.ShapeDtypeStruct((HEAD, rows), jnp.float32))
    *state, page_lengths = pl.pallas_call(
        functools.partial(first_kernel, fresh_block, count),
        out_shape=partial_shape + (jax.ShapeDtypeStruct((count, HEAD), jnp.int32),),
        in_specs=[SMEM_SPEC]
        + whole_specs(3)
        + [pl.BlockSpec(memory_space=pl.ANY)] * (1 + len(later)),
        out_specs=tuple(whole_specs(4)),
        compiler_params=LIMIT,
        cost_estimate=pl.CostEstimate(
            flops=16 * page_flops, bytes_accessed=8 << 20, transcendentals=0
        ),
    )(lengths, queries, own_keys, own_values, out_weight, *later)
    for start in range(0, len(held), 2):
        group = held[start : start + 2]
        operands = [part for _, keys, values in group for part in (keys, values)]
        state = pl.pallas_call(
            functools.partial(middle_kernel, [offset for offset, _, _ in group], fresh_block),
            out_shape=partial_shape,
            in_specs=whole_specs(5 + len(operands)),
            out_specs=tuple(whole_specs(3)),
            compiler_params=LIMIT,
            cost_estimate=pl.CostEstimate(
                flops=len(group) * page_flops, bytes_accessed=2 << 20, transcendentals=0
            ),
        )(queries, page_lengths, *operands, *state)
    block = jax.ShapeDtypeStruct((token_block, model_width), jnp.bfloat16)
    outs = pl.pallas_call(
        functools.partial(late_kernel, last[0], fresh_block),
        out_shape=(
            jax.ShapeDtypeStruct(queries.shape, jnp.bfloat16),
            jax.ShapeDtypeStruct(block.shape, jnp.float32),
        )
        + (block,) * (exp_count - 1),
        in_specs=whole_specs(8),
        out_specs=tuple(whole_specs(1 + exp_count)),
        scratch_shapes=[pltpu.VMEM((fresh_block, model_width), jnp.float32)],
        compiler_params=LIMIT,
        cost_estimate=pl.CostEstimate(
            flops=page_flops + 2 * fresh_block * width * model_width,
            bytes_accessed=6 << 20,
            transcendentals=0,
        ),
    )(queries, last[1], last[2], page_lengths, *state, out_weight)
    return outs[0], outs[1], outs[2:]


def finish_kernel(count, *refs):
    parts, (residual, gain, ids, scores, hidden_out, sent_out) = refs[:count], refs[count:]
    total = residual[...].astype(jnp.float32)
    for part in parts:
        total = total + part[...].astype(jnp.float32)
    hidden = total.astype(jnp.bfloat16)
    hidden_out[...] = hidden
    width = hidden.shape[1]
    sent_out[:, :width] = normalize(hidden, gain[...])
    chosen = jnp.transpose(scores[...])
    ids = jnp.transpose(ids[...])
    combine = (chosen / jnp.sum(chosen, axis=1, keepdims=True)).astype(jnp.bfloat16)
    combine = combine.astype(jnp.float32)
    tokens, choices = chosen.shape
    expert = lax.broadcasted_iota(jnp.int32, (tokens, sent_out.shape[1] - width), 1)
    dense = jnp.zeros(expert.shape, jnp.float32)
    for k in range(choices):
        dense = dense + jnp.where(ids[:, k : k + 1] == expert, combine[:, k : k + 1], 0.0)
    sent_out[:, width:] = dense.astype(jnp.bfloat16)


def finish(parts, residual, norm_gain, ids, scores, expert_count):
    tokens, width = residual.shape
    lanes = -(-expert_count // 128) * 128
    return pl.pallas_call(
        functools.partial(finish_kernel, len(parts)),
        out_shape=(
            jax.ShapeDtypeStruct((tokens, width), jnp.bfloat16),
            jax.ShapeDtypeStruct((tokens, width + lanes), jnp.bfloat16),
        ),
        in_specs=whole_specs(len(parts) + 4),
        out_specs=tuple(whole_specs(2)),
        compiler_params=LIMIT,
        cost_estimate=pl.CostEstimate(
            flops=8 * residual.size, bytes_accessed=1 << 19, transcendentals=0
        ),
    )(*parts, residual, norm_gain[None], ids, scores)


def down_kernel(inner, rows, down, keep_out, *send_out):
    expert = lax.axis_index("ctx") * lax.axis_size("exp") + lax.axis_index("exp")
    gate = inner[0]
    activated = (gate / (1.0 + jnp.exp(-gate)) * inner[1]).astype(jnp.bfloat16)
    piece = jnp.dot(activated, down[0], preferred_element_type=jnp.float32)
    dense = rows[:, piece.shape[1] :].astype(jnp.float32)
    lane = lax.broadcasted_iota(jnp.int32, dense.shape, 1)
    scale = jnp.sum(jnp.where(lane == expert, dense, 0.0), axis=1, keepdims=True)
    result = piece.astype(jnp.bfloat16).astype(jnp.float32) * scale
    size = keep_out.shape[0]
    keep_out[...] = result[:size]
    for out in send_out:
        out[...] = result[size:].astype(jnp.bfloat16)


def expert_apply(rows, gate_up, down, size):
    _, hidden, width = down.shape
    total = rows.shape[0]
    half = max(size, total // 2)
    inner = jnp.einsum(
        "nd,dgh->gnh", rows[:, :width], gate_up[0], preferred_element_type=jnp.float32
    )
    shapes = [jax.ShapeDtypeStruct((half, width), jnp.float32)]
    if total > half:
        shapes.append(jax.ShapeDtypeStruct((total - half, width), jnp.bfloat16))
    outs = pl.pallas_call(
        down_kernel,
        out_shape=shapes,
        in_specs=whole_specs(3),
        out_specs=whole_specs(len(shapes)),
        compiler_params=LIMIT,
        cost_estimate=pl.CostEstimate(
            flops=2 * total * width * hidden, bytes_accessed=2 << 20, transcendentals=0
        ),
    )(inner, rows, down)
    return outs[0], (outs[1] if total > half else None)


def return_near(keep, send, near):
    for stride in reversed(near):
        keep = keep + swap(send, "exp", stride).astype(jnp.float32)
        half = keep.shape[0] // 2
        if stride != near[0]:
            keep, send = keep[:half], keep[half:].astype(jnp.bfloat16)
    return keep


def chunks_of(count):
    chunks = [range(0, count, 2), range(1, count, 4), range(3, count, 4)]
    return [list(chunk) for chunk in chunks if len(chunk)]


def mixture_of(rows, gate_up, down):
    tokens = rows.shape[0]
    exp_strides = strides(lax.axis_size("exp"))
    far, near = exp_strides[:1], exp_strides[1:]
    chunks = chunks_of(lax.axis_size("ctx"))

    def gather(piece):
        held = [piece]
        for stride in near:
            held = held + [swap(part, "exp", stride) for part in held]
        return jnp.concatenate(held, axis=0)

    def results(held, size):
        return return_near(*expert_apply(held, gate_up, down, size), near)

    sent = []
    for chunk in chunks:
        blocks = [rows if offset == 0 else swap(rows, "ctx", offset) for offset in chunk]
        sent.append(jnp.concatenate(blocks, axis=0))
    crossed = []
    for piece in sent:
        arrived = [swap(piece, "exp", stride) for stride in far]
        if crossed:
            arrived, _ = lax.optimization_barrier((arrived, crossed[-1]))
        crossed.append([gather(part) for part in arrived])
    everything = jnp.concatenate(sent, axis=0)
    everything, _ = lax.optimization_barrier((everything, crossed[0]))
    home = results(gather(everything), everything.shape[0])
    homes, start = [], 0
    for piece in sent:
        homes.append(home[start : start + piece.shape[0]])
        start += piece.shape[0]
    homes = lax.optimization_barrier(homes)
    total, arrived = None, []
    for chunk, value, away in zip(chunks, homes, crossed):
        for part in away:
            other = results(part, value.shape[0]).astype(jnp.bfloat16)
            value = value + swap(other, "exp", far[0]).astype(jnp.float32)
        if arrived:
            value, _ = lax.optimization_barrier((value, arrived[0]))
        for position, offset in enumerate(chunk):
            block = value[position * tokens : (position + 1) * tokens]
            if offset == 0:
                total = block
            else:
                arrived.append(swap(block.astype(jnp.bfloat16), "ctx", offset))
    for block in arrived:
        total = total + block.astype(jnp.float32)
    return total


def per_device(
    queries,
    pages,
    cached_lengths,
    residual_in,
    out_weight,
    norm_gain,
    expert_ids,
    route_scores,
    expert_input,
    expert_output,
):
    requests = queries.shape[0]
    core_place = lax.axis_index("rep")
    rep_count = lax.axis_size("rep")
    exp_count = lax.axis_size("exp")
    expert_count = lax.axis_size("ctx") * exp_count
    token_block, model_width = residual_in.shape[1:]
    token_count = requests * token_block

    contexts, owns, sents = [], [], []
    for r in range(requests):
        context, own, sent = attention(
            queries[r],
            pages[r],
            cached_lengths[r],
            out_weight,
            token_block,
            (expert_output,),
        )
        contexts.append(context)
        owns.append(own)
        sents.append(sent)
    context = jnp.stack(contexts)

    parts = [jnp.concatenate(owns, axis=0)]
    for step in range(1, exp_count):
        blocks = jnp.concatenate([sent[step - 1] for sent in sents], axis=0)
        parts.append(swap(blocks, "exp", step))
    residual, ids, scores = residual_in, expert_ids, route_scores
    if rep_count > 1:
        share_size = token_block // rep_count
        share = sum(part.astype(jnp.float32) for part in parts).astype(jnp.bfloat16)
        share = share.reshape(requests, token_block, model_width)
        share = lax.psum_scatter(share, "rep", scatter_dimension=1, tiled=True)
        parts = [share.reshape(-1, model_width)]
        residual, ids, scores = (
            lax.dynamic_slice_in_dim(whole, core_place * share_size, share_size, 1)
            for whole in (residual, ids, scores)
        )
    own_hidden, normed = finish(
        parts,
        residual.reshape(-1, model_width),
        norm_gain,
        ids.reshape(-1, ids.shape[2]).T,
        scores.reshape(-1, ids.shape[2]).T,
        expert_count,
    )
    own_hidden = own_hidden.reshape(requests, -1, model_width)
    if rep_count > 1:
        normed = normed.reshape(requests, share_size, -1)
        normed = lax.all_gather(normed, "rep", axis=1, tiled=True)
        normed = normed.reshape(token_count, -1)

    mixture = mixture_of(normed, expert_input, expert_output)
    mixture = mixture.reshape(requests, token_block, model_width)
    if rep_count > 1:
        mixture = lax.psum_scatter(
            mixture.astype(jnp.bfloat16), "rep", scatter_dimension=1, tiled=True
        ).astype(jnp.float32)
    layer_out = (own_hidden.astype(jnp.float32) + mixture).astype(jnp.bfloat16)
    return (context, layer_out)


def solution(mesh):
    in_specs = (
        P("groups", "ctx", ("exp", "rep")),
        P("groups", "ctx", None, "exp"),
        P("groups", None),
        P("groups", ("ctx", "exp"), None),
        P(("exp", "rep"), None),
        P(),
        P("groups", ("ctx", "exp"), None),
        P("groups", ("ctx", "exp"), None),
        P(("ctx", "exp"), None, None, "rep"),
        P(("ctx", "exp"), "rep", None),
    )
    out_specs = (P("groups", "ctx", ("exp", "rep")), P("groups", ("ctx", "exp", "rep"), None))
    return jax.shard_map(
        per_device, mesh=mesh, in_specs=in_specs, out_specs=out_specs, check_vma=False
    )
```

```python
import functools

import jax
import jax.numpy as jnp
from jax import lax
from jax.experimental import pallas as pl
from jax.experimental.pallas import tpu as pltpu
from jax.sharding import PartitionSpec as P

HEAD = 128

floor_value = -1e30
norm_epsilon = 1e-06


def normalize(hidden, norm_gain):
    widened = hidden.astype(jnp.float32)
    mean_square = jnp.mean(widened * widened, axis=-1, keepdims=True)
    return (widened * lax.rsqrt(mean_square + norm_epsilon) * norm_gain).astype(jnp.bfloat16)


def strides(count):
    assert count & (count - 1) == 0
    return [1 << bit for bit in reversed(range(count.bit_length() - 1))]


def swap(value, axis, stride):
    return lax.ppermute(value, axis, [(i, i ^ stride) for i in range(lax.axis_size(axis))])


def shift(value, axis, step):
    count = lax.axis_size(axis)
    return lax.ppermute(value, axis, [(i, (i + step) % count) for i in range(count)])


def whole_specs(count):
    return [pl.BlockSpec(memory_space=pltpu.VMEM)] * count


SMEM_SPEC = pl.BlockSpec(memory_space=pltpu.SMEM)
LIMIT = pltpu.CompilerParams(vmem_limit_bytes=12 * 1024 * 1024)


def stack_heads(queries):
    heads = queries.shape[1] // HEAD
    return jnp.concatenate(
        [queries[:, h * HEAD : (h + 1) * HEAD] for h in range(heads)], axis=0
    )


def page_partial(stacked, keys, values, page, length, place, fresh_block):
    rows, page_size = stacked.shape[0], keys.shape[0]
    slab_size = page_size - fresh_block
    scores = lax.dot_general(
        keys, stacked, (((1,), (1,)), ((), ())), preferred_element_type=jnp.float32
    )
    lanes = HEAD if HEAD % fresh_block == 0 and rows % HEAD == 0 else rows
    offset = lax.broadcasted_iota(jnp.int32, (slab_size, lanes), 0)
    fresh = page * fresh_block + lax.broadcasted_iota(jnp.int32, (fresh_block, lanes), 0)
    lane = lax.broadcasted_iota(jnp.int32, (fresh_block, lanes), 1)
    position = place * fresh_block + lax.rem(lane, fresh_block)
    bias = jnp.concatenate(
        [
            jnp.where(offset < length, 0.0, floor_value),
            jnp.where(fresh <= position, 0.0, floor_value),
        ],
        axis=0,
    )
    masked = scores + jnp.concatenate([bias] * (rows // lanes), axis=1)
    peak = jnp.max(masked, axis=0, keepdims=True)
    weights = jnp.exp((masked - peak) * (HEAD**-0.5))
    total = jnp.sum(weights, axis=0, keepdims=True)
    summed = lax.dot_general(
        values,
        weights.astype(jnp.bfloat16),
        (((0,), (0,)), ((), ())),
        preferred_element_type=jnp.float32,
    )
    return peak, total, summed


def merge(first, second):
    peak = jnp.maximum(first[0], second[0])
    scale_first = jnp.exp((first[0] - peak) * (HEAD**-0.5))
    scale_second = jnp.exp((second[0] - peak) * (HEAD**-0.5))
    return (
        peak,
        first[1] * scale_first + second[1] * scale_second,
        first[2] * scale_first + second[2] * scale_second,
    )


def page_at(offset):
    count = lax.axis_size("ctx")
    return lax.rem(lax.axis_index("ctx") + offset + count, count)


def first_kernel(fresh_block, count, lengths, queries, keys, values, *refs):
    peak_out, total_out, summed_out, lengths_out = refs[-4:]
    for offset in range(count):
        lengths_out[offset : offset + 1, :] = jnp.full(
            (1, lengths_out.shape[1]), lengths[page_at(offset)], jnp.int32
        )
    place = lax.axis_index("ctx")
    peak_out[...], total_out[...], summed_out[...] = page_partial(
        stack_heads(queries[...]),
        keys[...],
        values[...],
        place,
        lengths[place],
        place,
        fresh_block,
    )


def middle_kernel(offsets, fresh_block, queries, lengths, *refs):
    count = len(offsets)
    pages, (peak, total, summed) = refs[: 2 * count], refs[2 * count : 2 * count + 3]
    outs = refs[2 * count + 3 :]
    stacked = stack_heads(queries[...])
    state = (peak[...], total[...], summed[...])
    for number, offset in enumerate(offsets):
        part = page_partial(
            stacked,
            pages[2 * number][...],
            pages[2 * number + 1][...],
            page_at(offset),
            lengths[offset : offset + 1, :],
            lax.axis_index("ctx"),
            fresh_block,
        )
        state = merge(state, part)
    for out, value in zip(outs, state):
        out[...] = value


def late_kernel(
    offset,
    fresh_block,
    queries,
    keys,
    values,
    lengths,
    peak,
    total,
    summed,
    weight,
    context_out,
    own_out,
    *rest,
):
    sent_outs, blocks = rest[:-1], rest[-1]
    page = page_at(offset)
    part = page_partial(
        stack_heads(queries[...]),
        keys[...],
        values[...],
        page,
        lengths[offset : offset + 1, :],
        lax.axis_index("ctx"),
        fresh_block,
    )
    state = merge((peak[...], total[...], summed[...]), part)
    result = jnp.transpose(state[2] / state[1])
    context = jnp.concatenate(
        [
            result[h * fresh_block : (h + 1) * fresh_block]
            for h in range(result.shape[0] // fresh_block)
        ],
        axis=1,
    ).astype(jnp.bfloat16)
    context_out[...] = context
    blocks[...] = jnp.dot(context, weight[...], preferred_element_type=jnp.float32)
    place = lax.axis_index("exp")
    size = own_out.shape[0]
    pick = lambda index: blocks[pl.ds(pl.multiple_of(index * size, size), size), :]
    own_out[...] = pick(place)
    for step, out in enumerate(sent_outs, 1):
        out[...] = pick(place ^ step).astype(jnp.bfloat16)


def attention(queries, pages, lengths, out_weight, token_block, later):
    fresh_block, width = queries.shape
    rows = width // HEAD * fresh_block
    count = lax.axis_size("ctx")
    exp_count = lax.axis_size("exp")
    model_width = out_weight.shape[1]
    own_keys, own_values = pages[:, 0], pages[:, 1]
    held = []
    left_keys, left_values = own_keys, own_values
    right_keys, right_values = own_keys, own_values
    for step in range(1, (count - 1) // 2 + 1):
        left_keys = shift(left_keys, "ctx", 1)
        right_values = shift(right_values, "ctx", -1)
        left_values = shift(left_values, "ctx", 1)
        right_keys = shift(right_keys, "ctx", -1)
        held.append((count - step, left_keys, left_values))
        held.append((step, right_keys, right_values))
    if count % 2 == 0:
        last = (count // 2, shift(left_keys, "ctx", 1), shift(right_values, "ctx", -1))
    else:
        last = held.pop()
    page_flops = 4 * rows * pages.shape[0] * HEAD
    line = jax.ShapeDtypeStruct((1, rows), jnp.float32)
    partial_shape = (line, line, jax.ShapeDtypeStruct((HEAD, rows), jnp.float32))
    *state, page_lengths = pl.pallas_call(
        functools.partial(first_kernel, fresh_block, count),
        out_shape=partial_shape + (jax.ShapeDtypeStruct((count, HEAD), jnp.int32),),
        in_specs=[SMEM_SPEC]
        + whole_specs(3)
        + [pl.BlockSpec(memory_space=pl.ANY)] * (1 + len(later)),
        out_specs=tuple(whole_specs(4)),
        compiler_params=LIMIT,
        cost_estimate=pl.CostEstimate(
            flops=16 * page_flops, bytes_accessed=8 << 20, transcendentals=0
        ),
    )(lengths, queries, own_keys, own_values, out_weight, *later)
    for start in range(0, len(held), 2):
        group = held[start : start + 2]
        operands = [part for _, keys, values in group for part in (keys, values)]
        state = pl.pallas_call(
            functools.partial(middle_kernel, [offset for offset, _, _ in group], fresh_block),
            out_shape=partial_shape,
            in_specs=whole_specs(5 + len(operands)),
            out_specs=tuple(whole_specs(3)),
            compiler_params=LIMIT,
            cost_estimate=pl.CostEstimate(
                flops=len(group) * page_flops, bytes_accessed=2 << 20, transcendentals=0
            ),
        )(queries, page_lengths, *operands, *state)
    block = jax.ShapeDtypeStruct((token_block, model_width), jnp.bfloat16)
    outs = pl.pallas_call(
        functools.partial(late_kernel, last[0], fresh_block),
        out_shape=(
            jax.ShapeDtypeStruct(queries.shape, jnp.bfloat16),
            jax.ShapeDtypeStruct(block.shape, jnp.float32),
        )
        + (block,) * (exp_count - 1),
        in_specs=whole_specs(8),
        out_specs=tuple(whole_specs(1 + exp_count)),
        scratch_shapes=[pltpu.VMEM((fresh_block, model_width), jnp.float32)],
        compiler_params=LIMIT,
        cost_estimate=pl.CostEstimate(
            flops=page_flops + 2 * fresh_block * width * model_width,
            bytes_accessed=6 << 20,
            transcendentals=0,
        ),
    )(queries, last[1], last[2], page_lengths, *state, out_weight)
    return outs[0], outs[1], outs[2:]


def finish_kernel(count, *refs):
    parts, (residual, gain, ids, scores, hidden_out, sent_out) = refs[:count], refs[count:]
    total = residual[...].astype(jnp.float32)
    for part in parts:
        total = total + part[...].astype(jnp.float32)
    hidden = total.astype(jnp.bfloat16)
    hidden_out[...] = hidden
    width = hidden.shape[1]
    sent_out[:, :width] = normalize(hidden, gain[...])
    chosen = jnp.transpose(scores[...])
    ids = jnp.transpose(ids[...])
    combine = (chosen / jnp.sum(chosen, axis=1, keepdims=True)).astype(jnp.bfloat16)
    combine = combine.astype(jnp.float32)
    tokens, choices = chosen.shape
    expert = lax.broadcasted_iota(jnp.int32, (tokens, sent_out.shape[1] - width), 1)
    dense = jnp.zeros(expert.shape, jnp.float32)
    for k in range(choices):
        dense = dense + jnp.where(ids[:, k : k + 1] == expert, combine[:, k : k + 1], 0.0)
    sent_out[:, width:] = dense.astype(jnp.bfloat16)


def finish(parts, residual, norm_gain, ids, scores, expert_count):
    tokens, width = residual.shape
    lanes = -(-expert_count // 128) * 128
    return pl.pallas_call(
        functools.partial(finish_kernel, len(parts)),
        out_shape=(
            jax.ShapeDtypeStruct((tokens, width), jnp.bfloat16),
            jax.ShapeDtypeStruct((tokens, width + lanes), jnp.bfloat16),
        ),
        in_specs=whole_specs(len(parts) + 4),
        out_specs=tuple(whole_specs(2)),
        compiler_params=LIMIT,
        cost_estimate=pl.CostEstimate(
            flops=8 * residual.size, bytes_accessed=1 << 19, transcendentals=0
        ),
    )(*parts, residual, norm_gain[None], ids, scores)


def down_kernel(inner, rows, down, keep_out, *send_out):
    expert = lax.axis_index("ctx") * lax.axis_size("exp") + lax.axis_index("exp")
    gate = inner[0]
    activated = (gate / (1.0 + jnp.exp(-gate)) * inner[1]).astype(jnp.bfloat16)
    piece = jnp.dot(activated, down[0], preferred_element_type=jnp.float32)
    dense = rows[:, piece.shape[1] :].astype(jnp.float32)
    lane = lax.broadcasted_iota(jnp.int32, dense.shape, 1)
    scale = jnp.sum(jnp.where(lane == expert, dense, 0.0), axis=1, keepdims=True)
    result = piece.astype(jnp.bfloat16).astype(jnp.float32) * scale
    size = keep_out.shape[0]
    keep_out[...] = result[:size]
    for out in send_out:
        out[...] = result[size:].astype(jnp.bfloat16)


def expert_apply(rows, gate_up, down, size):
    _, hidden, width = down.shape
    total = rows.shape[0]
    half = max(size, total // 2)
    inner = jnp.einsum(
        "nd,dgh->gnh", rows[:, :width], gate_up[0], preferred_element_type=jnp.float32
    )
    shapes = [jax.ShapeDtypeStruct((half, width), jnp.float32)]
    if total > half:
        shapes.append(jax.ShapeDtypeStruct((total - half, width), jnp.bfloat16))
    outs = pl.pallas_call(
        down_kernel,
        out_shape=shapes,
        in_specs=whole_specs(3),
        out_specs=whole_specs(len(shapes)),
        compiler_params=LIMIT,
        cost_estimate=pl.CostEstimate(
            flops=2 * total * width * hidden, bytes_accessed=2 << 20, transcendentals=0
        ),
    )(inner, rows, down)
    return outs[0], (outs[1] if total > half else None)


def return_near(keep, send, near):
    for stride in reversed(near):
        keep = keep + swap(send, "exp", stride).astype(jnp.float32)
        half = keep.shape[0] // 2
        if stride != near[0]:
            keep, send = keep[:half], keep[half:].astype(jnp.bfloat16)
    return keep


def chunks_of(count):
    chunks = [range((count + 1) // 2), range((count + 1) // 2, count)]
    return [list(chunk) for chunk in chunks if len(chunk)]


def mixture_of(rows, gate_up, down):
    tokens = rows.shape[0]
    exp_strides = strides(lax.axis_size("exp"))
    far, near = exp_strides[:1], exp_strides[1:]
    chunks = chunks_of(lax.axis_size("ctx"))

    def gather(piece):
        held = [piece]
        for stride in near:
            held = held + [swap(part, "exp", stride) for part in held]
        return jnp.concatenate(held, axis=0)

    def results(held, size):
        return return_near(*expert_apply(held, gate_up, down, size), near)

    sent = []
    for chunk in chunks:
        blocks = [rows if offset == 0 else swap(rows, "ctx", offset) for offset in chunk]
        sent.append(jnp.concatenate(blocks, axis=0))
    crossed = []
    for piece in sent:
        if crossed:
            piece, _ = lax.optimization_barrier((piece, arrived))
        arrived = [swap(piece, "exp", stride) for stride in far]
        crossed.append([gather(part) for part in arrived])
    everything = jnp.concatenate(sent, axis=0)
    everything, _ = lax.optimization_barrier((everything, crossed[0]))
    home = results(gather(everything), everything.shape[0])
    homes, start = [], 0
    for piece in sent:
        homes.append(home[start : start + piece.shape[0]])
        start += piece.shape[0]
    homes = lax.optimization_barrier(homes)
    total, arrived = None, []
    for chunk, value, away in zip(chunks, homes, crossed):
        for part in away:
            other = results(part, value.shape[0]).astype(jnp.bfloat16)
            value = value + swap(other, "exp", far[0]).astype(jnp.float32)
        if arrived:
            value, _ = lax.optimization_barrier((value, arrived[0]))
        for position, offset in enumerate(chunk):
            block = value[position * tokens : (position + 1) * tokens]
            if offset == 0:
                total = block
            else:
                arrived.append(swap(block.astype(jnp.bfloat16), "ctx", offset))
    for block in arrived:
        total = total + block.astype(jnp.float32)
    return total


def per_device(
    queries,
    pages,
    cached_lengths,
    residual_in,
    out_weight,
    norm_gain,
    expert_ids,
    route_scores,
    expert_input,
    expert_output,
):
    requests = queries.shape[0]
    core_place = lax.axis_index("rep")
    rep_count = lax.axis_size("rep")
    exp_count = lax.axis_size("exp")
    expert_count = lax.axis_size("ctx") * exp_count
    token_block, model_width = residual_in.shape[1:]
    token_count = requests * token_block

    contexts, owns, sents = [], [], []
    for r in range(requests):
        context, own, sent = attention(
            queries[r],
            pages[r],
            cached_lengths[r],
            out_weight,
            token_block,
            (expert_output,),
        )
        contexts.append(context)
        owns.append(own)
        sents.append(sent)
    context = jnp.stack(contexts)

    parts = [jnp.concatenate(owns, axis=0)]
    for step in range(1, exp_count):
        blocks = jnp.concatenate([sent[step - 1] for sent in sents], axis=0)
        parts.append(swap(blocks, "exp", step))
    residual, ids, scores = residual_in, expert_ids, route_scores
    if rep_count > 1:
        share_size = token_block // rep_count
        share = sum(part.astype(jnp.float32) for part in parts).astype(jnp.bfloat16)
        share = share.reshape(requests, token_block, model_width)
        share = lax.psum_scatter(share, "rep", scatter_dimension=1, tiled=True)
        parts = [share.reshape(-1, model_width)]
        residual, ids, scores = (
            lax.dynamic_slice_in_dim(whole, core_place * share_size, share_size, 1)
            for whole in (residual, ids, scores)
        )
    own_hidden, normed = finish(
        parts,
        residual.reshape(-1, model_width),
        norm_gain,
        ids.reshape(-1, ids.shape[2]).T,
        scores.reshape(-1, ids.shape[2]).T,
        expert_count,
    )
    own_hidden = own_hidden.reshape(requests, -1, model_width)
    if rep_count > 1:
        normed = normed.reshape(requests, share_size, -1)
        normed = lax.all_gather(normed, "rep", axis=1, tiled=True)
        normed = normed.reshape(token_count, -1)

    mixture = mixture_of(normed, expert_input, expert_output)
    mixture = mixture.reshape(requests, token_block, model_width)
    if rep_count > 1:
        mixture = lax.psum_scatter(
            mixture.astype(jnp.bfloat16), "rep", scatter_dimension=1, tiled=True
        ).astype(jnp.float32)
    layer_out = (own_hidden.astype(jnp.float32) + mixture).astype(jnp.bfloat16)
    return (context, layer_out)


def solution(mesh):
    in_specs = (
        P("groups", "ctx", ("exp", "rep")),
        P("groups", "ctx", None, "exp"),
        P("groups", None),
        P("groups", ("ctx", "exp"), None),
        P(("exp", "rep"), None),
        P(),
        P("groups", ("ctx", "exp"), None),
        P("groups", ("ctx", "exp"), None),
        P(("ctx", "exp"), None, None, "rep"),
        P(("ctx", "exp"), "rep", None),
    )
    out_specs = (P("groups", "ctx", ("exp", "rep")), P("groups", ("ctx", "exp", "rep"), None))
    return jax.shard_map(
        per_device, mesh=mesh, in_specs=in_specs, out_specs=out_specs, check_vma=False
    )
```

```python
import functools

import jax
import jax.numpy as jnp
from jax import lax
from jax.experimental import pallas as pl
from jax.experimental.pallas import tpu as pltpu
from jax.sharding import PartitionSpec as P

HEAD = 128

floor_value = -1e30
norm_epsilon = 1e-06


def normalize(hidden, norm_gain):
    widened = hidden.astype(jnp.float32)
    mean_square = jnp.mean(widened * widened, axis=-1, keepdims=True)
    return (widened * lax.rsqrt(mean_square + norm_epsilon) * norm_gain).astype(jnp.bfloat16)


def strides(count):
    assert count & (count - 1) == 0
    return [1 << bit for bit in reversed(range(count.bit_length() - 1))]


def swap(value, axis, stride):
    return lax.ppermute(value, axis, [(i, i ^ stride) for i in range(lax.axis_size(axis))])


def shift(value, axis, step):
    count = lax.axis_size(axis)
    return lax.ppermute(value, axis, [(i, (i + step) % count) for i in range(count)])


def whole_specs(count):
    return [pl.BlockSpec(memory_space=pltpu.VMEM)] * count


SMEM_SPEC = pl.BlockSpec(memory_space=pltpu.SMEM)
LIMIT = pltpu.CompilerParams(vmem_limit_bytes=12 * 1024 * 1024)


def stack_heads(queries):
    heads = queries.shape[1] // HEAD
    return jnp.concatenate(
        [queries[:, h * HEAD : (h + 1) * HEAD] for h in range(heads)], axis=0
    )


def page_partial(stacked, keys, values, page, length, place, fresh_block):
    rows, page_size = stacked.shape[0], keys.shape[0]
    slab_size = page_size - fresh_block
    scores = lax.dot_general(
        keys, stacked, (((1,), (1,)), ((), ())), preferred_element_type=jnp.float32
    )
    lanes = HEAD if HEAD % fresh_block == 0 and rows % HEAD == 0 else rows
    offset = lax.broadcasted_iota(jnp.int32, (slab_size, lanes), 0)
    fresh = page * fresh_block + lax.broadcasted_iota(jnp.int32, (fresh_block, lanes), 0)
    lane = lax.broadcasted_iota(jnp.int32, (fresh_block, lanes), 1)
    position = place * fresh_block + lax.rem(lane, fresh_block)
    bias = jnp.concatenate(
        [
            jnp.where(offset < length, 0.0, floor_value),
            jnp.where(fresh <= position, 0.0, floor_value),
        ],
        axis=0,
    )
    masked = scores + jnp.concatenate([bias] * (rows // lanes), axis=1)
    peak = jnp.max(masked, axis=0, keepdims=True)
    weights = jnp.exp((masked - peak) * (HEAD**-0.5))
    total = jnp.sum(weights, axis=0, keepdims=True)
    summed = lax.dot_general(
        values,
        weights.astype(jnp.bfloat16),
        (((0,), (0,)), ((), ())),
        preferred_element_type=jnp.float32,
    )
    return peak, total, summed


def merge(first, second):
    peak = jnp.maximum(first[0], second[0])
    scale_first = jnp.exp((first[0] - peak) * (HEAD**-0.5))
    scale_second = jnp.exp((second[0] - peak) * (HEAD**-0.5))
    return (
        peak,
        first[1] * scale_first + second[1] * scale_second,
        first[2] * scale_first + second[2] * scale_second,
    )


def page_at(offset):
    count = lax.axis_size("ctx")
    return lax.rem(lax.axis_index("ctx") + offset + count, count)


def first_kernel(fresh_block, count, lengths, queries, keys, values, *refs):
    peak_out, total_out, summed_out, lengths_out = refs[-4:]
    for offset in range(count):
        lengths_out[offset : offset + 1, :] = jnp.full(
            (1, lengths_out.shape[1]), lengths[page_at(offset)], jnp.int32
        )
    place = lax.axis_index("ctx")
    peak_out[...], total_out[...], summed_out[...] = page_partial(
        stack_heads(queries[...]),
        keys[...],
        values[...],
        place,
        lengths[place],
        place,
        fresh_block,
    )


def middle_kernel(offsets, fresh_block, queries, lengths, *refs):
    count = len(offsets)
    pages, (peak, total, summed) = refs[: 2 * count], refs[2 * count : 2 * count + 3]
    outs = refs[2 * count + 3 :]
    stacked = stack_heads(queries[...])
    state = (peak[...], total[...], summed[...])
    for number, offset in enumerate(offsets):
        part = page_partial(
            stacked,
            pages[2 * number][...],
            pages[2 * number + 1][...],
            page_at(offset),
            lengths[offset : offset + 1, :],
            lax.axis_index("ctx"),
            fresh_block,
        )
        state = merge(state, part)
    for out, value in zip(outs, state):
        out[...] = value


def late_kernel(
    offset,
    fresh_block,
    queries,
    keys,
    values,
    lengths,
    peak,
    total,
    summed,
    weight,
    context_out,
    own_out,
    *rest,
):
    sent_outs, blocks = rest[:-1], rest[-1]
    page = page_at(offset)
    part = page_partial(
        stack_heads(queries[...]),
        keys[...],
        values[...],
        page,
        lengths[offset : offset + 1, :],
        lax.axis_index("ctx"),
        fresh_block,
    )
    state = merge((peak[...], total[...], summed[...]), part)
    result = jnp.transpose(state[2] / state[1])
    context = jnp.concatenate(
        [
            result[h * fresh_block : (h + 1) * fresh_block]
            for h in range(result.shape[0] // fresh_block)
        ],
        axis=1,
    ).astype(jnp.bfloat16)
    context_out[...] = context
    blocks[...] = jnp.dot(context, weight[...], preferred_element_type=jnp.float32)
    place = lax.axis_index("exp")
    size = own_out.shape[0]
    pick = lambda index: blocks[pl.ds(pl.multiple_of(index * size, size), size), :]
    own_out[...] = pick(place)
    for step, out in enumerate(sent_outs, 1):
        out[...] = pick(place ^ step).astype(jnp.bfloat16)


def attention(queries, pages, lengths, out_weight, token_block, later):
    fresh_block, width = queries.shape
    rows = width // HEAD * fresh_block
    count = lax.axis_size("ctx")
    exp_count = lax.axis_size("exp")
    model_width = out_weight.shape[1]
    own_keys, own_values = pages[:, 0], pages[:, 1]
    held = []
    left_keys, left_values = own_keys, own_values
    right_keys, right_values = own_keys, own_values
    for step in range(1, (count - 1) // 2 + 1):
        left_keys = shift(left_keys, "ctx", 1)
        right_values = shift(right_values, "ctx", -1)
        left_values = shift(left_values, "ctx", 1)
        right_keys = shift(right_keys, "ctx", -1)
        held.append((count - step, left_keys, left_values))
        held.append((step, right_keys, right_values))
    if count % 2 == 0:
        last = (count // 2, shift(left_keys, "ctx", 1), shift(right_values, "ctx", -1))
    else:
        last = held.pop()
    page_flops = 4 * rows * pages.shape[0] * HEAD
    line = jax.ShapeDtypeStruct((1, rows), jnp.float32)
    partial_shape = (line, line, jax.ShapeDtypeStruct((HEAD, rows), jnp.float32))
    *state, page_lengths = pl.pallas_call(
        functools.partial(first_kernel, fresh_block, count),
        out_shape=partial_shape + (jax.ShapeDtypeStruct((count, HEAD), jnp.int32),),
        in_specs=[SMEM_SPEC]
        + whole_specs(3)
        + [pl.BlockSpec(memory_space=pl.ANY)] * (1 + len(later)),
        out_specs=tuple(whole_specs(4)),
        compiler_params=LIMIT,
        cost_estimate=pl.CostEstimate(
            flops=16 * page_flops, bytes_accessed=8 << 20, transcendentals=0
        ),
    )(lengths, queries, own_keys, own_values, out_weight, *later)
    for start in range(0, len(held), 2):
        group = held[start : start + 2]
        operands = [part for _, keys, values in group for part in (keys, values)]
        state = pl.pallas_call(
            functools.partial(middle_kernel, [offset for offset, _, _ in group], fresh_block),
            out_shape=partial_shape,
            in_specs=whole_specs(5 + len(operands)),
            out_specs=tuple(whole_specs(3)),
            compiler_params=LIMIT,
            cost_estimate=pl.CostEstimate(
                flops=len(group) * page_flops, bytes_accessed=2 << 20, transcendentals=0
            ),
        )(queries, page_lengths, *operands, *state)
    block = jax.ShapeDtypeStruct((token_block, model_width), jnp.bfloat16)
    outs = pl.pallas_call(
        functools.partial(late_kernel, last[0], fresh_block),
        out_shape=(
            jax.ShapeDtypeStruct(queries.shape, jnp.bfloat16),
            jax.ShapeDtypeStruct(block.shape, jnp.float32),
        )
        + (block,) * (exp_count - 1),
        in_specs=whole_specs(8),
        out_specs=tuple(whole_specs(1 + exp_count)),
        scratch_shapes=[pltpu.VMEM((fresh_block, model_width), jnp.float32)],
        compiler_params=LIMIT,
        cost_estimate=pl.CostEstimate(
            flops=page_flops + 2 * fresh_block * width * model_width,
            bytes_accessed=6 << 20,
            transcendentals=0,
        ),
    )(queries, last[1], last[2], page_lengths, *state, out_weight)
    return outs[0], outs[1], outs[2:]


def finish_kernel(count, *refs):
    parts, (residual, gain, ids, scores, hidden_out, sent_out) = refs[:count], refs[count:]
    total = residual[...].astype(jnp.float32)
    for part in parts:
        total = total + part[...].astype(jnp.float32)
    hidden = total.astype(jnp.bfloat16)
    hidden_out[...] = hidden
    width = hidden.shape[1]
    sent_out[:, :width] = normalize(hidden, gain[...])
    chosen = jnp.transpose(scores[...])
    ids = jnp.transpose(ids[...])
    combine = (chosen / jnp.sum(chosen, axis=1, keepdims=True)).astype(jnp.bfloat16)
    combine = combine.astype(jnp.float32)
    tokens, choices = chosen.shape
    expert = lax.broadcasted_iota(jnp.int32, (tokens, sent_out.shape[1] - width), 1)
    dense = jnp.zeros(expert.shape, jnp.float32)
    for k in range(choices):
        dense = dense + jnp.where(ids[:, k : k + 1] == expert, combine[:, k : k + 1], 0.0)
    sent_out[:, width:] = dense.astype(jnp.bfloat16)


def finish(parts, residual, norm_gain, ids, scores, expert_count):
    tokens, width = residual.shape
    lanes = -(-expert_count // 128) * 128
    return pl.pallas_call(
        functools.partial(finish_kernel, len(parts)),
        out_shape=(
            jax.ShapeDtypeStruct((tokens, width), jnp.bfloat16),
            jax.ShapeDtypeStruct((tokens, width + lanes), jnp.bfloat16),
        ),
        in_specs=whole_specs(len(parts) + 4),
        out_specs=tuple(whole_specs(2)),
        compiler_params=LIMIT,
        cost_estimate=pl.CostEstimate(
            flops=8 * residual.size, bytes_accessed=1 << 19, transcendentals=0
        ),
    )(*parts, residual, norm_gain[None], ids, scores)


def down_kernel(inner, rows, down, *outs):
    expert = lax.axis_index("ctx") * lax.axis_size("exp") + lax.axis_index("exp")
    gate = inner[0]
    activated = (gate / (1.0 + jnp.exp(-gate)) * inner[1]).astype(jnp.bfloat16)
    piece = jnp.dot(activated, down[0], preferred_element_type=jnp.float32)
    dense = rows[:, piece.shape[1] :].astype(jnp.float32)
    lane = lax.broadcasted_iota(jnp.int32, dense.shape, 1)
    scale = jnp.sum(jnp.where(lane == expert, dense, 0.0), axis=1, keepdims=True)
    result = piece.astype(jnp.bfloat16).astype(jnp.float32) * scale
    start = 0
    for out in outs:
        out[...] = result[start : start + out.shape[0]].astype(out.dtype)
        start += out.shape[0]


def expert_apply(groups, gate_up, down, split):
    _, hidden, width = down.shape
    rows = jnp.concatenate(groups, axis=0)
    total = rows.shape[0]
    inner = jnp.einsum(
        "nd,dgh->gnh", rows[:, :width], gate_up[0], preferred_element_type=jnp.float32
    )
    shapes = []
    for group in groups:
        size = group.shape[0]
        if split:
            shapes.append(jax.ShapeDtypeStruct((size // 2, width), jnp.float32))
            shapes.append(jax.ShapeDtypeStruct((size // 2, width), jnp.bfloat16))
        else:
            shapes.append(jax.ShapeDtypeStruct((size, width), jnp.float32))
    outs = pl.pallas_call(
        down_kernel,
        out_shape=shapes,
        in_specs=whole_specs(3),
        out_specs=whole_specs(len(shapes)),
        compiler_params=LIMIT,
        cost_estimate=pl.CostEstimate(
            flops=2 * total * width * hidden, bytes_accessed=2 << 20, transcendentals=0
        ),
    )(inner, rows, down)
    return list(zip(outs[::2], outs[1::2])) if split else [(out, None) for out in outs]


def return_near(keep, send, near):
    for stride in reversed(near):
        keep = keep + swap(send, "exp", stride).astype(jnp.float32)
        half = keep.shape[0] // 2
        if stride != near[0]:
            keep, send = keep[:half], keep[half:].astype(jnp.bfloat16)
    return keep


def chunks_of(count):
    chunks = [range((count + 1) // 2), range((count + 1) // 2, count)]
    return [list(chunk) for chunk in chunks if len(chunk)]


def mixture_of(rows, gate_up, down):
    tokens = rows.shape[0]
    exp_strides = strides(lax.axis_size("exp"))
    far, near = exp_strides[:1], exp_strides[1:]
    chunks = chunks_of(lax.axis_size("ctx"))

    def gather(piece):
        held = [piece]
        for stride in near:
            held = held + [swap(part, "exp", stride) for part in held]
        return jnp.concatenate(held, axis=0)

    sent = [
        {offset: rows if offset == 0 else swap(rows, "ctx", offset) for offset in chunk}
        for chunk in chunks
    ]
    joined = [jnp.concatenate(list(blocks.values()), axis=0) for blocks in sent]

    def cross(number):
        if not far:
            return None
        if number == 0:
            return swap(joined[0], "exp", far[0])
        blocks = list(sent[number].values())
        blocks[0], _ = lax.optimization_barrier((blocks[0], crossed[0]))
        return jnp.concatenate([swap(block, "exp", far[0]) for block in blocks], axis=0)

    crossed = []
    for number in range(len(chunks)):
        crossed.append(cross(number))
    groups = [[] if piece is None else [gather(piece)] for piece in crossed]
    everything = jnp.concatenate(joined, axis=0)
    everything, _ = lax.optimization_barrier((everything, crossed[0]))
    groups[-1].append(gather(everything))
    values = [
        [return_near(*pair, near) for pair in expert_apply(held, gate_up, down, bool(near))]
        if held
        else []
        for held in groups
    ]
    home = values[-1].pop()
    homes, start = [], 0
    for piece in joined:
        homes.append(home[start : start + piece.shape[0]])
        start += piece.shape[0]
    homes = lax.optimization_barrier(homes)
    total, arrived = None, []
    for number, (chunk, value, others) in enumerate(zip(chunks, homes, values)):
        size = value.shape[0]
        blocks = [value[low : low + tokens] for low in range(0, size, tokens)]
        for other in others:
            other = other.astype(jnp.bfloat16)
            if number == 0:
                other = swap(other, "exp", far[0])
                others = [other[low : low + tokens] for low in range(0, size, tokens)]
            else:
                others = [
                    swap(other[low : low + tokens], "exp", far[0])
                    for low in range(0, size, tokens)
                ]
            blocks = [
                block + other.astype(jnp.float32) for block, other in zip(blocks, others)
            ]
        if arrived:
            blocks[-1], _ = lax.optimization_barrier((blocks[-1], arrived[0]))
        for offset, block in zip(chunk, blocks):
            if offset == 0:
                total = block
            else:
                arrived.append(swap(block.astype(jnp.bfloat16), "ctx", offset))
    for block in arrived:
        total = total + block.astype(jnp.float32)
    return total


def per_device(
    queries,
    pages,
    cached_lengths,
    residual_in,
    out_weight,
    norm_gain,
    expert_ids,
    route_scores,
    expert_input,
    expert_output,
):
    requests = queries.shape[0]
    core_place = lax.axis_index("rep")
    rep_count = lax.axis_size("rep")
    exp_count = lax.axis_size("exp")
    expert_count = lax.axis_size("ctx") * exp_count
    token_block, model_width = residual_in.shape[1:]
    token_count = requests * token_block

    contexts, owns, sents = [], [], []
    for r in range(requests):
        context, own, sent = attention(
            queries[r],
            pages[r],
            cached_lengths[r],
            out_weight,
            token_block,
            (expert_output,),
        )
        contexts.append(context)
        owns.append(own)
        sents.append(sent)
    context = jnp.stack(contexts)

    parts = [jnp.concatenate(owns, axis=0)]
    for step in range(1, exp_count):
        blocks = jnp.concatenate([sent[step - 1] for sent in sents], axis=0)
        parts.append(swap(blocks, "exp", step))
    residual, ids, scores = residual_in, expert_ids, route_scores
    if rep_count > 1:
        share_size = token_block // rep_count
        share = sum(part.astype(jnp.float32) for part in parts).astype(jnp.bfloat16)
        share = share.reshape(requests, token_block, model_width)
        share = lax.psum_scatter(share, "rep", scatter_dimension=1, tiled=True)
        parts = [share.reshape(-1, model_width)]
        residual, ids, scores = (
            lax.dynamic_slice_in_dim(whole, core_place * share_size, share_size, 1)
            for whole in (residual, ids, scores)
        )
    own_hidden, normed = finish(
        parts,
        residual.reshape(-1, model_width),
        norm_gain,
        ids.reshape(-1, ids.shape[2]).T,
        scores.reshape(-1, ids.shape[2]).T,
        expert_count,
    )
    own_hidden = own_hidden.reshape(requests, -1, model_width)
    if rep_count > 1:
        normed = normed.reshape(requests, share_size, -1)
        normed = lax.all_gather(normed, "rep", axis=1, tiled=True)
        normed = normed.reshape(token_count, -1)

    mixture = mixture_of(normed, expert_input, expert_output)
    mixture = mixture.reshape(requests, token_block, model_width)
    if rep_count > 1:
        mixture = lax.psum_scatter(
            mixture.astype(jnp.bfloat16), "rep", scatter_dimension=1, tiled=True
        ).astype(jnp.float32)
    layer_out = (own_hidden.astype(jnp.float32) + mixture).astype(jnp.bfloat16)
    return (context, layer_out)


def solution(mesh):
    in_specs = (
        P("groups", "ctx", ("exp", "rep")),
        P("groups", "ctx", None, "exp"),
        P("groups", None),
        P("groups", ("ctx", "exp"), None),
        P(("exp", "rep"), None),
        P(),
        P("groups", ("ctx", "exp"), None),
        P("groups", ("ctx", "exp"), None),
        P(("ctx", "exp"), None, None, "rep"),
        P(("ctx", "exp"), "rep", None),
    )
    out_specs = (P("groups", "ctx", ("exp", "rep")), P("groups", ("ctx", "exp", "rep"), None))
    return jax.shard_map(
        per_device, mesh=mesh, in_specs=in_specs, out_specs=out_specs, check_vma=False
    )
```

```python
import functools

import jax
import jax.numpy as jnp
from jax import lax
from jax.experimental import pallas as pl
from jax.experimental.pallas import tpu as pltpu
from jax.sharding import PartitionSpec as P

HEAD = 128

floor_value = -1e30
norm_epsilon = 1e-06


def normalize(hidden, norm_gain):
    widened = hidden.astype(jnp.float32)
    mean_square = jnp.mean(widened * widened, axis=-1, keepdims=True)
    return (widened * lax.rsqrt(mean_square + norm_epsilon) * norm_gain).astype(jnp.bfloat16)


def strides(count):
    assert count & (count - 1) == 0
    return [1 << bit for bit in reversed(range(count.bit_length() - 1))]


def swap(value, axis, stride):
    return lax.ppermute(value, axis, [(i, i ^ stride) for i in range(lax.axis_size(axis))])


def shift(value, axis, step):
    count = lax.axis_size(axis)
    return lax.ppermute(value, axis, [(i, (i + step) % count) for i in range(count)])


def whole_specs(count):
    return [pl.BlockSpec(memory_space=pltpu.VMEM)] * count


SMEM_SPEC = pl.BlockSpec(memory_space=pltpu.SMEM)
LIMIT = pltpu.CompilerParams(vmem_limit_bytes=12 * 1024 * 1024)


def stack_heads(queries):
    heads = queries.shape[1] // HEAD
    return jnp.concatenate(
        [queries[:, h * HEAD : (h + 1) * HEAD] for h in range(heads)], axis=0
    )


def page_partial(stacked, keys, values, page, length, place, fresh_block):
    rows, page_size = stacked.shape[0], keys.shape[0]
    slab_size = page_size - fresh_block
    scores = lax.dot_general(
        keys, stacked, (((1,), (1,)), ((), ())), preferred_element_type=jnp.float32
    )
    lanes = HEAD if HEAD % fresh_block == 0 and rows % HEAD == 0 else rows
    offset = lax.broadcasted_iota(jnp.int32, (slab_size, lanes), 0)
    fresh = page * fresh_block + lax.broadcasted_iota(jnp.int32, (fresh_block, lanes), 0)
    lane = lax.broadcasted_iota(jnp.int32, (fresh_block, lanes), 1)
    position = place * fresh_block + lax.rem(lane, fresh_block)
    bias = jnp.concatenate(
        [
            jnp.where(offset < length, 0.0, floor_value),
            jnp.where(fresh <= position, 0.0, floor_value),
        ],
        axis=0,
    )
    masked = scores + jnp.concatenate([bias] * (rows // lanes), axis=1)
    peak = jnp.max(masked, axis=0, keepdims=True)
    weights = jnp.exp((masked - peak) * (HEAD**-0.5))
    total = jnp.sum(weights, axis=0, keepdims=True)
    summed = lax.dot_general(
        values,
        weights.astype(jnp.bfloat16),
        (((0,), (0,)), ((), ())),
        preferred_element_type=jnp.float32,
    )
    return peak, total, summed


def merge(first, second):
    peak = jnp.maximum(first[0], second[0])
    scale_first = jnp.exp((first[0] - peak) * (HEAD**-0.5))
    scale_second = jnp.exp((second[0] - peak) * (HEAD**-0.5))
    return (
        peak,
        first[1] * scale_first + second[1] * scale_second,
        first[2] * scale_first + second[2] * scale_second,
    )


def page_at(offset):
    count = lax.axis_size("ctx")
    return lax.rem(lax.axis_index("ctx") + offset + count, count)


def first_kernel(fresh_block, count, lengths, queries, keys, values, *refs):
    peak_out, total_out, summed_out, lengths_out = refs[-4:]
    for offset in range(count):
        lengths_out[offset : offset + 1, :] = jnp.full(
            (1, lengths_out.shape[1]), lengths[page_at(offset)], jnp.int32
        )
    place = lax.axis_index("ctx")
    peak_out[...], total_out[...], summed_out[...] = page_partial(
        stack_heads(queries[...]),
        keys[...],
        values[...],
        place,
        lengths[place],
        place,
        fresh_block,
    )


def middle_kernel(offsets, fresh_block, queries, lengths, *refs):
    count = len(offsets)
    pages, (peak, total, summed) = refs[: 2 * count], refs[2 * count : 2 * count + 3]
    outs = refs[2 * count + 3 :]
    stacked = stack_heads(queries[...])
    state = (peak[...], total[...], summed[...])
    for number, offset in enumerate(offsets):
        part = page_partial(
            stacked,
            pages[2 * number][...],
            pages[2 * number + 1][...],
            page_at(offset),
            lengths[offset : offset + 1, :],
            lax.axis_index("ctx"),
            fresh_block,
        )
        state = merge(state, part)
    for out, value in zip(outs, state):
        out[...] = value


def late_kernel(
    offset,
    fresh_block,
    sent_count,
    queries,
    keys,
    values,
    lengths,
    peak,
    total,
    summed,
    weight,
    *rest,
):
    context_out, own_out = rest[-sent_count - 3 : -sent_count - 1]
    sent_outs, blocks = rest[-sent_count - 1 : -1], rest[-1]
    page = page_at(offset)
    part = page_partial(
        stack_heads(queries[...]),
        keys[...],
        values[...],
        page,
        lengths[offset : offset + 1, :],
        lax.axis_index("ctx"),
        fresh_block,
    )
    state = merge((peak[...], total[...], summed[...]), part)
    result = jnp.transpose(state[2] / state[1])
    context = jnp.concatenate(
        [
            result[h * fresh_block : (h + 1) * fresh_block]
            for h in range(result.shape[0] // fresh_block)
        ],
        axis=1,
    ).astype(jnp.bfloat16)
    context_out[...] = context
    blocks[...] = jnp.dot(context, weight[...], preferred_element_type=jnp.float32)
    place = lax.axis_index("exp")
    size = own_out.shape[0]
    pick = lambda index: blocks[pl.ds(pl.multiple_of(index * size, size), size), :]
    own_out[...] = pick(place)
    for step, out in enumerate(sent_outs, 1):
        out[...] = pick(place ^ step).astype(jnp.bfloat16)


def attention(queries, pages, lengths, out_weight, token_block, later, swapped):
    fresh_block, width = queries.shape
    rows = width // HEAD * fresh_block
    count = lax.axis_size("ctx")
    exp_count = lax.axis_size("exp")
    model_width = out_weight.shape[1]
    own_keys, own_values = pages[:, 0], pages[:, 1]
    held = []
    left_keys, left_values = own_keys, own_values
    right_keys, right_values = own_keys, own_values
    for step in range(1, (count - 1) // 2 + 1):
        left_keys = shift(left_keys, "ctx", 1)
        right_values = shift(right_values, "ctx", -1)
        left_values = shift(left_values, "ctx", 1)
        right_keys = shift(right_keys, "ctx", -1)
        held.append((count - step, left_keys, left_values))
        held.append((step, right_keys, right_values))
    if count % 2 == 0:
        last = (count // 2, shift(left_keys, "ctx", 1), shift(right_values, "ctx", -1))
    else:
        last = held.pop()
    page_flops = 4 * rows * pages.shape[0] * HEAD
    line = jax.ShapeDtypeStruct((1, rows), jnp.float32)
    partial_shape = (line, line, jax.ShapeDtypeStruct((HEAD, rows), jnp.float32))
    *state, page_lengths = pl.pallas_call(
        functools.partial(first_kernel, fresh_block, count),
        out_shape=partial_shape + (jax.ShapeDtypeStruct((count, HEAD), jnp.int32),),
        in_specs=[SMEM_SPEC]
        + whole_specs(3)
        + [pl.BlockSpec(memory_space=pl.ANY)] * (1 + len(later)),
        out_specs=tuple(whole_specs(4)),
        compiler_params=LIMIT,
        cost_estimate=pl.CostEstimate(
            flops=16 * page_flops, bytes_accessed=8 << 20, transcendentals=0
        ),
    )(lengths, queries, own_keys, own_values, out_weight, *later)
    for start in range(0, len(held), 2):
        group = held[start : start + 2]
        operands = [part for _, keys, values in group for part in (keys, values)]
        state = pl.pallas_call(
            functools.partial(middle_kernel, [offset for offset, _, _ in group], fresh_block),
            out_shape=partial_shape,
            in_specs=whole_specs(5 + len(operands)),
            out_specs=tuple(whole_specs(3)),
            compiler_params=LIMIT,
            cost_estimate=pl.CostEstimate(
                flops=len(group) * page_flops, bytes_accessed=2 << 20, transcendentals=0
            ),
        )(queries, page_lengths, *operands, *state)
    block = jax.ShapeDtypeStruct((token_block, model_width), jnp.bfloat16)
    outs = pl.pallas_call(
        functools.partial(late_kernel, last[0], fresh_block, exp_count - 1),
        out_shape=(
            jax.ShapeDtypeStruct(queries.shape, jnp.bfloat16),
            jax.ShapeDtypeStruct(block.shape, jnp.float32),
        )
        + (block,) * (exp_count - 1),
        in_specs=whole_specs(8) + [pl.BlockSpec(memory_space=pl.ANY)] * len(swapped),
        out_specs=tuple(whole_specs(1 + exp_count)),
        scratch_shapes=[pltpu.VMEM((fresh_block, model_width), jnp.float32)],
        compiler_params=LIMIT,
        cost_estimate=pl.CostEstimate(
            flops=page_flops + 2 * fresh_block * width * model_width,
            bytes_accessed=6 << 20,
            transcendentals=0,
        ),
    )(queries, last[1], last[2], page_lengths, *state, out_weight, *swapped)
    return outs[0], outs[1], outs[2:]


def finish_kernel(count, *refs):
    parts, (residual, gain, ids, scores, hidden_out, sent_out) = refs[:count], refs[count:]
    total = residual[...].astype(jnp.float32)
    for part in parts:
        total = total + part[...].astype(jnp.float32)
    hidden = total.astype(jnp.bfloat16)
    hidden_out[...] = hidden
    width = hidden.shape[1]
    sent_out[:, :width] = normalize(hidden, gain[...])
    chosen = jnp.transpose(scores[...])
    ids = jnp.transpose(ids[...])
    combine = (chosen / jnp.sum(chosen, axis=1, keepdims=True)).astype(jnp.bfloat16)
    combine = combine.astype(jnp.float32)
    tokens, choices = chosen.shape
    expert = lax.broadcasted_iota(jnp.int32, (tokens, sent_out.shape[1] - width), 1)
    dense = jnp.zeros(expert.shape, jnp.float32)
    for k in range(choices):
        dense = dense + jnp.where(ids[:, k : k + 1] == expert, combine[:, k : k + 1], 0.0)
    sent_out[:, width:] = dense.astype(jnp.bfloat16)


def finish(parts, residual, norm_gain, ids, scores, expert_count):
    tokens, width = residual.shape
    lanes = -(-expert_count // 128) * 128
    return pl.pallas_call(
        functools.partial(finish_kernel, len(parts)),
        out_shape=(
            jax.ShapeDtypeStruct((tokens, width), jnp.bfloat16),
            jax.ShapeDtypeStruct((tokens, width + lanes), jnp.bfloat16),
        ),
        in_specs=whole_specs(len(parts) + 4),
        out_specs=tuple(whole_specs(2)),
        compiler_params=LIMIT,
        cost_estimate=pl.CostEstimate(
            flops=8 * residual.size, bytes_accessed=1 << 19, transcendentals=0
        ),
    )(*parts, residual, norm_gain[None], ids, scores)


def down_kernel(offsets, rows, *refs):
    count = len(offsets)
    inners, downs, outs = refs[:count], refs[count : 2 * count], refs[2 * count :]
    dense = rows[:, outs[0].shape[1] :].astype(jnp.float32)
    lane = lax.broadcasted_iota(jnp.int32, dense.shape, 1)
    base = lax.axis_index("ctx") * lax.axis_size("exp")
    total = 0.0
    for offset, inner, down in zip(offsets, inners, downs):
        gate = inner[0]
        activated = (gate / (1.0 + jnp.exp(-gate)) * inner[1]).astype(jnp.bfloat16)
        piece = jnp.dot(activated, down[0], preferred_element_type=jnp.float32)
        expert = base + (lax.axis_index("exp") ^ offset)
        scale = jnp.sum(jnp.where(lane == expert, dense, 0.0), axis=1, keepdims=True)
        total = total + piece.astype(jnp.bfloat16).astype(jnp.float32) * scale
    start = 0
    for out in outs:
        out[...] = total[start : start + out.shape[0]].astype(out.dtype)
        start += out.shape[0]


def expert_apply(groups, kinds, weights):
    count = len(weights)
    rows = jnp.concatenate(groups, axis=0)
    _, hidden, width = weights[0][2].shape
    inners = [
        jnp.einsum("nd,dgh->gnh", rows[:, :width], gate_up[0], preferred_element_type=jnp.float32)
        for _, gate_up, _ in weights
    ]

    return pl.pallas_call(
        functools.partial(down_kernel, [offset for offset, _, _ in weights]),
        out_shape=[
            jax.ShapeDtypeStruct((group.shape[0], width), kind)
            for group, kind in zip(groups, kinds)
        ],
        in_specs=whole_specs(1 + 2 * count),
        out_specs=whole_specs(len(groups)),
        compiler_params=LIMIT,
        cost_estimate=pl.CostEstimate(
            flops=2 * count * rows.shape[0] * width * hidden,
            bytes_accessed=2 << 20,
            transcendentals=0,
        ),
    )(rows, *inners, *[down for _, _, down in weights])


def near_weights(gate_up, down):
    held = [(0, gate_up, down)]
    for stride in strides(lax.axis_size("exp"))[1:]:
        held = held + [
            (offset ^ stride, swap(first, "exp", stride), swap(second, "exp", stride))
            for offset, first, second in held
        ]
    return held


def chunks_of(count):
    chunks = [range((count + 1) // 2, count), range((count + 1) // 2)]
    return [list(chunk) for chunk in chunks if len(chunk)]


def mixture_of(rows, weights):
    tokens = rows.shape[0]
    far = strides(lax.axis_size("exp"))[:1]
    chunks = chunks_of(lax.axis_size("ctx"))

    joined = [
        jnp.concatenate(
            [rows if offset == 0 else swap(rows, "ctx", offset) for offset in chunk], axis=0
        )
        for chunk in chunks
    ]
    crossed = []
    for piece in joined if far else []:
        crossed.append(swap(piece, "exp", far[0]))
    *homes, first = expert_apply(
        joined + (crossed or joined)[:1], [jnp.float32] * len(joined) + [jnp.bfloat16], weights
    )
    total, arrived = None, []
    for number, (chunk, value) in enumerate(zip(chunks, homes)):
        if far:
            other = first
            if number:
                (other,) = expert_apply(crossed[number : number + 1], [jnp.bfloat16], weights)
            value = value + swap(other, "exp", far[0]).astype(jnp.float32)
        for position, offset in enumerate(chunk):
            block = value[position * tokens : (position + 1) * tokens]
            if offset == 0:
                total = block
            else:
                arrived.append(swap(block.astype(jnp.bfloat16), "ctx", offset))
    for block in arrived:
        total = total + block.astype(jnp.float32)
    return total


def per_device(
    queries,
    pages,
    cached_lengths,
    residual_in,
    out_weight,
    norm_gain,
    expert_ids,
    route_scores,
    expert_input,
    expert_output,
):
    requests = queries.shape[0]
    core_place = lax.axis_index("rep")
    rep_count = lax.axis_size("rep")
    exp_count = lax.axis_size("exp")
    expert_count = lax.axis_size("ctx") * exp_count
    token_block, model_width = residual_in.shape[1:]
    token_count = requests * token_block

    weights = near_weights(expert_input, expert_output)
    swapped = [part for _, *pair in weights[1:] for part in pair]
    contexts, owns, sents = [], [], []
    for r in range(requests):
        context, own, sent = attention(
            queries[r],
            pages[r],
            cached_lengths[r],
            out_weight,
            token_block,
            (expert_output,),
            swapped if r == 0 else (),
        )
        contexts.append(context)
        owns.append(own)
        sents.append(sent)
    context = jnp.stack(contexts)

    parts = [jnp.concatenate(owns, axis=0)]
    for step in range(1, exp_count):
        blocks = jnp.concatenate([sent[step - 1] for sent in sents], axis=0)
        parts.append(swap(blocks, "exp", step))
    residual, ids, scores = residual_in, expert_ids, route_scores
    if rep_count > 1:
        share_size = token_block // rep_count
        share = sum(part.astype(jnp.float32) for part in parts).astype(jnp.bfloat16)
        share = share.reshape(requests, token_block, model_width)
        share = lax.psum_scatter(share, "rep", scatter_dimension=1, tiled=True)
        parts = [share.reshape(-1, model_width)]
        residual, ids, scores = (
            lax.dynamic_slice_in_dim(whole, core_place * share_size, share_size, 1)
            for whole in (residual, ids, scores)
        )
    own_hidden, normed = finish(
        parts,
        residual.reshape(-1, model_width),
        norm_gain,
        ids.reshape(-1, ids.shape[2]).T,
        scores.reshape(-1, ids.shape[2]).T,
        expert_count,
    )
    own_hidden = own_hidden.reshape(requests, -1, model_width)
    if rep_count > 1:
        normed = normed.reshape(requests, share_size, -1)
        normed = lax.all_gather(normed, "rep", axis=1, tiled=True)
        normed = normed.reshape(token_count, -1)

    mixture = mixture_of(normed, weights)
    mixture = mixture.reshape(requests, token_block, model_width)
    if rep_count > 1:
        mixture = lax.psum_scatter(
            mixture.astype(jnp.bfloat16), "rep", scatter_dimension=1, tiled=True
        ).astype(jnp.float32)
    layer_out = (own_hidden.astype(jnp.float32) + mixture).astype(jnp.bfloat16)
    return (context, layer_out)


def solution(mesh):
    in_specs = (
        P("groups", "ctx", ("exp", "rep")),
        P("groups", "ctx", None, "exp"),
        P("groups", None),
        P("groups", ("ctx", "exp"), None),
        P(("exp", "rep"), None),
        P(),
        P("groups", ("ctx", "exp"), None),
        P("groups", ("ctx", "exp"), None),
        P(("ctx", "exp"), None, None, "rep"),
        P(("ctx", "exp"), "rep", None),
    )
    out_specs = (P("groups", "ctx", ("exp", "rep")), P("groups", ("ctx", "exp", "rep"), None))
    return jax.shard_map(
        per_device, mesh=mesh, in_specs=in_specs, out_specs=out_specs, check_vma=False
    )
```

```python
import functools

import jax
import jax.numpy as jnp
from jax import lax
from jax.experimental import pallas as pl
from jax.experimental.pallas import tpu as pltpu
from jax.sharding import PartitionSpec as P

HEAD = 128

floor_value = -1e30
norm_epsilon = 1e-06


def normalize(hidden, norm_gain):
    widened = hidden.astype(jnp.float32)
    mean_square = jnp.mean(widened * widened, axis=-1, keepdims=True)
    return (widened * lax.rsqrt(mean_square + norm_epsilon) * norm_gain).astype(jnp.bfloat16)


def strides(count):
    assert count & (count - 1) == 0
    return [1 << bit for bit in reversed(range(count.bit_length() - 1))]


def swap(value, axis, stride):
    return lax.ppermute(value, axis, [(i, i ^ stride) for i in range(lax.axis_size(axis))])


def shift(value, axis, step):
    count = lax.axis_size(axis)
    return lax.ppermute(value, axis, [(i, (i + step) % count) for i in range(count)])


def whole_specs(count):
    return [pl.BlockSpec(memory_space=pltpu.VMEM)] * count


SMEM_SPEC = pl.BlockSpec(memory_space=pltpu.SMEM)
LIMIT = pltpu.CompilerParams(vmem_limit_bytes=12 * 1024 * 1024)


def stack_heads(queries):
    heads = queries.shape[1] // HEAD
    return jnp.concatenate(
        [queries[:, h * HEAD : (h + 1) * HEAD] for h in range(heads)], axis=0
    )


def page_partial(stacked, keys, values, page, length, place, fresh_block):
    rows, page_size = stacked.shape[0], keys.shape[0]
    slab_size = page_size - fresh_block
    scores = lax.dot_general(
        keys, stacked, (((1,), (1,)), ((), ())), preferred_element_type=jnp.float32
    )
    lanes = HEAD if HEAD % fresh_block == 0 and rows % HEAD == 0 else rows
    offset = lax.broadcasted_iota(jnp.int32, (slab_size, lanes), 0)
    fresh = page * fresh_block + lax.broadcasted_iota(jnp.int32, (fresh_block, lanes), 0)
    lane = lax.broadcasted_iota(jnp.int32, (fresh_block, lanes), 1)
    position = place * fresh_block + lax.rem(lane, fresh_block)
    bias = jnp.concatenate(
        [
            jnp.where(offset < length, 0.0, floor_value),
            jnp.where(fresh <= position, 0.0, floor_value),
        ],
        axis=0,
    )
    masked = scores + jnp.concatenate([bias] * (rows // lanes), axis=1)
    peak = jnp.max(masked, axis=0, keepdims=True)
    weights = jnp.exp((masked - peak) * (HEAD**-0.5))
    total = jnp.sum(weights, axis=0, keepdims=True)
    summed = lax.dot_general(
        values,
        weights.astype(jnp.bfloat16),
        (((0,), (0,)), ((), ())),
        preferred_element_type=jnp.float32,
    )
    return peak, total, summed


def merge(first, second):
    peak = jnp.maximum(first[0], second[0])
    scale_first = jnp.exp((first[0] - peak) * (HEAD**-0.5))
    scale_second = jnp.exp((second[0] - peak) * (HEAD**-0.5))
    return (
        peak,
        first[1] * scale_first + second[1] * scale_second,
        first[2] * scale_first + second[2] * scale_second,
    )


def ring_page(offset):
    count = lax.axis_size("ctx")
    return lax.rem(lax.axis_index("ctx") + offset + count, count)


def at_end():
    place = lax.axis_index("ctx")
    return (place == 0) | (place == lax.axis_size("ctx") - 1)


def line_page(at_ends, inside):
    place = lax.axis_index("ctx")
    return jnp.where(at_end(), place ^ at_ends, place ^ inside)


def page_order():
    count = lax.axis_size("ctx")
    if count == 4:
        return [functools.partial(line_page, *pair) for pair in ((1, 1), (2, 3), (3, 2))]
    steps = [sign * step for step in range(1, (count - 1) // 2 + 1) for sign in (-1, 1)]
    return [functools.partial(ring_page, step) for step in steps + [count // 2] * (1 - count % 2)]


def ring_pages(keys, values):
    count = lax.axis_size("ctx")
    held = []
    left_keys, left_values, right_keys, right_values = keys, values, keys, values
    for step in range(1, (count - 1) // 2 + 1):
        left_keys = shift(left_keys, "ctx", 1)
        right_values = shift(right_values, "ctx", -1)
        left_values = shift(left_values, "ctx", 1)
        right_keys = shift(right_keys, "ctx", -1)
        held.append([(left_keys, left_values)])
        held.append([(right_keys, right_values)])
    if count % 2 == 0:
        held.append([(shift(left_keys, "ctx", 1), shift(right_values, "ctx", -1))])
    return held


def line_pages(keys, values, weight_held, own_done):
    send = lambda part, pairs: lax.ppermute(part, "ctx", pairs)
    after = lambda part, other: lax.optimization_barrier((part, other))[0]
    across, outward = [(1, 2), (2, 1)], [(1, 0), (2, 3)]
    beside = [send(part, [(0, 1), (1, 0), (2, 3), (3, 2)]) for part in (keys, values)]
    middle = [send(part, across) for part in (keys, values)]
    handed = [send(after(middle[0], weight_held), outward), send(middle[1], outward)]
    farther = [send(part, across) for part in beside]
    last = [send(after(farther[0], own_done), outward), send(farther[1], outward)]
    return [[beside], [handed, middle], [last, farther]]


def hold_kernel(weight, out):
    out[...] = jnp.zeros(out.shape, out.dtype)


def first_kernel(fresh_block, pages, lengths, queries, keys, values, *refs):
    peak_out, total_out, summed_out, lengths_out = refs[-4:]
    for row, page in enumerate(pages):
        lengths_out[row : row + 1, :] = jnp.full(
            (1, lengths_out.shape[1]), lengths[page()], jnp.int32
        )
    place = lax.axis_index("ctx")
    peak_out[...], total_out[...], summed_out[...] = page_partial(
        stack_heads(queries[...]),
        keys[...],
        values[...],
        place,
        lengths[place],
        place,
        fresh_block,
    )


def page_refs(ways, refs):
    keys, values = refs[0][...], refs[1][...]
    if ways == 2:
        keys = jnp.where(at_end(), keys, refs[2][...])
        values = jnp.where(at_end(), values, refs[3][...])
    return keys, values, refs[2 * ways :]


def middle_kernel(row, parts, fresh_block, queries, lengths, *refs):
    stacked = stack_heads(queries[...])
    (peak, total, summed), refs, outs = refs[:3], refs[3:-3], refs[-3:]
    state = (peak[...], total[...], summed[...])
    for number, (page, ways) in enumerate(parts):
        keys, values, refs = page_refs(ways, refs)
        part = page_partial(
            stacked,
            keys,
            values,
            page(),
            lengths[row + number : row + number + 1, :],
            lax.axis_index("ctx"),
            fresh_block,
        )
        state = merge(state, part)
    for out, value in zip(outs, state):
        out[...] = value


def late_kernel(row, part, fresh_block, sent_count, queries, lengths, peak, total, summed, *refs):
    page, ways = part
    keys, values, refs = page_refs(ways, refs)
    weight = refs[0]
    context_out, own_out, *sent_outs, blocks = refs[-sent_count - 3 :]
    part = page_partial(
        stack_heads(queries[...]),
        keys,
        values,
        page(),
        lengths[row : row + 1, :],
        lax.axis_index("ctx"),
        fresh_block,
    )
    state = merge((peak[...], total[...], summed[...]), part)
    result = jnp.transpose(state[2] / state[1])
    context = jnp.concatenate(
        [
            result[h * fresh_block : (h + 1) * fresh_block]
            for h in range(result.shape[0] // fresh_block)
        ],
        axis=1,
    ).astype(jnp.bfloat16)
    context_out[...] = context
    blocks[...] = jnp.dot(context, weight[...], preferred_element_type=jnp.float32)
    place = lax.axis_index("exp")
    size = own_out.shape[0]
    pick = lambda index: blocks[pl.ds(pl.multiple_of(index * size, size), size), :]
    own_out[...] = pick(place)
    for step, out in enumerate(sent_outs, 1):
        out[...] = pick(place ^ step).astype(jnp.bfloat16)


def attention(queries, pages, lengths, out_weight, token_block, swapped):
    fresh_block, width = queries.shape
    rows = width // HEAD * fresh_block
    count = lax.axis_size("ctx")
    exp_count = lax.axis_size("exp")
    model_width = out_weight.shape[1]
    own_keys, own_values = pages[:, 0], pages[:, 1]
    order = page_order()
    anywhere = pl.BlockSpec(memory_space=pl.ANY)
    weight_held = pl.pallas_call(
        hold_kernel,
        out_shape=jax.ShapeDtypeStruct((8, HEAD), jnp.float32),
        in_specs=[anywhere],
        out_specs=whole_specs(1)[0],
        compiler_params=LIMIT,
        cost_estimate=pl.CostEstimate(flops=0, bytes_accessed=4 << 20, transcendentals=0),
    )(out_weight)
    page_flops = 4 * rows * pages.shape[0] * HEAD
    line = jax.ShapeDtypeStruct((1, rows), jnp.float32)
    partial_shape = (line, line, jax.ShapeDtypeStruct((HEAD, rows), jnp.float32))
    *state, page_lengths = pl.pallas_call(
        functools.partial(first_kernel, fresh_block, order),
        out_shape=partial_shape + (jax.ShapeDtypeStruct((len(order), HEAD), jnp.int32),),
        in_specs=[SMEM_SPEC] + whole_specs(3) + [anywhere],
        out_specs=tuple(whole_specs(4)),
        compiler_params=LIMIT,
        cost_estimate=pl.CostEstimate(
            flops=16 * page_flops, bytes_accessed=8 << 20, transcendentals=0
        ),
    )(lengths, queries, own_keys, own_values, weight_held)
    if count == 4:
        sources = line_pages(own_keys, own_values, weight_held, page_lengths)
    else:
        sources = ring_pages(own_keys, own_values)
    held = list(zip(order, sources))
    for start in range(0, len(held) - 1, 2):
        group = held[start : min(start + 2, len(held) - 1)]
        operands = [part for _, sources in group for pair in sources for part in pair]
        state = pl.pallas_call(
            functools.partial(
                middle_kernel,
                start,
                [(page, len(sources)) for page, sources in group],
                fresh_block,
            ),
            out_shape=partial_shape,
            in_specs=whole_specs(5 + len(operands)),
            out_specs=tuple(whole_specs(3)),
            compiler_params=LIMIT,
            cost_estimate=pl.CostEstimate(
                flops=len(group) * page_flops, bytes_accessed=2 << 20, transcendentals=0
            ),
        )(queries, page_lengths, *state, *operands)
    page, sources = held[-1]
    operands = [part for pair in sources for part in pair]
    block = jax.ShapeDtypeStruct((token_block, model_width), jnp.bfloat16)
    outs = pl.pallas_call(
        functools.partial(
            late_kernel, len(held) - 1, (page, len(sources)), fresh_block, exp_count - 1
        ),
        out_shape=(
            jax.ShapeDtypeStruct(queries.shape, jnp.bfloat16),
            jax.ShapeDtypeStruct(block.shape, jnp.float32),
        )
        + (block,) * (exp_count - 1),
        in_specs=whole_specs(6 + len(operands))
        + [anywhere] * len(swapped),
        out_specs=tuple(whole_specs(1 + exp_count)),
        scratch_shapes=[pltpu.VMEM((fresh_block, model_width), jnp.float32)],
        compiler_params=LIMIT,
        cost_estimate=pl.CostEstimate(
            flops=page_flops + 2 * fresh_block * width * model_width,
            bytes_accessed=6 << 20,
            transcendentals=0,
        ),
    )(queries, page_lengths, *state, *operands, out_weight, *swapped)
    return outs[0], outs[1], outs[2:]


def finish_kernel(count, *refs):
    parts, (residual, gain, ids, scores, hidden_out, sent_out) = refs[:count], refs[count:]
    total = residual[...].astype(jnp.float32)
    for part in parts:
        total = total + part[...].astype(jnp.float32)
    hidden = total.astype(jnp.bfloat16)
    hidden_out[...] = hidden
    width = hidden.shape[1]
    sent_out[:, :width] = normalize(hidden, gain[...])
    chosen = jnp.transpose(scores[...])
    ids = jnp.transpose(ids[...])
    combine = (chosen / jnp.sum(chosen, axis=1, keepdims=True)).astype(jnp.bfloat16)
    combine = combine.astype(jnp.float32)
    tokens, choices = chosen.shape
    expert = lax.broadcasted_iota(jnp.int32, (tokens, sent_out.shape[1] - width), 1)
    dense = jnp.zeros(expert.shape, jnp.float32)
    for k in range(choices):
        dense = dense + jnp.where(ids[:, k : k + 1] == expert, combine[:, k : k + 1], 0.0)
    sent_out[:, width:] = dense.astype(jnp.bfloat16)


def finish(parts, residual, norm_gain, ids, scores, expert_count):
    tokens, width = residual.shape
    lanes = -(-expert_count // 128) * 128
    return pl.pallas_call(
        functools.partial(finish_kernel, len(parts)),
        out_shape=(
            jax.ShapeDtypeStruct((tokens, width), jnp.bfloat16),
            jax.ShapeDtypeStruct((tokens, width + lanes), jnp.bfloat16),
        ),
        in_specs=whole_specs(len(parts) + 4),
        out_specs=tuple(whole_specs(2)),
        compiler_params=LIMIT,
        cost_estimate=pl.CostEstimate(
            flops=8 * residual.size, bytes_accessed=1 << 19, transcendentals=0
        ),
    )(*parts, residual, norm_gain[None], ids, scores)


def down_kernel(offsets, rows, *refs):
    count = len(offsets)
    inners, downs, outs = refs[:count], refs[count : 2 * count], refs[2 * count :]
    dense = rows[:, outs[0].shape[1] :].astype(jnp.float32)
    lane = lax.broadcasted_iota(jnp.int32, dense.shape, 1)
    base = lax.axis_index("ctx") * lax.axis_size("exp")
    total = 0.0
    for offset, inner, down in zip(offsets, inners, downs):
        gate = inner[0]
        activated = (gate / (1.0 + jnp.exp(-gate)) * inner[1]).astype(jnp.bfloat16)
        piece = jnp.dot(activated, down[0], preferred_element_type=jnp.float32)
        expert = base + (lax.axis_index("exp") ^ offset)
        scale = jnp.sum(jnp.where(lane == expert, dense, 0.0), axis=1, keepdims=True)
        total = total + piece.astype(jnp.bfloat16).astype(jnp.float32) * scale
    start = 0
    for out in outs:
        out[...] = total[start : start + out.shape[0]].astype(out.dtype)
        start += out.shape[0]


def expert_apply(groups, kinds, weights):
    count = len(weights)
    rows = jnp.concatenate(groups, axis=0)
    _, hidden, width = weights[0][2].shape
    inners = [
        jnp.einsum("nd,dgh->gnh", rows[:, :width], gate_up[0], preferred_element_type=jnp.float32)
        for _, gate_up, _ in weights
    ]

    return pl.pallas_call(
        functools.partial(down_kernel, [offset for offset, _, _ in weights]),
        out_shape=[
            jax.ShapeDtypeStruct((group.shape[0], width), kind)
            for group, kind in zip(groups, kinds)
        ],
        in_specs=whole_specs(1 + 2 * count),
        out_specs=whole_specs(len(groups)),
        compiler_params=LIMIT,
        cost_estimate=pl.CostEstimate(
            flops=2 * count * rows.shape[0] * width * hidden,
            bytes_accessed=2 << 20,
            transcendentals=0,
        ),
    )(rows, *inners, *[down for _, _, down in weights])


def near_weights(gate_up, down):
    held = [(0, gate_up, down)]
    for stride in strides(lax.axis_size("exp"))[1:]:
        held = held + [
            (offset ^ stride, swap(first, "exp", stride), swap(second, "exp", stride))
            for offset, first, second in held
        ]
    return held


def chunks_of(count):
    chunks = [range((count + 1) // 2, count), range((count + 1) // 2)]
    return [list(chunk) for chunk in chunks if len(chunk)]


def mixture_of(rows, weights):
    tokens = rows.shape[0]
    far = strides(lax.axis_size("exp"))[:1]
    chunks = chunks_of(lax.axis_size("ctx"))

    joined = [
        jnp.concatenate(
            [rows if offset == 0 else swap(rows, "ctx", offset) for offset in chunk], axis=0
        )
        for chunk in chunks
    ]
    crossed = []
    for piece in joined if far else []:
        crossed.append(swap(piece, "exp", far[0]))
    *homes, first = expert_apply(
        joined + (crossed or joined)[:1], [jnp.float32] * len(joined) + [jnp.bfloat16], weights
    )
    total, arrived = None, []
    for number, (chunk, value) in enumerate(zip(chunks, homes)):
        if far:
            other = first
            if number:
                (other,) = expert_apply(crossed[number : number + 1], [jnp.bfloat16], weights)
            value = value + swap(other, "exp", far[0]).astype(jnp.float32)
        for position, offset in enumerate(chunk):
            block = value[position * tokens : (position + 1) * tokens]
            if offset == 0:
                total = block
            else:
                arrived.append(swap(block.astype(jnp.bfloat16), "ctx", offset))
    for block in arrived:
        total = total + block.astype(jnp.float32)
    return total


def per_device(
    queries,
    pages,
    cached_lengths,
    residual_in,
    out_weight,
    norm_gain,
    expert_ids,
    route_scores,
    expert_input,
    expert_output,
):
    requests = queries.shape[0]
    core_place = lax.axis_index("rep")
    rep_count = lax.axis_size("rep")
    exp_count = lax.axis_size("exp")
    expert_count = lax.axis_size("ctx") * exp_count
    token_block, model_width = residual_in.shape[1:]
    token_count = requests * token_block

    weights = near_weights(expert_input, expert_output)
    swapped = [part for _, *pair in weights[1:] for part in pair]
    contexts, owns, sents = [], [], []
    for r in range(requests):
        context, own, sent = attention(
            queries[r],
            pages[r],
            cached_lengths[r],
            out_weight,
            token_block,
            swapped if r == 0 else (),
        )
        contexts.append(context)
        owns.append(own)
        sents.append(sent)
    context = jnp.stack(contexts)

    parts = [jnp.concatenate(owns, axis=0)]
    for step in range(1, exp_count):
        blocks = jnp.concatenate([sent[step - 1] for sent in sents], axis=0)
        parts.append(swap(blocks, "exp", step))
    residual, ids, scores = residual_in, expert_ids, route_scores
    if rep_count > 1:
        share_size = token_block // rep_count
        share = sum(part.astype(jnp.float32) for part in parts).astype(jnp.bfloat16)
        share = share.reshape(requests, token_block, model_width)
        share = lax.psum_scatter(share, "rep", scatter_dimension=1, tiled=True)
        parts = [share.reshape(-1, model_width)]
        residual, ids, scores = (
            lax.dynamic_slice_in_dim(whole, core_place * share_size, share_size, 1)
            for whole in (residual, ids, scores)
        )
    own_hidden, normed = finish(
        parts,
        residual.reshape(-1, model_width),
        norm_gain,
        ids.reshape(-1, ids.shape[2]).T,
        scores.reshape(-1, ids.shape[2]).T,
        expert_count,
    )
    own_hidden = own_hidden.reshape(requests, -1, model_width)
    if rep_count > 1:
        normed = normed.reshape(requests, share_size, -1)
        normed = lax.all_gather(normed, "rep", axis=1, tiled=True)
        normed = normed.reshape(token_count, -1)

    mixture = mixture_of(normed, weights)
    mixture = mixture.reshape(requests, token_block, model_width)
    if rep_count > 1:
        mixture = lax.psum_scatter(
            mixture.astype(jnp.bfloat16), "rep", scatter_dimension=1, tiled=True
        ).astype(jnp.float32)
    layer_out = (own_hidden.astype(jnp.float32) + mixture).astype(jnp.bfloat16)
    return (context, layer_out)


def solution(mesh):
    in_specs = (
        P("groups", "ctx", ("exp", "rep")),
        P("groups", "ctx", None, "exp"),
        P("groups", None),
        P("groups", ("ctx", "exp"), None),
        P(("exp", "rep"), None),
        P(),
        P("groups", ("ctx", "exp"), None),
        P("groups", ("ctx", "exp"), None),
        P(("ctx", "exp"), None, None, "rep"),
        P(("ctx", "exp"), "rep", None),
    )
    out_specs = (P("groups", "ctx", ("exp", "rep")), P("groups", ("ctx", "exp", "rep"), None))
    return jax.shard_map(
        per_device, mesh=mesh, in_specs=in_specs, out_specs=out_specs, check_vma=False
    )
```

```python
import functools

import jax
import jax.numpy as jnp
from jax import lax
from jax.experimental import pallas as pl
from jax.experimental.pallas import tpu as pltpu
from jax.sharding import PartitionSpec as P

HEAD = 128

floor_value = -1e30
norm_epsilon = 1e-06


def normalize(hidden, norm_gain):
    widened = hidden.astype(jnp.float32)
    mean_square = jnp.mean(widened * widened, axis=-1, keepdims=True)
    return (widened * lax.rsqrt(mean_square + norm_epsilon) * norm_gain).astype(jnp.bfloat16)


def strides(count):
    assert count & (count - 1) == 0
    return [1 << bit for bit in reversed(range(count.bit_length() - 1))]


def swap(value, axis, stride):
    return lax.ppermute(value, axis, [(i, i ^ stride) for i in range(lax.axis_size(axis))])


def shift(value, axis, step):
    count = lax.axis_size(axis)
    return lax.ppermute(value, axis, [(i, (i + step) % count) for i in range(count)])


def whole_specs(count):
    return [pl.BlockSpec(memory_space=pltpu.VMEM)] * count


SMEM_SPEC = pl.BlockSpec(memory_space=pltpu.SMEM)
LIMIT = pltpu.CompilerParams(vmem_limit_bytes=12 * 1024 * 1024)


def stack_heads(queries):
    heads = queries.shape[1] // HEAD
    return jnp.concatenate(
        [queries[:, h * HEAD : (h + 1) * HEAD] for h in range(heads)], axis=0
    )


def page_partial(stacked, keys, values, page, length, place, fresh_block):
    rows, page_size = stacked.shape[0], keys.shape[0]
    slab_size = page_size - fresh_block
    scores = lax.dot_general(
        keys, stacked, (((1,), (1,)), ((), ())), preferred_element_type=jnp.float32
    )
    lanes = HEAD if HEAD % fresh_block == 0 and rows % HEAD == 0 else rows
    offset = lax.broadcasted_iota(jnp.int32, (slab_size, lanes), 0)
    fresh = page * fresh_block + lax.broadcasted_iota(jnp.int32, (fresh_block, lanes), 0)
    lane = lax.broadcasted_iota(jnp.int32, (fresh_block, lanes), 1)
    position = place * fresh_block + lax.rem(lane, fresh_block)
    bias = jnp.concatenate(
        [
            jnp.where(offset < length, 0.0, floor_value),
            jnp.where(fresh <= position, 0.0, floor_value),
        ],
        axis=0,
    )
    masked = scores + jnp.concatenate([bias] * (rows // lanes), axis=1)
    peak = jnp.max(masked, axis=0, keepdims=True)
    weights = jnp.exp((masked - peak) * (HEAD**-0.5))
    total = jnp.sum(weights, axis=0, keepdims=True)
    summed = lax.dot_general(
        values,
        weights.astype(jnp.bfloat16),
        (((0,), (0,)), ((), ())),
        preferred_element_type=jnp.float32,
    )
    return peak, total, summed


def merge(first, second):
    peak = jnp.maximum(first[0], second[0])
    scale_first = jnp.exp((first[0] - peak) * (HEAD**-0.5))
    scale_second = jnp.exp((second[0] - peak) * (HEAD**-0.5))
    return (
        peak,
        first[1] * scale_first + second[1] * scale_second,
        first[2] * scale_first + second[2] * scale_second,
    )


def page_at(offset):
    count = lax.axis_size("ctx")
    return lax.rem(lax.axis_index("ctx") + offset + count, count)


def first_kernel(fresh_block, count, lengths, queries, keys, values, *refs):
    peak_out, total_out, summed_out, lengths_out = refs[-4:]
    for offset in range(count):
        lengths_out[offset : offset + 1, :] = jnp.full(
            (1, lengths_out.shape[1]), lengths[page_at(offset)], jnp.int32
        )
    place = lax.axis_index("ctx")
    peak_out[...], total_out[...], summed_out[...] = page_partial(
        stack_heads(queries[...]),
        keys[...],
        values[...],
        place,
        lengths[place],
        place,
        fresh_block,
    )


def middle_kernel(offsets, fresh_block, queries, lengths, *refs):
    count = len(offsets)
    pages, (peak, total, summed) = refs[: 2 * count], refs[2 * count : 2 * count + 3]
    outs = refs[2 * count + 3 :]
    stacked = stack_heads(queries[...])
    state = (peak[...], total[...], summed[...])
    for number, offset in enumerate(offsets):
        part = page_partial(
            stacked,
            pages[2 * number][...],
            pages[2 * number + 1][...],
            page_at(offset),
            lengths[offset : offset + 1, :],
            lax.axis_index("ctx"),
            fresh_block,
        )
        state = merge(state, part)
    for out, value in zip(outs, state):
        out[...] = value


def late_kernel(
    offset,
    fresh_block,
    sent_count,
    queries,
    keys,
    values,
    lengths,
    peak,
    total,
    summed,
    weight,
    *rest,
):
    context_out, own_out = rest[-sent_count - 3 : -sent_count - 1]
    sent_outs, blocks = rest[-sent_count - 1 : -1], rest[-1]
    page = page_at(offset)
    part = page_partial(
        stack_heads(queries[...]),
        keys[...],
        values[...],
        page,
        lengths[offset : offset + 1, :],
        lax.axis_index("ctx"),
        fresh_block,
    )
    state = merge((peak[...], total[...], summed[...]), part)
    result = jnp.transpose(state[2] / state[1])
    context = jnp.concatenate(
        [
            result[h * fresh_block : (h + 1) * fresh_block]
            for h in range(result.shape[0] // fresh_block)
        ],
        axis=1,
    ).astype(jnp.bfloat16)
    context_out[...] = context
    blocks[...] = jnp.dot(context, weight[...], preferred_element_type=jnp.float32)
    place = lax.axis_index("exp")
    size = own_out.shape[0]
    pick = lambda index: blocks[pl.ds(pl.multiple_of(index * size, size), size), :]
    own_out[...] = pick(place)
    for step, out in enumerate(sent_outs, 1):
        out[...] = pick(place ^ step).astype(jnp.bfloat16)


def attention(queries, pages, lengths, out_weight, token_block):
    fresh_block, width = queries.shape
    rows = width // HEAD * fresh_block
    count = lax.axis_size("ctx")
    exp_count = lax.axis_size("exp")
    model_width = out_weight.shape[1]
    own_keys, own_values = pages[:, 0], pages[:, 1]
    held = []
    left_keys, left_values = own_keys, own_values
    right_keys, right_values = own_keys, own_values
    for step in range(1, (count - 1) // 2 + 1):
        left_keys = shift(left_keys, "ctx", 1)
        right_values = shift(right_values, "ctx", -1)
        left_values = shift(left_values, "ctx", 1)
        right_keys = shift(right_keys, "ctx", -1)
        held.append((count - step, left_keys, left_values))
        held.append((step, right_keys, right_values))
    if count % 2 == 0:
        last = (count // 2, shift(left_keys, "ctx", 1), shift(right_values, "ctx", -1))
    else:
        last = held.pop()
    page_flops = 4 * rows * pages.shape[0] * HEAD
    line = jax.ShapeDtypeStruct((1, rows), jnp.float32)
    partial_shape = (line, line, jax.ShapeDtypeStruct((HEAD, rows), jnp.float32))
    *state, page_lengths = pl.pallas_call(
        functools.partial(first_kernel, fresh_block, count),
        out_shape=partial_shape + (jax.ShapeDtypeStruct((count, HEAD), jnp.int32),),
        in_specs=[SMEM_SPEC]
        + whole_specs(3)
        + [pl.BlockSpec(memory_space=pl.ANY)],
        out_specs=tuple(whole_specs(4)),
        compiler_params=LIMIT,
        cost_estimate=pl.CostEstimate(
            flops=16 * page_flops, bytes_accessed=8 << 20, transcendentals=0
        ),
    )(lengths, queries, own_keys, own_values, out_weight)
    for start in range(0, len(held), 2):
        group = held[start : start + 2]
        operands = [part for _, keys, values in group for part in (keys, values)]
        state = pl.pallas_call(
            functools.partial(middle_kernel, [offset for offset, _, _ in group], fresh_block),
            out_shape=partial_shape,
            in_specs=whole_specs(5 + len(operands)),
            out_specs=tuple(whole_specs(3)),
            compiler_params=LIMIT,
            cost_estimate=pl.CostEstimate(
                flops=len(group) * page_flops, bytes_accessed=2 << 20, transcendentals=0
            ),
        )(queries, page_lengths, *operands, *state)
    block = jax.ShapeDtypeStruct((token_block, model_width), jnp.bfloat16)
    outs = pl.pallas_call(
        functools.partial(late_kernel, last[0], fresh_block, exp_count - 1),
        out_shape=(
            jax.ShapeDtypeStruct(queries.shape, jnp.bfloat16),
            jax.ShapeDtypeStruct(block.shape, jnp.float32),
        )
        + (block,) * (exp_count - 1),
        in_specs=whole_specs(8),
        out_specs=tuple(whole_specs(1 + exp_count)),
        scratch_shapes=[pltpu.VMEM((fresh_block, model_width), jnp.float32)],
        compiler_params=LIMIT,
        cost_estimate=pl.CostEstimate(
            flops=page_flops + 2 * fresh_block * width * model_width,
            bytes_accessed=6 << 20,
            transcendentals=0,
        ),
    )(queries, last[1], last[2], page_lengths, *state, out_weight)
    return outs[0], outs[1], outs[2:], state[0]


def finish_kernel(count, *refs):
    parts, (residual, gain, ids, scores), (hidden_out, sent_out) = (
        refs[:count],
        refs[count : count + 4],
        refs[-2:],
    )
    total = residual[...].astype(jnp.float32)
    for part in parts:
        total = total + part[...].astype(jnp.float32)
    hidden = total.astype(jnp.bfloat16)
    hidden_out[...] = hidden
    width = hidden.shape[1]
    sent_out[:, :width] = normalize(hidden, gain[...])
    chosen = jnp.transpose(scores[...])
    ids = jnp.transpose(ids[...])
    combine = (chosen / jnp.sum(chosen, axis=1, keepdims=True)).astype(jnp.bfloat16)
    combine = combine.astype(jnp.float32)
    tokens, choices = chosen.shape
    expert = lax.broadcasted_iota(jnp.int32, (tokens, sent_out.shape[1] - width), 1)
    dense = jnp.zeros(expert.shape, jnp.float32)
    for k in range(choices):
        dense = dense + jnp.where(ids[:, k : k + 1] == expert, combine[:, k : k + 1], 0.0)
    sent_out[:, width:] = dense.astype(jnp.bfloat16)


def finish(parts, swapped, residual, norm_gain, ids, scores, expert_count):
    tokens, width = residual.shape
    lanes = -(-expert_count // 128) * 128
    return pl.pallas_call(
        functools.partial(finish_kernel, len(parts)),
        out_shape=(
            jax.ShapeDtypeStruct((tokens, width), jnp.bfloat16),
            jax.ShapeDtypeStruct((tokens, width + lanes), jnp.bfloat16),
        ),
        in_specs=whole_specs(len(parts) + 4)
        + [pl.BlockSpec(memory_space=pl.ANY)] * len(swapped),
        out_specs=tuple(whole_specs(2)),
        compiler_params=LIMIT,
        cost_estimate=pl.CostEstimate(
            flops=8 * residual.size, bytes_accessed=1 << 19, transcendentals=0
        ),
    )(*parts, residual, norm_gain[None], ids, scores, *swapped)


def down_kernel(offsets, rows, *refs):
    count = len(offsets)
    inners, downs, outs = refs[:count], refs[count : 2 * count], refs[2 * count :]
    dense = rows[:, outs[0].shape[1] :].astype(jnp.float32)
    lane = lax.broadcasted_iota(jnp.int32, dense.shape, 1)
    base = lax.axis_index("ctx") * lax.axis_size("exp")
    total = 0.0
    for offset, inner, down in zip(offsets, inners, downs):
        gate = inner[0]
        activated = (gate / (1.0 + jnp.exp(-gate)) * inner[1]).astype(jnp.bfloat16)
        piece = jnp.dot(activated, down[0], preferred_element_type=jnp.float32)
        expert = base + (lax.axis_index("exp") ^ offset)
        scale = jnp.sum(jnp.where(lane == expert, dense, 0.0), axis=1, keepdims=True)
        total = total + piece.astype(jnp.bfloat16).astype(jnp.float32) * scale
    start = 0
    for out in outs:
        out[...] = total[start : start + out.shape[0]].astype(out.dtype)
        start += out.shape[0]


def expert_apply(groups, kinds, weights):
    count = len(weights)
    rows = jnp.concatenate(groups, axis=0)
    _, hidden, width = weights[0][2].shape
    inners = [
        jnp.einsum("nd,dgh->gnh", rows[:, :width], gate_up[0], preferred_element_type=jnp.float32)
        for _, gate_up, _ in weights
    ]

    return pl.pallas_call(
        functools.partial(down_kernel, [offset for offset, _, _ in weights]),
        out_shape=[
            jax.ShapeDtypeStruct((group.shape[0], width), kind)
            for group, kind in zip(groups, kinds)
        ],
        in_specs=whole_specs(1 + 2 * count),
        out_specs=whole_specs(len(groups)),
        compiler_params=LIMIT,
        cost_estimate=pl.CostEstimate(
            flops=2 * count * rows.shape[0] * width * hidden,
            bytes_accessed=2 << 20,
            transcendentals=0,
        ),
    )(rows, *inners, *[down for _, _, down in weights])


def near_parts(part):
    held = [(0, part)]
    for stride in strides(lax.axis_size("exp"))[1:]:
        held = held + [(offset ^ stride, swap(first, "exp", stride)) for offset, first in held]
    return held


def chunks_of(count):
    chunks = [range((count + 1) // 2, count), range((count + 1) // 2)]
    return [list(chunk) for chunk in chunks if len(chunk)]


def mixture_of(rows, weights):
    tokens = rows.shape[0]
    far = strides(lax.axis_size("exp"))[:1]
    chunks = chunks_of(lax.axis_size("ctx"))

    joined = [
        jnp.concatenate(
            [rows if offset == 0 else swap(rows, "ctx", offset) for offset in chunk], axis=0
        )
        for chunk in chunks
    ]
    crossed = []
    for piece in joined if far else []:
        crossed.append(swap(piece, "exp", far[0]))
    *homes, first = expert_apply(
        joined + (crossed or joined)[:1], [jnp.float32] * len(joined) + [jnp.bfloat16], weights
    )
    total, arrived = None, []
    for number, (chunk, value) in enumerate(zip(chunks, homes)):
        if far:
            other = first
            if number:
                (other,) = expert_apply(crossed[number : number + 1], [jnp.bfloat16], weights)
            value = value + swap(other, "exp", far[0]).astype(jnp.float32)
        for position, offset in enumerate(chunk):
            block = value[position * tokens : (position + 1) * tokens]
            if offset == 0:
                total = block
            else:
                arrived.append(swap(block.astype(jnp.bfloat16), "ctx", offset))
    for block in arrived:
        total = total + block.astype(jnp.float32)
    return total


def per_device(
    queries,
    pages,
    cached_lengths,
    residual_in,
    out_weight,
    norm_gain,
    expert_ids,
    route_scores,
    expert_input,
    expert_output,
):
    requests = queries.shape[0]
    core_place = lax.axis_index("rep")
    rep_count = lax.axis_size("rep")
    exp_count = lax.axis_size("exp")
    expert_count = lax.axis_size("ctx") * exp_count
    token_block, model_width = residual_in.shape[1:]
    token_count = requests * token_block

    gate_ups = near_parts(expert_input)
    contexts, owns, sents = [], [], []
    for r in range(requests):
        context, own, sent, arrived = attention(
            queries[r],
            pages[r],
            cached_lengths[r],
            out_weight,
            token_block,
        )
        contexts.append(context)
        owns.append(own)
        sents.append(sent)
    context = jnp.stack(contexts)
    downs = near_parts(lax.optimization_barrier((expert_output, owns[-1]))[0])
    weights = [(offset, first, down) for (offset, first), (_, down) in zip(gate_ups, downs)]
    swapped = [part for _, *pair in weights[1:] for part in pair]

    parts = [jnp.concatenate(owns, axis=0)]
    for step in range(1, exp_count):
        blocks = jnp.concatenate([sent[step - 1] for sent in sents], axis=0)
        parts.append(swap(blocks, "exp", step))
    residual, ids, scores = residual_in, expert_ids, route_scores
    if rep_count > 1:
        share_size = token_block // rep_count
        share = sum(part.astype(jnp.float32) for part in parts).astype(jnp.bfloat16)
        share = share.reshape(requests, token_block, model_width)
        share = lax.psum_scatter(share, "rep", scatter_dimension=1, tiled=True)
        parts = [share.reshape(-1, model_width)]
        residual, ids, scores = (
            lax.dynamic_slice_in_dim(whole, core_place * share_size, share_size, 1)
            for whole in (residual, ids, scores)
        )
    own_hidden, normed = finish(
        parts,
        swapped,
        residual.reshape(-1, model_width),
        norm_gain,
        ids.reshape(-1, ids.shape[2]).T,
        scores.reshape(-1, ids.shape[2]).T,
        expert_count,
    )
    own_hidden = own_hidden.reshape(requests, -1, model_width)
    if rep_count > 1:
        normed = normed.reshape(requests, share_size, -1)
        normed = lax.all_gather(normed, "rep", axis=1, tiled=True)
        normed = normed.reshape(token_count, -1)

    mixture = mixture_of(normed, weights)
    mixture = mixture.reshape(requests, token_block, model_width)
    if rep_count > 1:
        mixture = lax.psum_scatter(
            mixture.astype(jnp.bfloat16), "rep", scatter_dimension=1, tiled=True
        ).astype(jnp.float32)
    layer_out = (own_hidden.astype(jnp.float32) + mixture).astype(jnp.bfloat16)
    return (context, layer_out)


def solution(mesh):
    in_specs = (
        P("groups", "ctx", ("exp", "rep")),
        P("groups", "ctx", None, "exp"),
        P("groups", None),
        P("groups", ("ctx", "exp"), None),
        P(("exp", "rep"), None),
        P(),
        P("groups", ("ctx", "exp"), None),
        P("groups", ("ctx", "exp"), None),
        P(("ctx", "exp"), None, None, "rep"),
        P(("ctx", "exp"), "rep", None),
    )
    out_specs = (P("groups", "ctx", ("exp", "rep")), P("groups", ("ctx", "exp", "rep"), None))
    return jax.shard_map(
        per_device, mesh=mesh, in_specs=in_specs, out_specs=out_specs, check_vma=False
    )
```

```python
import functools

import jax
import jax.numpy as jnp
from jax import lax
from jax.experimental import pallas as pl
from jax.experimental.pallas import tpu as pltpu
from jax.sharding import PartitionSpec as P

HEAD = 128

floor_value = -1e30
norm_epsilon = 1e-06


def normalize(hidden, norm_gain):
    widened = hidden.astype(jnp.float32)
    mean_square = jnp.mean(widened * widened, axis=-1, keepdims=True)
    return (widened * lax.rsqrt(mean_square + norm_epsilon) * norm_gain).astype(jnp.bfloat16)


def strides(count):
    assert count & (count - 1) == 0
    return [1 << bit for bit in reversed(range(count.bit_length() - 1))]


def sum_order(held):
    offsets = [0]
    for stride in held:
        offsets = offsets + [offset ^ stride for offset in offsets]
    return offsets


def swap(value, axis, stride):
    return lax.ppermute(value, axis, [(i, i ^ stride) for i in range(lax.axis_size(axis))])


def shift(value, axis, step):
    count = lax.axis_size(axis)
    return lax.ppermute(value, axis, [(i, (i + step) % count) for i in range(count)])


def whole_specs(count):
    return [pl.BlockSpec(memory_space=pltpu.VMEM)] * count


SMEM_SPEC = pl.BlockSpec(memory_space=pltpu.SMEM)
LIMIT = pltpu.CompilerParams(vmem_limit_bytes=12 * 1024 * 1024)


def stack_heads(queries):
    heads = queries.shape[1] // HEAD
    return jnp.concatenate(
        [queries[:, h * HEAD : (h + 1) * HEAD] for h in range(heads)], axis=0
    )


def page_partial(stacked, keys, values, page, length, place, fresh_block):
    rows, page_size = stacked.shape[0], keys.shape[0]
    slab_size = page_size - fresh_block
    scores = lax.dot_general(
        keys, stacked, (((1,), (1,)), ((), ())), preferred_element_type=jnp.float32
    )
    lanes = HEAD if HEAD % fresh_block == 0 and rows % HEAD == 0 else rows
    offset = lax.broadcasted_iota(jnp.int32, (slab_size, lanes), 0)
    fresh = page * fresh_block + lax.broadcasted_iota(jnp.int32, (fresh_block, lanes), 0)
    lane = lax.broadcasted_iota(jnp.int32, (fresh_block, lanes), 1)
    position = place * fresh_block + lax.rem(lane, fresh_block)
    bias = jnp.concatenate(
        [
            jnp.where(offset < length, 0.0, floor_value),
            jnp.where(fresh <= position, 0.0, floor_value),
        ],
        axis=0,
    )
    masked = scores + jnp.concatenate([bias] * (rows // lanes), axis=1)
    peak = jnp.max(masked, axis=0, keepdims=True)
    weights = jnp.exp((masked - peak) * (HEAD**-0.5))
    total = jnp.sum(weights, axis=0, keepdims=True)
    summed = lax.dot_general(
        values,
        weights.astype(jnp.bfloat16),
        (((0,), (0,)), ((), ())),
        preferred_element_type=jnp.float32,
    )
    return peak, total, summed


def merge(first, second):
    peak = jnp.maximum(first[0], second[0])
    scale_first = jnp.exp((first[0] - peak) * (HEAD**-0.5))
    scale_second = jnp.exp((second[0] - peak) * (HEAD**-0.5))
    return (
        peak,
        first[1] * scale_first + second[1] * scale_second,
        first[2] * scale_first + second[2] * scale_second,
    )


def page_at(offset):
    count = lax.axis_size("ctx")
    return lax.rem(lax.axis_index("ctx") + offset + count, count)


def first_kernel(fresh_block, count, lengths, queries, keys, values, *refs):
    peak_out, total_out, summed_out, lengths_out = refs[-4:]
    for offset in range(count):
        lengths_out[offset : offset + 1, :] = jnp.full(
            (1, lengths_out.shape[1]), lengths[page_at(offset)], jnp.int32
        )
    place = lax.axis_index("ctx")
    peak_out[...], total_out[...], summed_out[...] = page_partial(
        stack_heads(queries[...]),
        keys[...],
        values[...],
        place,
        lengths[place],
        place,
        fresh_block,
    )


def middle_kernel(offsets, fresh_block, queries, lengths, *refs):
    count = len(offsets)
    pages, (peak, total, summed) = refs[: 2 * count], refs[2 * count : 2 * count + 3]
    outs = refs[2 * count + 3 :]
    stacked = stack_heads(queries[...])
    state = (peak[...], total[...], summed[...])
    for number, offset in enumerate(offsets):
        part = page_partial(
            stacked,
            pages[2 * number][...],
            pages[2 * number + 1][...],
            page_at(offset),
            lengths[offset : offset + 1, :],
            lax.axis_index("ctx"),
            fresh_block,
        )
        state = merge(state, part)
    for out, value in zip(outs, state):
        out[...] = value


def late_kernel(
    offset,
    fresh_block,
    queries,
    keys,
    values,
    lengths,
    peak,
    total,
    summed,
    weight,
    context_out,
    keep_out,
    *rest,
):
    send_out, blocks = rest[:-1], rest[-1]
    page = page_at(offset)
    part = page_partial(
        stack_heads(queries[...]),
        keys[...],
        values[...],
        page,
        lengths[offset : offset + 1, :],
        lax.axis_index("ctx"),
        fresh_block,
    )
    state = merge((peak[...], total[...], summed[...]), part)
    result = jnp.transpose(state[2] / state[1])
    context = jnp.concatenate(
        [
            result[h * fresh_block : (h + 1) * fresh_block]
            for h in range(result.shape[0] // fresh_block)
        ],
        axis=1,
    ).astype(jnp.bfloat16)
    context_out[...] = context
    blocks[...] = jnp.dot(context, weight[...], preferred_element_type=jnp.float32)
    place = lax.axis_index("exp")
    offsets = sum_order(strides(lax.axis_size("exp")))
    size = blocks.shape[0] // len(offsets)
    half = keep_out.shape[0] // size
    for number, offset in enumerate(offsets):
        index = place ^ offset
        value = blocks[pl.ds(pl.multiple_of(index * size, size), size), :]
        if number < half:
            keep_out[number * size : (number + 1) * size, :] = value
        else:
            low = (number - half) * size
            send_out[0][low : low + size, :] = value.astype(jnp.bfloat16)


def attention(queries, pages, lengths, out_weight, token_block):
    fresh_block, width = queries.shape
    rows = width // HEAD * fresh_block
    count = lax.axis_size("ctx")
    exp_count = lax.axis_size("exp")
    model_width = out_weight.shape[1]
    own_keys, own_values = pages[:, 0], pages[:, 1]
    held = []
    left_keys, left_values = own_keys, own_values
    right_keys, right_values = own_keys, own_values
    for step in range(1, (count - 1) // 2 + 1):
        left_keys = shift(left_keys, "ctx", 1)
        right_values = shift(right_values, "ctx", -1)
        left_values = shift(left_values, "ctx", 1)
        right_keys = shift(right_keys, "ctx", -1)
        held.append((count - step, left_keys, left_values))
        held.append((step, right_keys, right_values))
    if count % 2 == 0:
        last = (count // 2, shift(left_keys, "ctx", 1), shift(right_values, "ctx", -1))
    else:
        last = held.pop()
    page_flops = 4 * rows * pages.shape[0] * HEAD
    line = jax.ShapeDtypeStruct((1, rows), jnp.float32)
    partial_shape = (line, line, jax.ShapeDtypeStruct((HEAD, rows), jnp.float32))
    *state, page_lengths = pl.pallas_call(
        functools.partial(first_kernel, fresh_block, count),
        out_shape=partial_shape + (jax.ShapeDtypeStruct((count, HEAD), jnp.int32),),
        in_specs=[SMEM_SPEC]
        + whole_specs(3)
        + [pl.BlockSpec(memory_space=pl.ANY)],
        out_specs=tuple(whole_specs(4)),
        compiler_params=LIMIT,
        cost_estimate=pl.CostEstimate(
            flops=16 * page_flops, bytes_accessed=8 << 20, transcendentals=0
        ),
    )(lengths, queries, own_keys, own_values, out_weight)
    for start in range(0, len(held), 2):
        group = held[start : start + 2]
        operands = [part for _, keys, values in group for part in (keys, values)]
        state = pl.pallas_call(
            functools.partial(middle_kernel, [offset for offset, _, _ in group], fresh_block),
            out_shape=partial_shape,
            in_specs=whole_specs(5 + len(operands)),
            out_specs=tuple(whole_specs(3)),
            compiler_params=LIMIT,
            cost_estimate=pl.CostEstimate(
                flops=len(group) * page_flops, bytes_accessed=2 << 20, transcendentals=0
            ),
        )(queries, page_lengths, *operands, *state)
    half = (max(1, exp_count // 2) * token_block, model_width)
    shapes = [
        jax.ShapeDtypeStruct(queries.shape, jnp.bfloat16),
        jax.ShapeDtypeStruct(half, jnp.float32),
    ]
    if exp_count > 1:
        shapes.append(jax.ShapeDtypeStruct(half, jnp.bfloat16))
    outs = pl.pallas_call(
        functools.partial(late_kernel, last[0], fresh_block),
        out_shape=shapes,
        in_specs=whole_specs(8),
        out_specs=whole_specs(len(shapes)),
        scratch_shapes=[pltpu.VMEM((fresh_block, model_width), jnp.float32)],
        compiler_params=LIMIT,
        cost_estimate=pl.CostEstimate(
            flops=page_flops + 2 * fresh_block * width * model_width,
            bytes_accessed=6 << 20,
            transcendentals=0,
        ),
    )(queries, last[1], last[2], page_lengths, *state, out_weight)
    return outs[0], outs[1], outs[2:]


def finish_kernel(count, *refs):
    parts, (residual, gain, ids, scores), (hidden_out, sent_out) = (
        refs[:count],
        refs[count : count + 4],
        refs[-2:],
    )
    total = residual[...].astype(jnp.float32)
    for part in parts:
        total = total + part[...].astype(jnp.float32)
    hidden = total.astype(jnp.bfloat16)
    hidden_out[...] = hidden
    width = hidden.shape[1]
    sent_out[:, :width] = normalize(hidden, gain[...])
    chosen = jnp.transpose(scores[...])
    ids = jnp.transpose(ids[...])
    combine = (chosen / jnp.sum(chosen, axis=1, keepdims=True)).astype(jnp.bfloat16)
    combine = combine.astype(jnp.float32)
    tokens, choices = chosen.shape
    expert = lax.broadcasted_iota(jnp.int32, (tokens, sent_out.shape[1] - width), 1)
    dense = jnp.zeros(expert.shape, jnp.float32)
    for k in range(choices):
        dense = dense + jnp.where(ids[:, k : k + 1] == expert, combine[:, k : k + 1], 0.0)
    sent_out[:, width:] = dense.astype(jnp.bfloat16)


def finish(parts, swapped, residual, norm_gain, ids, scores, expert_count):
    tokens, width = residual.shape
    lanes = -(-expert_count // 128) * 128
    return pl.pallas_call(
        functools.partial(finish_kernel, len(parts)),
        out_shape=(
            jax.ShapeDtypeStruct((tokens, width), jnp.bfloat16),
            jax.ShapeDtypeStruct((tokens, width + lanes), jnp.bfloat16),
        ),
        in_specs=whole_specs(len(parts) + 4)
        + [pl.BlockSpec(memory_space=pl.ANY)] * len(swapped),
        out_specs=tuple(whole_specs(2)),
        compiler_params=LIMIT,
        cost_estimate=pl.CostEstimate(
            flops=8 * residual.size, bytes_accessed=1 << 19, transcendentals=0
        ),
    )(*parts, residual, norm_gain[None], ids, scores, *swapped)


def down_kernel(offsets, rows, *refs):
    count = len(offsets)
    inners, downs, outs = refs[:count], refs[count : 2 * count], refs[2 * count :]
    dense = rows[:, outs[0].shape[1] :].astype(jnp.float32)
    lane = lax.broadcasted_iota(jnp.int32, dense.shape, 1)
    base = lax.axis_index("ctx") * lax.axis_size("exp")
    total = 0.0
    for offset, inner, down in zip(offsets, inners, downs):
        gate = inner[0]
        activated = (gate / (1.0 + jnp.exp(-gate)) * inner[1]).astype(jnp.bfloat16)
        piece = jnp.dot(activated, down[0], preferred_element_type=jnp.float32)
        expert = base + (lax.axis_index("exp") ^ offset)
        scale = jnp.sum(jnp.where(lane == expert, dense, 0.0), axis=1, keepdims=True)
        total = total + piece.astype(jnp.bfloat16).astype(jnp.float32) * scale
    start = 0
    for out in outs:
        out[...] = total[start : start + out.shape[0]].astype(out.dtype)
        start += out.shape[0]


def expert_apply(groups, kinds, weights):
    count = len(weights)
    rows = jnp.concatenate(groups, axis=0)
    _, hidden, width = weights[0][2].shape
    inners = [
        jnp.einsum("nd,dgh->gnh", rows[:, :width], gate_up[0], preferred_element_type=jnp.float32)
        for _, gate_up, _ in weights
    ]

    return pl.pallas_call(
        functools.partial(down_kernel, [offset for offset, _, _ in weights]),
        out_shape=[
            jax.ShapeDtypeStruct((group.shape[0], width), kind)
            for group, kind in zip(groups, kinds)
        ],
        in_specs=whole_specs(1 + 2 * count),
        out_specs=whole_specs(len(groups)),
        compiler_params=LIMIT,
        cost_estimate=pl.CostEstimate(
            flops=2 * count * rows.shape[0] * width * hidden,
            bytes_accessed=2 << 20,
            transcendentals=0,
        ),
    )(rows, *inners, *[down for _, _, down in weights])


def near_parts(part):
    held = [(0, part)]
    for stride in strides(lax.axis_size("exp"))[1:]:
        held = held + [(offset ^ stride, swap(first, "exp", stride)) for offset, first in held]
    return held


def chunks_of(count):
    chunks = [range((count + 1) // 2, count), range((count + 1) // 2)]
    return [list(chunk) for chunk in chunks if len(chunk)]


def mixture_of(rows, weights):
    tokens = rows.shape[0]
    far = strides(lax.axis_size("exp"))[:1]
    chunks = chunks_of(lax.axis_size("ctx"))

    joined = [
        jnp.concatenate(
            [rows if offset == 0 else swap(rows, "ctx", offset) for offset in chunk], axis=0
        )
        for chunk in chunks
    ]
    crossed = []
    for piece in joined if far else []:
        crossed.append(swap(piece, "exp", far[0]))
    *homes, first = expert_apply(
        joined + (crossed or joined)[:1], [jnp.float32] * len(joined) + [jnp.bfloat16], weights
    )
    total, arrived = None, []
    for number, (chunk, value) in enumerate(zip(chunks, homes)):
        if far:
            other = first
            if number:
                (other,) = expert_apply(crossed[number : number + 1], [jnp.bfloat16], weights)
            value = value + swap(other, "exp", far[0]).astype(jnp.float32)
        for position, offset in enumerate(chunk):
            block = value[position * tokens : (position + 1) * tokens]
            if offset == 0:
                total = block
            else:
                arrived.append(swap(block.astype(jnp.bfloat16), "ctx", offset))
    for block in arrived:
        total = total + block.astype(jnp.float32)
    return total


def per_device(
    queries,
    pages,
    cached_lengths,
    residual_in,
    out_weight,
    norm_gain,
    expert_ids,
    route_scores,
    expert_input,
    expert_output,
):
    requests = queries.shape[0]
    core_place = lax.axis_index("rep")
    rep_count = lax.axis_size("rep")
    exp_count = lax.axis_size("exp")
    expert_count = lax.axis_size("ctx") * exp_count
    token_block, model_width = residual_in.shape[1:]
    token_count = requests * token_block

    gate_ups = near_parts(expert_input)
    contexts, keeps, sends = [], [], []
    for r in range(requests):
        context, keep, send = attention(
            queries[r],
            pages[r],
            cached_lengths[r],
            out_weight,
            token_block,
        )
        contexts.append(context)
        keeps.append(keep)
        sends.extend(send)
    context = jnp.stack(contexts)

    by_block = lambda values: [value.reshape(-1, token_block, model_width) for value in values]
    parts = [jnp.stack(by_block(keeps), axis=1)]
    send = jnp.stack(by_block(sends), axis=1) if sends else None
    for stride in reversed(strides(exp_count)):
        arrived = swap(send, "exp", stride)
        if parts[0].shape[0] > 1:
            total = parts[0] + arrived.astype(jnp.float32)
            half = total.shape[0] // 2
            parts, send = [total[:half]], total[half:].astype(jnp.bfloat16)
        else:
            parts = [parts[0], arrived]
    downs = near_parts(lax.optimization_barrier((expert_output, parts[0]))[0])
    weights = [(offset, first, down) for (offset, first), (_, down) in zip(gate_ups, downs)]
    parts = [part.reshape(-1, model_width) for part in parts]
    residual, ids, scores = residual_in, expert_ids, route_scores
    if rep_count > 1:
        share_size = token_block // rep_count
        share = sum(part.astype(jnp.float32) for part in parts).astype(jnp.bfloat16)
        share = share.reshape(requests, token_block, model_width)
        share = lax.psum_scatter(share, "rep", scatter_dimension=1, tiled=True)
        parts = [share.reshape(-1, model_width)]
        residual, ids, scores = (
            lax.dynamic_slice_in_dim(whole, core_place * share_size, share_size, 1)
            for whole in (residual, ids, scores)
        )
    own_hidden, normed = finish(
        parts,
        [first for _, first in gate_ups[1:]],
        residual.reshape(-1, model_width),
        norm_gain,
        ids.reshape(-1, ids.shape[2]).T,
        scores.reshape(-1, ids.shape[2]).T,
        expert_count,
    )
    own_hidden = own_hidden.reshape(requests, -1, model_width)
    if rep_count > 1:
        normed = normed.reshape(requests, share_size, -1)
        normed = lax.all_gather(normed, "rep", axis=1, tiled=True)
        normed = normed.reshape(token_count, -1)

    mixture = mixture_of(normed, weights)
    mixture = mixture.reshape(requests, token_block, model_width)
    if rep_count > 1:
        mixture = lax.psum_scatter(
            mixture.astype(jnp.bfloat16), "rep", scatter_dimension=1, tiled=True
        ).astype(jnp.float32)
    layer_out = (own_hidden.astype(jnp.float32) + mixture).astype(jnp.bfloat16)
    return (context, layer_out)


def solution(mesh):
    in_specs = (
        P("groups", "ctx", ("exp", "rep")),
        P("groups", "ctx", None, "exp"),
        P("groups", None),
        P("groups", ("ctx", "exp"), None),
        P(("exp", "rep"), None),
        P(),
        P("groups", ("ctx", "exp"), None),
        P("groups", ("ctx", "exp"), None),
        P(("ctx", "exp"), None, None, "rep"),
        P(("ctx", "exp"), "rep", None),
    )
    out_specs = (P("groups", "ctx", ("exp", "rep")), P("groups", ("ctx", "exp", "rep"), None))
    return jax.shard_map(
        per_device, mesh=mesh, in_specs=in_specs, out_specs=out_specs, check_vma=False
    )
```

```python
import functools

import jax
import jax.numpy as jnp
from jax import lax
from jax.experimental import pallas as pl
from jax.experimental.pallas import tpu as pltpu
from jax.sharding import PartitionSpec as P

HEAD = 128

floor_value = -1e30
norm_epsilon = 1e-06


def normalize(hidden, norm_gain):
    widened = hidden.astype(jnp.float32)
    mean_square = jnp.mean(widened * widened, axis=-1, keepdims=True)
    return (widened * lax.rsqrt(mean_square + norm_epsilon) * norm_gain).astype(jnp.bfloat16)


def strides(count):
    assert count & (count - 1) == 0
    return [1 << bit for bit in reversed(range(count.bit_length() - 1))]


def sum_order(held):
    offsets = [0]
    for stride in held:
        offsets = offsets + [offset ^ stride for offset in offsets]
    return offsets


def swap(value, axis, stride):
    return lax.ppermute(value, axis, [(i, i ^ stride) for i in range(lax.axis_size(axis))])


def shift(value, axis, step):
    count = lax.axis_size(axis)
    return lax.ppermute(value, axis, [(i, (i + step) % count) for i in range(count)])


def whole_specs(count):
    return [pl.BlockSpec(memory_space=pltpu.VMEM)] * count


SMEM_SPEC = pl.BlockSpec(memory_space=pltpu.SMEM)
LIMIT = pltpu.CompilerParams(vmem_limit_bytes=12 * 1024 * 1024)


def stack_heads(queries):
    heads = queries.shape[1] // HEAD
    return jnp.concatenate(
        [queries[:, h * HEAD : (h + 1) * HEAD] for h in range(heads)], axis=0
    )


def page_partial(stacked, keys, values, page, length, place, fresh_block):
    rows, page_size = stacked.shape[0], keys.shape[0]
    slab_size = page_size - fresh_block
    scores = lax.dot_general(
        keys, stacked, (((1,), (1,)), ((), ())), preferred_element_type=jnp.float32
    )
    lanes = HEAD if HEAD % fresh_block == 0 and rows % HEAD == 0 else rows
    offset = lax.broadcasted_iota(jnp.int32, (slab_size, lanes), 0)
    fresh = page * fresh_block + lax.broadcasted_iota(jnp.int32, (fresh_block, lanes), 0)
    lane = lax.broadcasted_iota(jnp.int32, (fresh_block, lanes), 1)
    position = place * fresh_block + lax.rem(lane, fresh_block)
    bias = jnp.concatenate(
        [
            jnp.where(offset < length, 0.0, floor_value),
            jnp.where(fresh <= position, 0.0, floor_value),
        ],
        axis=0,
    )
    masked = scores + jnp.concatenate([bias] * (rows // lanes), axis=1)
    peak = jnp.max(masked, axis=0, keepdims=True)
    weights = jnp.exp((masked - peak) * (HEAD**-0.5))
    total = jnp.sum(weights, axis=0, keepdims=True)
    summed = lax.dot_general(
        values,
        weights.astype(jnp.bfloat16),
        (((0,), (0,)), ((), ())),
        preferred_element_type=jnp.float32,
    )
    return peak, total, summed


def merge(first, second):
    peak = jnp.maximum(first[0], second[0])
    scale_first = jnp.exp((first[0] - peak) * (HEAD**-0.5))
    scale_second = jnp.exp((second[0] - peak) * (HEAD**-0.5))
    return (
        peak,
        first[1] * scale_first + second[1] * scale_second,
        first[2] * scale_first + second[2] * scale_second,
    )


def page_at(offset):
    count = lax.axis_size("ctx")
    return lax.rem(lax.axis_index("ctx") + offset + count, count)


def first_kernel(fresh_block, count, lengths, queries, keys, values, *refs):
    peak_out, total_out, summed_out, lengths_out = refs[-4:]
    for offset in range(count):
        lengths_out[offset : offset + 1, :] = jnp.full(
            (1, lengths_out.shape[1]), lengths[page_at(offset)], jnp.int32
        )
    place = lax.axis_index("ctx")
    peak_out[...], total_out[...], summed_out[...] = page_partial(
        stack_heads(queries[...]),
        keys[...],
        values[...],
        place,
        lengths[place],
        place,
        fresh_block,
    )


def middle_kernel(offsets, fresh_block, queries, lengths, *refs):
    count = len(offsets)
    pages, (peak, total, summed) = refs[: 2 * count], refs[2 * count : 2 * count + 3]
    outs = refs[2 * count + 3 :]
    stacked = stack_heads(queries[...])
    state = (peak[...], total[...], summed[...])
    for number, offset in enumerate(offsets):
        part = page_partial(
            stacked,
            pages[2 * number][...],
            pages[2 * number + 1][...],
            page_at(offset),
            lengths[offset : offset + 1, :],
            lax.axis_index("ctx"),
            fresh_block,
        )
        state = merge(state, part)
    for out, value in zip(outs, state):
        out[...] = value


def late_kernel(
    offset,
    fresh_block,
    queries,
    keys,
    values,
    lengths,
    peak,
    total,
    summed,
    weight,
    context_out,
    keep_out,
    *rest,
):
    send_out, blocks = rest[:-1], rest[-1]
    page = page_at(offset)
    part = page_partial(
        stack_heads(queries[...]),
        keys[...],
        values[...],
        page,
        lengths[offset : offset + 1, :],
        lax.axis_index("ctx"),
        fresh_block,
    )
    state = merge((peak[...], total[...], summed[...]), part)
    result = jnp.transpose(state[2] / state[1])
    context = jnp.concatenate(
        [
            result[h * fresh_block : (h + 1) * fresh_block]
            for h in range(result.shape[0] // fresh_block)
        ],
        axis=1,
    ).astype(jnp.bfloat16)
    context_out[...] = context
    blocks[...] = jnp.dot(context, weight[...], preferred_element_type=jnp.float32)
    place = lax.axis_index("exp")
    offsets = sum_order(strides(lax.axis_size("exp")))
    size = blocks.shape[0] // len(offsets)
    half = keep_out.shape[0] // size
    for number, offset in enumerate(offsets):
        index = place ^ offset
        value = blocks[pl.ds(pl.multiple_of(index * size, size), size), :]
        if number < half:
            keep_out[number * size : (number + 1) * size, :] = value
        else:
            low = (number - half) * size
            send_out[0][low : low + size, :] = value.astype(jnp.bfloat16)


def attention(queries, pages, lengths, out_weight, token_block):
    fresh_block, width = queries.shape
    rows = width // HEAD * fresh_block
    count = lax.axis_size("ctx")
    exp_count = lax.axis_size("exp")
    model_width = out_weight.shape[1]
    own_keys, own_values = pages[:, 0], pages[:, 1]
    held = []
    left_keys, left_values = own_keys, own_values
    right_keys, right_values = own_keys, own_values
    for step in range(1, (count - 1) // 2 + 1):
        left_keys = shift(left_keys, "ctx", 1)
        right_values = shift(right_values, "ctx", -1)
        left_values = shift(left_values, "ctx", 1)
        right_keys = shift(right_keys, "ctx", -1)
        held.append((count - step, left_keys, left_values))
        held.append((step, right_keys, right_values))
    if count % 2 == 0:
        last = (count // 2, shift(left_keys, "ctx", 1), shift(right_values, "ctx", -1))
    else:
        last = held.pop()
    page_flops = 4 * rows * pages.shape[0] * HEAD
    line = jax.ShapeDtypeStruct((1, rows), jnp.float32)
    partial_shape = (line, line, jax.ShapeDtypeStruct((HEAD, rows), jnp.float32))
    *state, page_lengths = pl.pallas_call(
        functools.partial(first_kernel, fresh_block, count),
        out_shape=partial_shape + (jax.ShapeDtypeStruct((count, HEAD), jnp.int32),),
        in_specs=[SMEM_SPEC]
        + whole_specs(3)
        + [pl.BlockSpec(memory_space=pl.ANY)],
        out_specs=tuple(whole_specs(4)),
        compiler_params=LIMIT,
        cost_estimate=pl.CostEstimate(
            flops=16 * page_flops, bytes_accessed=8 << 20, transcendentals=0
        ),
    )(lengths, queries, own_keys, own_values, out_weight)
    for start in range(0, len(held), 2):
        group = held[start : start + 2]
        operands = [part for _, keys, values in group for part in (keys, values)]
        state = pl.pallas_call(
            functools.partial(middle_kernel, [offset for offset, _, _ in group], fresh_block),
            out_shape=partial_shape,
            in_specs=whole_specs(5 + len(operands)),
            out_specs=tuple(whole_specs(3)),
            compiler_params=LIMIT,
            cost_estimate=pl.CostEstimate(
                flops=len(group) * page_flops, bytes_accessed=2 << 20, transcendentals=0
            ),
        )(queries, page_lengths, *operands, *state)
    half = (max(1, exp_count // 2) * token_block, model_width)
    shapes = [
        jax.ShapeDtypeStruct(queries.shape, jnp.bfloat16),
        jax.ShapeDtypeStruct(half, jnp.float32),
    ]
    if exp_count > 1:
        shapes.append(jax.ShapeDtypeStruct(half, jnp.bfloat16))
    outs = pl.pallas_call(
        functools.partial(late_kernel, last[0], fresh_block),
        out_shape=shapes,
        in_specs=whole_specs(8),
        out_specs=whole_specs(len(shapes)),
        scratch_shapes=[pltpu.VMEM((fresh_block, model_width), jnp.float32)],
        compiler_params=LIMIT,
        cost_estimate=pl.CostEstimate(
            flops=page_flops + 2 * fresh_block * width * model_width,
            bytes_accessed=6 << 20,
            transcendentals=0,
        ),
    )(queries, last[1], last[2], page_lengths, *state, out_weight)
    return outs[0], outs[1], outs[2:]


def finish_kernel(count, *refs):
    parts, (residual, gain, ids, scores), (hidden_out, sent_out) = (
        refs[:count],
        refs[count : count + 4],
        refs[-2:],
    )
    total = residual[...].astype(jnp.float32)
    for part in parts:
        total = total + part[...].astype(jnp.float32)
    hidden = total.astype(jnp.bfloat16)
    hidden_out[...] = hidden
    width = hidden.shape[1]
    sent_out[:, :width] = normalize(hidden, gain[...])
    chosen = jnp.transpose(scores[...])
    ids = jnp.transpose(ids[...])
    combine = (chosen / jnp.sum(chosen, axis=1, keepdims=True)).astype(jnp.bfloat16)
    combine = combine.astype(jnp.float32)
    tokens, choices = chosen.shape
    expert = lax.broadcasted_iota(jnp.int32, (tokens, sent_out.shape[1] - width), 1)
    dense = jnp.zeros(expert.shape, jnp.float32)
    for k in range(choices):
        dense = dense + jnp.where(ids[:, k : k + 1] == expert, combine[:, k : k + 1], 0.0)
    sent_out[:, width:] = dense.astype(jnp.bfloat16)


def finish(parts, swapped, residual, norm_gain, ids, scores, expert_count):
    tokens, width = residual.shape
    lanes = -(-expert_count // 128) * 128
    return pl.pallas_call(
        functools.partial(finish_kernel, len(parts)),
        out_shape=(
            jax.ShapeDtypeStruct((tokens, width), jnp.bfloat16),
            jax.ShapeDtypeStruct((tokens, width + lanes), jnp.bfloat16),
        ),
        in_specs=whole_specs(len(parts) + 4)
        + [pl.BlockSpec(memory_space=pl.ANY)] * len(swapped),
        out_specs=tuple(whole_specs(2)),
        compiler_params=LIMIT,
        cost_estimate=pl.CostEstimate(
            flops=8 * residual.size, bytes_accessed=1 << 19, transcendentals=0
        ),
    )(*parts, residual, norm_gain[None], ids, scores, *swapped)


def down_kernel(offsets, rows, *refs):
    count = len(offsets)
    inners, downs, outs = refs[:count], refs[count : 2 * count], refs[2 * count :]
    dense = rows[:, outs[0].shape[1] :].astype(jnp.float32)
    lane = lax.broadcasted_iota(jnp.int32, dense.shape, 1)
    base = lax.axis_index("ctx") * lax.axis_size("exp")
    total = 0.0
    for offset, inner, down in zip(offsets, inners, downs):
        gate = inner[0]
        activated = (gate / (1.0 + jnp.exp(-gate)) * inner[1]).astype(jnp.bfloat16)
        piece = jnp.dot(activated, down[0], preferred_element_type=jnp.float32)
        expert = base + (lax.axis_index("exp") ^ offset)
        scale = jnp.sum(jnp.where(lane == expert, dense, 0.0), axis=1, keepdims=True)
        total = total + piece.astype(jnp.bfloat16).astype(jnp.float32) * scale
    start = 0
    for out in outs:
        out[...] = total[start : start + out.shape[0]].astype(out.dtype)
        start += out.shape[0]


def expert_apply(groups, kinds, weights):
    count = len(weights)
    rows = jnp.concatenate(groups, axis=0)
    _, hidden, width = weights[0][2].shape
    inners = [
        jnp.einsum("nd,dgh->gnh", rows[:, :width], gate_up[0], preferred_element_type=jnp.float32)
        for _, gate_up, _ in weights
    ]

    return pl.pallas_call(
        functools.partial(down_kernel, [offset for offset, _, _ in weights]),
        out_shape=[
            jax.ShapeDtypeStruct((group.shape[0], width), kind)
            for group, kind in zip(groups, kinds)
        ],
        in_specs=whole_specs(1 + 2 * count),
        out_specs=whole_specs(len(groups)),
        compiler_params=LIMIT,
        cost_estimate=pl.CostEstimate(
            flops=2 * count * rows.shape[0] * width * hidden,
            bytes_accessed=2 << 20,
            transcendentals=0,
        ),
    )(rows, *inners, *[down for _, _, down in weights])


def near_parts(part):
    held = [(0, part)]
    for stride in strides(lax.axis_size("exp"))[1:]:
        held = held + [(offset ^ stride, swap(first, "exp", stride)) for offset, first in held]
    return held


def chunks_of(count):
    chunks = [range((count + 1) // 2, count), range((count + 1) // 2)]
    return [list(chunk) for chunk in chunks if len(chunk)]


def mixture_of(rows, weights):
    tokens = rows.shape[0]
    far = strides(lax.axis_size("exp"))[:1]
    chunks = chunks_of(lax.axis_size("ctx"))

    joined, source = [], rows
    for chunk in chunks:
        blocks = [rows if offset == 0 else swap(source, "ctx", offset) for offset in chunk]
        joined.append(jnp.concatenate(blocks, axis=0))
        source, _ = lax.optimization_barrier((rows, blocks[-1]))
    crossed = []
    for piece in joined if far else []:
        crossed.append(swap(piece, "exp", far[0]))
    *homes, first = expert_apply(
        joined + (crossed or joined)[:1], [jnp.float32] * len(joined) + [jnp.bfloat16], weights
    )
    total, arrived = None, []
    for number, (chunk, value) in enumerate(zip(chunks, homes)):
        if far:
            other = first
            if number:
                piece = crossed[number]
                (other,) = expert_apply([piece], [jnp.bfloat16], weights)
            value = value + swap(other, "exp", far[0]).astype(jnp.float32)
        for position, offset in enumerate(chunk):
            block = value[position * tokens : (position + 1) * tokens]
            if offset == 0:
                total = block
            else:
                arrived.append(swap(block.astype(jnp.bfloat16), "ctx", offset))
    for block in arrived:
        total = total + block.astype(jnp.float32)
    return total


def per_device(
    queries,
    pages,
    cached_lengths,
    residual_in,
    out_weight,
    norm_gain,
    expert_ids,
    route_scores,
    expert_input,
    expert_output,
):
    requests = queries.shape[0]
    core_place = lax.axis_index("rep")
    rep_count = lax.axis_size("rep")
    exp_count = lax.axis_size("exp")
    expert_count = lax.axis_size("ctx") * exp_count
    token_block, model_width = residual_in.shape[1:]
    token_count = requests * token_block

    gate_ups = near_parts(expert_input)
    contexts, keeps, sends = [], [], []
    for r in range(requests):
        context, keep, send = attention(
            queries[r],
            pages[r],
            cached_lengths[r],
            out_weight,
            token_block,
        )
        contexts.append(context)
        keeps.append(keep)
        sends.extend(send)
    context = jnp.stack(contexts)

    by_block = lambda values: [value.reshape(-1, token_block, model_width) for value in values]
    parts = [jnp.stack(by_block(keeps), axis=1)]
    send = jnp.stack(by_block(sends), axis=1) if sends else None
    for stride in reversed(strides(exp_count)):
        arrived = swap(send, "exp", stride)
        if parts[0].shape[0] > 1:
            total = parts[0] + arrived.astype(jnp.float32)
            half = total.shape[0] // 2
            parts, send = [total[:half]], total[half:].astype(jnp.bfloat16)
        else:
            parts = [parts[0], arrived]
    downs = near_parts(lax.optimization_barrier((expert_output, parts[0]))[0])
    weights = [(offset, first, down) for (offset, first), (_, down) in zip(gate_ups, downs)]
    parts = [part.reshape(-1, model_width) for part in parts]
    residual, ids, scores = residual_in, expert_ids, route_scores
    if rep_count > 1:
        share_size = token_block // rep_count
        share = sum(part.astype(jnp.float32) for part in parts).astype(jnp.bfloat16)
        share = share.reshape(requests, token_block, model_width)
        share = lax.psum_scatter(share, "rep", scatter_dimension=1, tiled=True)
        parts = [share.reshape(-1, model_width)]
        residual, ids, scores = (
            lax.dynamic_slice_in_dim(whole, core_place * share_size, share_size, 1)
            for whole in (residual, ids, scores)
        )
    own_hidden, normed = finish(
        parts,
        [first for _, first in gate_ups[1:]],
        residual.reshape(-1, model_width),
        norm_gain,
        ids.reshape(-1, ids.shape[2]).T,
        scores.reshape(-1, ids.shape[2]).T,
        expert_count,
    )
    own_hidden = own_hidden.reshape(requests, -1, model_width)
    if rep_count > 1:
        normed = normed.reshape(requests, share_size, -1)
        normed = lax.all_gather(normed, "rep", axis=1, tiled=True)
        normed = normed.reshape(token_count, -1)

    mixture = mixture_of(normed, weights)
    mixture = mixture.reshape(requests, token_block, model_width)
    if rep_count > 1:
        mixture = lax.psum_scatter(
            mixture.astype(jnp.bfloat16), "rep", scatter_dimension=1, tiled=True
        ).astype(jnp.float32)
    layer_out = (own_hidden.astype(jnp.float32) + mixture).astype(jnp.bfloat16)
    return (context, layer_out)


def solution(mesh):
    in_specs = (
        P("groups", "ctx", ("exp", "rep")),
        P("groups", "ctx", None, "exp"),
        P("groups", None),
        P("groups", ("ctx", "exp"), None),
        P(("exp", "rep"), None),
        P(),
        P("groups", ("ctx", "exp"), None),
        P("groups", ("ctx", "exp"), None),
        P(("ctx", "exp"), None, None, "rep"),
        P(("ctx", "exp"), "rep", None),
    )
    out_specs = (P("groups", "ctx", ("exp", "rep")), P("groups", ("ctx", "exp", "rep"), None))
    return jax.shard_map(
        per_device, mesh=mesh, in_specs=in_specs, out_specs=out_specs, check_vma=False
    )
```

```python
import functools

import jax
import jax.numpy as jnp
from jax import lax
from jax.experimental import pallas as pl
from jax.experimental.pallas import tpu as pltpu
from jax.sharding import PartitionSpec as P

HEAD = 128

floor_value = -1e30
norm_epsilon = 1e-06


def normalize(hidden, norm_gain):
    widened = hidden.astype(jnp.float32)
    mean_square = jnp.mean(widened * widened, axis=-1, keepdims=True)
    return (widened * lax.rsqrt(mean_square + norm_epsilon) * norm_gain).astype(jnp.bfloat16)


def strides(count):
    assert count & (count - 1) == 0
    return [1 << bit for bit in reversed(range(count.bit_length() - 1))]


def sum_order(held):
    offsets = [0]
    for stride in held:
        offsets = offsets + [offset ^ stride for offset in offsets]
    return offsets


def swap(value, axis, stride):
    return lax.ppermute(value, axis, [(i, i ^ stride) for i in range(lax.axis_size(axis))])


def shift(value, axis, step):
    count = lax.axis_size(axis)
    return lax.ppermute(value, axis, [(i, (i + step) % count) for i in range(count)])


def whole_specs(count):
    return [pl.BlockSpec(memory_space=pltpu.VMEM)] * count


SMEM_SPEC = pl.BlockSpec(memory_space=pltpu.SMEM)
LIMIT = pltpu.CompilerParams(vmem_limit_bytes=12 * 1024 * 1024)


def stack_heads(queries):
    heads = queries.shape[1] // HEAD
    return jnp.concatenate(
        [queries[:, h * HEAD : (h + 1) * HEAD] for h in range(heads)], axis=0
    )


def page_weights(stacked, keys, page, length, place, fresh_block):
    rows, page_size = stacked.shape[0], keys.shape[0]
    slab_size = page_size - fresh_block
    scores = lax.dot_general(
        keys, stacked, (((1,), (1,)), ((), ())), preferred_element_type=jnp.float32
    )
    lanes = HEAD if HEAD % fresh_block == 0 and rows % HEAD == 0 else rows
    offset = lax.broadcasted_iota(jnp.int32, (slab_size, lanes), 0)
    fresh = page * fresh_block + lax.broadcasted_iota(jnp.int32, (fresh_block, lanes), 0)
    lane = lax.broadcasted_iota(jnp.int32, (fresh_block, lanes), 1)
    position = place * fresh_block + lax.rem(lane, fresh_block)
    bias = jnp.concatenate(
        [
            jnp.where(offset < length, 0.0, floor_value),
            jnp.where(fresh <= position, 0.0, floor_value),
        ],
        axis=0,
    )
    masked = scores + jnp.concatenate([bias] * (rows // lanes), axis=1)
    peak = jnp.max(masked, axis=0, keepdims=True)
    weights = jnp.exp((masked - peak) * (HEAD**-0.5))
    total = jnp.sum(weights, axis=0, keepdims=True)
    return peak, total, weights.astype(jnp.bfloat16)


def weighted(values, weights):
    return lax.dot_general(
        values, weights, (((0,), (0,)), ((), ())), preferred_element_type=jnp.float32
    )


def page_partial(stacked, keys, values, page, length, place, fresh_block):
    peak, total, weights = page_weights(stacked, keys, page, length, place, fresh_block)
    return peak, total, weighted(values, weights)


def merge(first, second):
    peak = jnp.maximum(first[0], second[0])
    scale_first = jnp.exp((first[0] - peak) * (HEAD**-0.5))
    scale_second = jnp.exp((second[0] - peak) * (HEAD**-0.5))
    return (
        peak,
        first[1] * scale_first + second[1] * scale_second,
        first[2] * scale_first + second[2] * scale_second,
    )


def page_at(offset):
    count = lax.axis_size("ctx")
    return lax.rem(lax.axis_index("ctx") + offset + count, count)


def first_kernel(fresh_block, count, lengths, queries, keys, values, *refs):
    peak_out, total_out, summed_out, lengths_out = refs[-4:]
    for offset in range(count):
        lengths_out[offset : offset + 1, :] = jnp.full(
            (1, lengths_out.shape[1]), lengths[page_at(offset)], jnp.int32
        )
    place = lax.axis_index("ctx")
    peak_out[...], total_out[...], summed_out[...] = page_partial(
        stack_heads(queries[...]),
        keys[...],
        values[...],
        place,
        lengths[place],
        place,
        fresh_block,
    )


def middle_kernel(offsets, fresh_block, queries, lengths, *refs):
    count = len(offsets)
    pages, (peak, total, summed) = refs[: 2 * count], refs[2 * count : 2 * count + 3]
    outs = refs[2 * count + 3 :]
    stacked = stack_heads(queries[...])
    state = (peak[...], total[...], summed[...])
    for number, offset in enumerate(offsets):
        part = page_partial(
            stacked,
            pages[2 * number][...],
            pages[2 * number + 1][...],
            page_at(offset),
            lengths[offset : offset + 1, :],
            lax.axis_index("ctx"),
            fresh_block,
        )
        state = merge(state, part)
    for out, value in zip(outs, state):
        out[...] = value


def weights_kernel(offset, fresh_block, queries, keys, lengths, peak_out, total_out, weights_out):
    peak_out[...], total_out[...], weights_out[...] = page_weights(
        stack_heads(queries[...]),
        keys[...],
        page_at(offset),
        lengths[offset : offset + 1, :],
        lax.axis_index("ctx"),
        fresh_block,
    )


def late_kernel(
    fresh_block,
    values,
    last_peak,
    last_total,
    weights,
    peak,
    total,
    summed,
    weight,
    context_out,
    keep_out,
    *rest,
):
    send_out, blocks = rest[:-1], rest[-1]
    part = (last_peak[...], last_total[...], weighted(values[...], weights[...]))
    state = merge((peak[...], total[...], summed[...]), part)
    result = jnp.transpose(state[2] / state[1])
    context = jnp.concatenate(
        [
            result[h * fresh_block : (h + 1) * fresh_block]
            for h in range(result.shape[0] // fresh_block)
        ],
        axis=1,
    ).astype(jnp.bfloat16)
    context_out[...] = context
    blocks[...] = jnp.dot(context, weight[...], preferred_element_type=jnp.float32)
    place = lax.axis_index("exp")
    offsets = sum_order(strides(lax.axis_size("exp")))
    size = blocks.shape[0] // len(offsets)
    half = keep_out.shape[0] // size
    for number, offset in enumerate(offsets):
        index = place ^ offset
        value = blocks[pl.ds(pl.multiple_of(index * size, size), size), :]
        if number < half:
            keep_out[number * size : (number + 1) * size, :] = value
        else:
            low = (number - half) * size
            send_out[0][low : low + size, :] = value.astype(jnp.bfloat16)


def attention(queries, pages, lengths, out_weight, token_block):
    fresh_block, width = queries.shape
    rows = width // HEAD * fresh_block
    count = lax.axis_size("ctx")
    exp_count = lax.axis_size("exp")
    model_width = out_weight.shape[1]
    own_keys, own_values = pages[:, 0], pages[:, 1]
    held = []
    left_keys, left_values = own_keys, own_values
    right_keys, right_values = own_keys, own_values
    for step in range(1, (count - 1) // 2 + 1):
        right_keys = shift(right_keys, "ctx", -1)
        left_values = shift(left_values, "ctx", 1)
        right_values = shift(right_values, "ctx", -1)
        left_keys = shift(left_keys, "ctx", 1)
        held.append((count - step, left_keys, left_values))
        held.append((step, right_keys, right_values))
    if count % 2 == 0:
        last = (count // 2, shift(right_keys, "ctx", -1), shift(left_values, "ctx", 1))
    else:
        last = held.pop()
    page_flops = 4 * rows * pages.shape[0] * HEAD
    line = jax.ShapeDtypeStruct((1, rows), jnp.float32)
    partial_shape = (line, line, jax.ShapeDtypeStruct((HEAD, rows), jnp.float32))
    *state, page_lengths = pl.pallas_call(
        functools.partial(first_kernel, fresh_block, count),
        out_shape=partial_shape + (jax.ShapeDtypeStruct((count, HEAD), jnp.int32),),
        in_specs=[SMEM_SPEC]
        + whole_specs(3)
        + [pl.BlockSpec(memory_space=pl.ANY)],
        out_specs=tuple(whole_specs(4)),
        compiler_params=LIMIT,
        cost_estimate=pl.CostEstimate(
            flops=16 * page_flops, bytes_accessed=8 << 20, transcendentals=0
        ),
    )(lengths, queries, own_keys, own_values, out_weight)
    for start in range(0, len(held), 2):
        group = held[start : start + 2]
        operands = [part for _, keys, values in group for part in (keys, values)]
        state = pl.pallas_call(
            functools.partial(middle_kernel, [offset for offset, _, _ in group], fresh_block),
            out_shape=partial_shape,
            in_specs=whole_specs(5 + len(operands)),
            out_specs=tuple(whole_specs(3)),
            compiler_params=LIMIT,
            cost_estimate=pl.CostEstimate(
                flops=len(group) * page_flops, bytes_accessed=2 << 20, transcendentals=0
            ),
        )(queries, page_lengths, *operands, *state)
    half = (max(1, exp_count // 2) * token_block, model_width)
    shapes = [
        jax.ShapeDtypeStruct(queries.shape, jnp.bfloat16),
        jax.ShapeDtypeStruct(half, jnp.float32),
    ]
    if exp_count > 1:
        shapes.append(jax.ShapeDtypeStruct(half, jnp.bfloat16))
    last_weights = pl.pallas_call(
        functools.partial(weights_kernel, last[0], fresh_block),
        out_shape=(line, line, jax.ShapeDtypeStruct((pages.shape[0], rows), jnp.bfloat16)),
        in_specs=whole_specs(3),
        out_specs=tuple(whole_specs(3)),
        compiler_params=LIMIT,
        cost_estimate=pl.CostEstimate(
            flops=page_flops, bytes_accessed=1 << 20, transcendentals=0
        ),
    )(queries, last[1], page_lengths)
    outs = pl.pallas_call(
        functools.partial(late_kernel, fresh_block),
        out_shape=shapes,
        in_specs=whole_specs(8),
        out_specs=whole_specs(len(shapes)),
        scratch_shapes=[pltpu.VMEM((fresh_block, model_width), jnp.float32)],
        compiler_params=LIMIT,
        cost_estimate=pl.CostEstimate(
            flops=page_flops + 2 * fresh_block * width * model_width,
            bytes_accessed=6 << 20,
            transcendentals=0,
        ),
    )(last[2], *last_weights, *state, out_weight)
    return outs[0], outs[1], outs[2:]


def finish_kernel(count, *refs):
    parts, (residual, gain, ids, scores), (hidden_out, sent_out) = (
        refs[:count],
        refs[count : count + 4],
        refs[-2:],
    )
    total = residual[...].astype(jnp.float32)
    for part in parts:
        total = total + part[...].astype(jnp.float32)
    hidden = total.astype(jnp.bfloat16)
    hidden_out[...] = hidden
    width = hidden.shape[1]
    sent_out[:, :width] = normalize(hidden, gain[...])
    chosen = jnp.transpose(scores[...])
    ids = jnp.transpose(ids[...])
    combine = (chosen / jnp.sum(chosen, axis=1, keepdims=True)).astype(jnp.bfloat16)
    combine = combine.astype(jnp.float32)
    tokens, choices = chosen.shape
    expert = lax.broadcasted_iota(jnp.int32, (tokens, sent_out.shape[1] - width), 1)
    dense = jnp.zeros(expert.shape, jnp.float32)
    for k in range(choices):
        dense = dense + jnp.where(ids[:, k : k + 1] == expert, combine[:, k : k + 1], 0.0)
    sent_out[:, width:] = dense.astype(jnp.bfloat16)


def finish(parts, swapped, residual, norm_gain, ids, scores, expert_count):
    tokens, width = residual.shape
    lanes = -(-expert_count // 128) * 128
    return pl.pallas_call(
        functools.partial(finish_kernel, len(parts)),
        out_shape=(
            jax.ShapeDtypeStruct((tokens, width), jnp.bfloat16),
            jax.ShapeDtypeStruct((tokens, width + lanes), jnp.bfloat16),
        ),
        in_specs=whole_specs(len(parts) + 4)
        + [pl.BlockSpec(memory_space=pl.ANY)] * len(swapped),
        out_specs=tuple(whole_specs(2)),
        compiler_params=LIMIT,
        cost_estimate=pl.CostEstimate(
            flops=8 * residual.size, bytes_accessed=1 << 19, transcendentals=0
        ),
    )(*parts, residual, norm_gain[None], ids, scores, *swapped)


def down_kernel(offsets, rows, *refs):
    count = len(offsets)
    inners, downs, outs = refs[:count], refs[count : 2 * count], refs[2 * count :]
    dense = rows[:, outs[0].shape[1] :].astype(jnp.float32)
    lane = lax.broadcasted_iota(jnp.int32, dense.shape, 1)
    base = lax.axis_index("ctx") * lax.axis_size("exp")
    total = 0.0
    for offset, inner, down in zip(offsets, inners, downs):
        gate = inner[0]
        activated = (gate / (1.0 + jnp.exp(-gate)) * inner[1]).astype(jnp.bfloat16)
        piece = jnp.dot(activated, down[0], preferred_element_type=jnp.float32)
        expert = base + (lax.axis_index("exp") ^ offset)
        scale = jnp.sum(jnp.where(lane == expert, dense, 0.0), axis=1, keepdims=True)
        total = total + piece.astype(jnp.bfloat16).astype(jnp.float32) * scale
    start = 0
    for out in outs:
        out[...] = total[start : start + out.shape[0]].astype(out.dtype)
        start += out.shape[0]


def expert_apply(groups, kinds, weights):
    count = len(weights)
    rows = jnp.concatenate(groups, axis=0)
    _, hidden, width = weights[0][2].shape
    inners = [
        jnp.einsum("nd,dgh->gnh", rows[:, :width], gate_up[0], preferred_element_type=jnp.float32)
        for _, gate_up, _ in weights
    ]

    return pl.pallas_call(
        functools.partial(down_kernel, [offset for offset, _, _ in weights]),
        out_shape=[
            jax.ShapeDtypeStruct((group.shape[0], width), kind)
            for group, kind in zip(groups, kinds)
        ],
        in_specs=whole_specs(1 + 2 * count),
        out_specs=whole_specs(len(groups)),
        compiler_params=LIMIT,
        cost_estimate=pl.CostEstimate(
            flops=2 * count * rows.shape[0] * width * hidden,
            bytes_accessed=2 << 20,
            transcendentals=0,
        ),
    )(rows, *inners, *[down for _, _, down in weights])


def near_parts(part):
    held = [(0, part)]
    for stride in strides(lax.axis_size("exp"))[1:]:
        held = held + [(offset ^ stride, swap(first, "exp", stride)) for offset, first in held]
    return held


def chunks_of(count):
    chunks = [range((count + 1) // 2, count), range((count + 1) // 2)]
    return [list(chunk) for chunk in chunks if len(chunk)]


def mixture_of(rows, weights):
    tokens = rows.shape[0]
    far = strides(lax.axis_size("exp"))[:1]
    chunks = chunks_of(lax.axis_size("ctx"))

    joined = [
        jnp.concatenate(
            [rows if offset == 0 else swap(rows, "ctx", offset) for offset in chunk], axis=0
        )
        for chunk in chunks
    ]
    crossed = []
    for piece in joined if far else []:
        crossed.append(swap(piece, "exp", far[0]))
    *homes, first = expert_apply(
        joined + (crossed or joined)[:1], [jnp.float32] * len(joined) + [jnp.bfloat16], weights
    )
    total, arrived = None, []
    for number, (chunk, value) in enumerate(zip(chunks, homes)):
        if far:
            other = first
            if number:
                (other,) = expert_apply(crossed[number : number + 1], [jnp.bfloat16], weights)
            value = value + swap(other, "exp", far[0]).astype(jnp.float32)
        for position, offset in enumerate(chunk):
            block = value[position * tokens : (position + 1) * tokens]
            if offset == 0:
                total = block
            else:
                arrived.append(swap(block.astype(jnp.bfloat16), "ctx", offset))
    for block in arrived:
        total = total + block.astype(jnp.float32)
    return total


def per_device(
    queries,
    pages,
    cached_lengths,
    residual_in,
    out_weight,
    norm_gain,
    expert_ids,
    route_scores,
    expert_input,
    expert_output,
):
    requests = queries.shape[0]
    core_place = lax.axis_index("rep")
    rep_count = lax.axis_size("rep")
    exp_count = lax.axis_size("exp")
    expert_count = lax.axis_size("ctx") * exp_count
    token_block, model_width = residual_in.shape[1:]
    token_count = requests * token_block

    gate_ups = near_parts(expert_input)
    contexts, keeps, sends = [], [], []
    for r in range(requests):
        context, keep, send = attention(
            queries[r],
            pages[r],
            cached_lengths[r],
            out_weight,
            token_block,
        )
        contexts.append(context)
        keeps.append(keep)
        sends.extend(send)
    context = jnp.stack(contexts)

    by_block = lambda values: [value.reshape(-1, token_block, model_width) for value in values]
    parts = [jnp.stack(by_block(keeps), axis=1)]
    send = jnp.stack(by_block(sends), axis=1) if sends else None
    for stride in reversed(strides(exp_count)):
        arrived = swap(send, "exp", stride)
        if parts[0].shape[0] > 1:
            total = parts[0] + arrived.astype(jnp.float32)
            half = total.shape[0] // 2
            parts, send = [total[:half]], total[half:].astype(jnp.bfloat16)
        else:
            parts = [parts[0], arrived]
    downs = near_parts(lax.optimization_barrier((expert_output, parts[0]))[0])
    weights = [(offset, first, down) for (offset, first), (_, down) in zip(gate_ups, downs)]
    parts = [part.reshape(-1, model_width) for part in parts]
    residual, ids, scores = residual_in, expert_ids, route_scores
    if rep_count > 1:
        share_size = token_block // rep_count
        share = sum(part.astype(jnp.float32) for part in parts).astype(jnp.bfloat16)
        share = share.reshape(requests, token_block, model_width)
        share = lax.psum_scatter(share, "rep", scatter_dimension=1, tiled=True)
        parts = [share.reshape(-1, model_width)]
        residual, ids, scores = (
            lax.dynamic_slice_in_dim(whole, core_place * share_size, share_size, 1)
            for whole in (residual, ids, scores)
        )
    own_hidden, normed = finish(
        parts,
        [first for _, first in gate_ups[1:]],
        residual.reshape(-1, model_width),
        norm_gain,
        ids.reshape(-1, ids.shape[2]).T,
        scores.reshape(-1, ids.shape[2]).T,
        expert_count,
    )
    own_hidden = own_hidden.reshape(requests, -1, model_width)
    if rep_count > 1:
        normed = normed.reshape(requests, share_size, -1)
        normed = lax.all_gather(normed, "rep", axis=1, tiled=True)
        normed = normed.reshape(token_count, -1)

    mixture = mixture_of(normed, weights)
    mixture = mixture.reshape(requests, token_block, model_width)
    if rep_count > 1:
        mixture = lax.psum_scatter(
            mixture.astype(jnp.bfloat16), "rep", scatter_dimension=1, tiled=True
        ).astype(jnp.float32)
    layer_out = (own_hidden.astype(jnp.float32) + mixture).astype(jnp.bfloat16)
    return (context, layer_out)


def solution(mesh):
    in_specs = (
        P("groups", "ctx", ("exp", "rep")),
        P("groups", "ctx", None, "exp"),
        P("groups", None),
        P("groups", ("ctx", "exp"), None),
        P(("exp", "rep"), None),
        P(),
        P("groups", ("ctx", "exp"), None),
        P("groups", ("ctx", "exp"), None),
        P(("ctx", "exp"), None, None, "rep"),
        P(("ctx", "exp"), "rep", None),
    )
    out_specs = (P("groups", "ctx", ("exp", "rep")), P("groups", ("ctx", "exp", "rep"), None))
    return jax.shard_map(
        per_device, mesh=mesh, in_specs=in_specs, out_specs=out_specs, check_vma=False
    )
```

```python
import functools

import jax
import jax.numpy as jnp
from jax import lax
from jax.experimental import pallas as pl
from jax.experimental.pallas import tpu as pltpu
from jax.sharding import PartitionSpec as P

HEAD = 128

floor_value = -1e30
norm_epsilon = 1e-06


def normalize(hidden, norm_gain):
    widened = hidden.astype(jnp.float32)
    mean_square = jnp.mean(widened * widened, axis=-1, keepdims=True)
    return (widened * lax.rsqrt(mean_square + norm_epsilon) * norm_gain).astype(jnp.bfloat16)


def strides(count):
    assert count & (count - 1) == 0
    return [1 << bit for bit in reversed(range(count.bit_length() - 1))]


def sum_order(held):
    offsets = [0]
    for stride in held:
        offsets = offsets + [offset ^ stride for offset in offsets]
    return offsets


def swap(value, axis, stride):
    return lax.ppermute(value, axis, [(i, i ^ stride) for i in range(lax.axis_size(axis))])


def shift(value, axis, step):
    count = lax.axis_size(axis)
    return lax.ppermute(value, axis, [(i, (i + step) % count) for i in range(count)])


def whole_specs(count):
    return [pl.BlockSpec(memory_space=pltpu.VMEM)] * count


SMEM_SPEC = pl.BlockSpec(memory_space=pltpu.SMEM)
LIMIT = pltpu.CompilerParams(vmem_limit_bytes=12 * 1024 * 1024)


def stack_heads(queries):
    heads = queries.shape[1] // HEAD
    return jnp.concatenate(
        [queries[:, h * HEAD : (h + 1) * HEAD] for h in range(heads)], axis=0
    )


def page_weights(stacked, keys, page, length, place, fresh_block):
    rows, page_size = stacked.shape[0], keys.shape[0]
    slab_size = page_size - fresh_block
    scores = lax.dot_general(
        keys, stacked, (((1,), (1,)), ((), ())), preferred_element_type=jnp.float32
    )
    lanes = HEAD if HEAD % fresh_block == 0 and rows % HEAD == 0 else rows
    offset = lax.broadcasted_iota(jnp.int32, (slab_size, lanes), 0)
    fresh = page * fresh_block + lax.broadcasted_iota(jnp.int32, (fresh_block, lanes), 0)
    lane = lax.broadcasted_iota(jnp.int32, (fresh_block, lanes), 1)
    position = place * fresh_block + lax.rem(lane, fresh_block)
    bias = jnp.concatenate(
        [
            jnp.where(offset < length, 0.0, floor_value),
            jnp.where(fresh <= position, 0.0, floor_value),
        ],
        axis=0,
    )
    masked = scores + jnp.concatenate([bias] * (rows // lanes), axis=1)
    peak = jnp.max(masked, axis=0, keepdims=True)
    weights = jnp.exp((masked - peak) * (HEAD**-0.5))
    total = jnp.sum(weights, axis=0, keepdims=True)
    return peak, total, weights.astype(jnp.bfloat16)


def weighted(values, weights):
    return lax.dot_general(
        values, weights, (((0,), (0,)), ((), ())), preferred_element_type=jnp.float32
    )


def page_partial(stacked, keys, values, page, length, place, fresh_block):
    peak, total, weights = page_weights(stacked, keys, page, length, place, fresh_block)
    return peak, total, weighted(values, weights)


def merge(first, second):
    peak = jnp.maximum(first[0], second[0])
    scale_first = jnp.exp((first[0] - peak) * (HEAD**-0.5))
    scale_second = jnp.exp((second[0] - peak) * (HEAD**-0.5))
    return (
        peak,
        first[1] * scale_first + second[1] * scale_second,
        first[2] * scale_first + second[2] * scale_second,
    )


def page_at(offset):
    count = lax.axis_size("ctx")
    return lax.rem(lax.axis_index("ctx") + offset + count, count)


def first_kernel(fresh_block, count, lengths, queries, keys, values, *refs):
    peak_out, total_out, summed_out, lengths_out = refs[-4:]
    for offset in range(count):
        lengths_out[offset : offset + 1, :] = jnp.full(
            (1, lengths_out.shape[1]), lengths[page_at(offset)], jnp.int32
        )
    place = lax.axis_index("ctx")
    peak_out[...], total_out[...], summed_out[...] = page_partial(
        stack_heads(queries[...]),
        keys[...],
        values[...],
        place,
        lengths[place],
        place,
        fresh_block,
    )


def middle_kernel(offsets, fresh_block, queries, lengths, *refs):
    count = len(offsets)
    pages, (peak, total, summed) = refs[: 2 * count], refs[2 * count : 2 * count + 3]
    outs = refs[2 * count + 3 :]
    stacked = stack_heads(queries[...])
    state = (peak[...], total[...], summed[...])
    for number, offset in enumerate(offsets):
        part = page_partial(
            stacked,
            pages[2 * number][...],
            pages[2 * number + 1][...],
            page_at(offset),
            lengths[offset : offset + 1, :],
            lax.axis_index("ctx"),
            fresh_block,
        )
        state = merge(state, part)
    for out, value in zip(outs, state):
        out[...] = value


def weights_kernel(offset, fresh_block, queries, keys, lengths, peak_out, total_out, weights_out):
    peak_out[...], total_out[...], weights_out[...] = page_weights(
        stack_heads(queries[...]),
        keys[...],
        page_at(offset),
        lengths[offset : offset + 1, :],
        lax.axis_index("ctx"),
        fresh_block,
    )


def late_kernel(
    fresh_block,
    values,
    last_peak,
    last_total,
    weights,
    peak,
    total,
    summed,
    weight,
    context_out,
    keep_out,
    *rest,
):
    send_out, blocks = rest[:-1], rest[-1]
    part = (last_peak[...], last_total[...], weighted(values[...], weights[...]))
    state = merge((peak[...], total[...], summed[...]), part)
    result = jnp.transpose(state[2] / state[1])
    context = jnp.concatenate(
        [
            result[h * fresh_block : (h + 1) * fresh_block]
            for h in range(result.shape[0] // fresh_block)
        ],
        axis=1,
    ).astype(jnp.bfloat16)
    context_out[...] = context
    blocks[...] = jnp.dot(context, weight[...], preferred_element_type=jnp.float32)
    place = lax.axis_index("exp")
    offsets = sum_order(strides(lax.axis_size("exp")))
    size = blocks.shape[0] // len(offsets)
    half = keep_out.shape[0] // size
    for number, offset in enumerate(offsets):
        index = place ^ offset
        value = blocks[pl.ds(pl.multiple_of(index * size, size), size), :]
        if number < half:
            keep_out[number * size : (number + 1) * size, :] = value
        else:
            low = (number - half) * size
            send_out[0][low : low + size, :] = value.astype(jnp.bfloat16)


def attention(queries, pages, lengths, out_weight, token_block):
    fresh_block, width = queries.shape
    rows = width // HEAD * fresh_block
    count = lax.axis_size("ctx")
    exp_count = lax.axis_size("exp")
    model_width = out_weight.shape[1]
    own_keys, own_values = pages[:, 0], pages[:, 1]
    held = []
    left_keys, left_values = own_keys, own_values
    right_keys, right_values = own_keys, own_values
    for step in range(1, (count - 1) // 2 + 1):
        right_keys = shift(right_keys, "ctx", -1)
        left_values = shift(left_values, "ctx", 1)
        right_values = shift(right_values, "ctx", -1)
        left_keys = shift(left_keys, "ctx", 1)
        held.append((count - step, left_keys, left_values))
        held.append((step, right_keys, right_values))
    if count % 2 == 0:
        last = (count // 2, shift(right_keys, "ctx", -1), shift(left_values, "ctx", 1))
    else:
        last = held.pop()
    page_flops = 4 * rows * pages.shape[0] * HEAD
    line = jax.ShapeDtypeStruct((1, rows), jnp.float32)
    partial_shape = (line, line, jax.ShapeDtypeStruct((HEAD, rows), jnp.float32))
    *state, page_lengths = pl.pallas_call(
        functools.partial(first_kernel, fresh_block, count),
        out_shape=partial_shape + (jax.ShapeDtypeStruct((count, HEAD), jnp.int32),),
        in_specs=[SMEM_SPEC]
        + whole_specs(3)
        + [pl.BlockSpec(memory_space=pl.ANY)],
        out_specs=tuple(whole_specs(4)),
        compiler_params=LIMIT,
        cost_estimate=pl.CostEstimate(
            flops=16 * page_flops, bytes_accessed=8 << 20, transcendentals=0
        ),
    )(lengths, queries, own_keys, own_values, out_weight)
    for start in range(0, len(held), 2):
        group = held[start : start + 2]
        operands = [part for _, keys, values in group for part in (keys, values)]
        state = pl.pallas_call(
            functools.partial(middle_kernel, [offset for offset, _, _ in group], fresh_block),
            out_shape=partial_shape,
            in_specs=whole_specs(5 + len(operands)),
            out_specs=tuple(whole_specs(3)),
            compiler_params=LIMIT,
            cost_estimate=pl.CostEstimate(
                flops=len(group) * page_flops, bytes_accessed=2 << 20, transcendentals=0
            ),
        )(queries, page_lengths, *operands, *state)
    half = (max(1, exp_count // 2) * token_block, model_width)
    shapes = [
        jax.ShapeDtypeStruct(queries.shape, jnp.bfloat16),
        jax.ShapeDtypeStruct(half, jnp.float32),
    ]
    if exp_count > 1:
        shapes.append(jax.ShapeDtypeStruct(half, jnp.bfloat16))
    last_weights = pl.pallas_call(
        functools.partial(weights_kernel, last[0], fresh_block),
        out_shape=(line, line, jax.ShapeDtypeStruct((pages.shape[0], rows), jnp.bfloat16)),
        in_specs=whole_specs(3),
        out_specs=tuple(whole_specs(3)),
        compiler_params=LIMIT,
        cost_estimate=pl.CostEstimate(
            flops=page_flops, bytes_accessed=1 << 20, transcendentals=0
        ),
    )(queries, last[1], page_lengths)
    outs = pl.pallas_call(
        functools.partial(late_kernel, fresh_block),
        out_shape=shapes,
        in_specs=whole_specs(8),
        out_specs=whole_specs(len(shapes)),
        scratch_shapes=[pltpu.VMEM((fresh_block, model_width), jnp.float32)],
        compiler_params=LIMIT,
        cost_estimate=pl.CostEstimate(
            flops=page_flops + 2 * fresh_block * width * model_width,
            bytes_accessed=6 << 20,
            transcendentals=0,
        ),
    )(last[2], *last_weights, *state, out_weight)
    return outs[0], outs[1], outs[2:]


def finish_kernel(count, *refs):
    parts, (residual, gain, ids, scores), (hidden_out, sent_out) = (
        refs[:count],
        refs[count : count + 4],
        refs[-2:],
    )
    total = residual[...].astype(jnp.float32)
    for part in parts:
        total = total + part[...].astype(jnp.float32)
    hidden = total.astype(jnp.bfloat16)
    hidden_out[...] = hidden
    width = hidden.shape[1]
    sent_out[:, :width] = normalize(hidden, gain[...])
    chosen = jnp.transpose(scores[...])
    ids = jnp.transpose(ids[...])
    combine = (chosen / jnp.sum(chosen, axis=1, keepdims=True)).astype(jnp.bfloat16)
    combine = combine.astype(jnp.float32)
    tokens, choices = chosen.shape
    expert = lax.broadcasted_iota(jnp.int32, (tokens, sent_out.shape[1] - width), 1)
    dense = jnp.zeros(expert.shape, jnp.float32)
    for k in range(choices):
        dense = dense + jnp.where(ids[:, k : k + 1] == expert, combine[:, k : k + 1], 0.0)
    sent_out[:, width:] = dense.astype(jnp.bfloat16)


def finish(parts, swapped, residual, norm_gain, ids, scores, expert_count):
    tokens, width = residual.shape
    lanes = -(-expert_count // 128) * 128
    return pl.pallas_call(
        functools.partial(finish_kernel, len(parts)),
        out_shape=(
            jax.ShapeDtypeStruct((tokens, width), jnp.bfloat16),
            jax.ShapeDtypeStruct((tokens, width + lanes), jnp.bfloat16),
        ),
        in_specs=whole_specs(len(parts) + 4)
        + [pl.BlockSpec(memory_space=pl.ANY)] * len(swapped),
        out_specs=tuple(whole_specs(2)),
        compiler_params=LIMIT,
        cost_estimate=pl.CostEstimate(
            flops=8 * residual.size, bytes_accessed=1 << 19, transcendentals=0
        ),
    )(*parts, residual, norm_gain[None], ids, scores, *swapped)


def down_kernel(offsets, rows, *refs):
    count = len(offsets)
    inners, downs, outs = refs[:count], refs[count : 2 * count], refs[2 * count :]
    dense = rows[:, outs[0].shape[1] :].astype(jnp.float32)
    lane = lax.broadcasted_iota(jnp.int32, dense.shape, 1)
    base = lax.axis_index("ctx") * lax.axis_size("exp")
    total = 0.0
    for offset, inner, down in zip(offsets, inners, downs):
        gate = inner[0]
        activated = (gate / (1.0 + jnp.exp(-gate)) * inner[1]).astype(jnp.bfloat16)
        piece = jnp.dot(activated, down[0], preferred_element_type=jnp.float32)
        expert = base + (lax.axis_index("exp") ^ offset)
        scale = jnp.sum(jnp.where(lane == expert, dense, 0.0), axis=1, keepdims=True)
        total = total + piece.astype(jnp.bfloat16).astype(jnp.float32) * scale
    start = 0
    for out in outs:
        out[...] = total[start : start + out.shape[0]].astype(out.dtype)
        start += out.shape[0]


def expert_apply(groups, kinds, weights):
    count = len(weights)
    rows = jnp.concatenate(groups, axis=0)
    _, hidden, width = weights[0][2].shape
    inners = [
        jnp.einsum("nd,dgh->gnh", rows[:, :width], gate_up[0], preferred_element_type=jnp.float32)
        for _, gate_up, _ in weights
    ]

    return pl.pallas_call(
        functools.partial(down_kernel, [offset for offset, _, _ in weights]),
        out_shape=[
            jax.ShapeDtypeStruct((group.shape[0], width), kind)
            for group, kind in zip(groups, kinds)
        ],
        in_specs=whole_specs(1 + 2 * count),
        out_specs=whole_specs(len(groups)),
        compiler_params=LIMIT,
        cost_estimate=pl.CostEstimate(
            flops=2 * count * rows.shape[0] * width * hidden,
            bytes_accessed=2 << 20,
            transcendentals=0,
        ),
    )(rows, *inners, *[down for _, _, down in weights])


def near_parts(part):
    held = [(0, part)]
    for stride in strides(lax.axis_size("exp"))[1:]:
        held = held + [(offset ^ stride, swap(first, "exp", stride)) for offset, first in held]
    return held


def chunks_of(count):
    chunks = [range((count + 1) // 2, count), range((count + 1) // 2)]
    return [list(chunk) for chunk in chunks if len(chunk)]


def mixture_of(rows, weights):
    tokens = rows.shape[0]
    far = strides(lax.axis_size("exp"))[:1]
    chunks = chunks_of(lax.axis_size("ctx"))

    blocks = [
        [rows if offset == 0 else swap(rows, "ctx", offset) for offset in chunk]
        for chunk in chunks
    ]
    joined = [jnp.concatenate(parts, axis=0) for parts in blocks]
    crossed = []
    if far:
        near = swap(joined[-1], "exp", far[0])
        for parts in blocks[:-1]:
            parts[0], _ = lax.optimization_barrier((parts[0], near))
            crossed.append(jnp.concatenate([swap(part, "exp", far[0]) for part in parts], axis=0))
        crossed.append(near)
    *homes, first = expert_apply(
        joined + (crossed or joined)[:1], [jnp.float32] * len(joined) + [jnp.bfloat16], weights
    )
    total, arrived = None, []
    for number, (chunk, value) in enumerate(zip(chunks, homes)):
        if far:
            other = first
            if number:
                (other,) = expert_apply(crossed[number : number + 1], [jnp.bfloat16], weights)
            value = value + swap(other, "exp", far[0]).astype(jnp.float32)
        for position, offset in enumerate(chunk):
            block = value[position * tokens : (position + 1) * tokens]
            if offset == 0:
                total = block
            else:
                arrived.append(swap(block.astype(jnp.bfloat16), "ctx", offset))
    for block in arrived:
        total = total + block.astype(jnp.float32)
    return total


def per_device(
    queries,
    pages,
    cached_lengths,
    residual_in,
    out_weight,
    norm_gain,
    expert_ids,
    route_scores,
    expert_input,
    expert_output,
):
    requests = queries.shape[0]
    core_place = lax.axis_index("rep")
    rep_count = lax.axis_size("rep")
    exp_count = lax.axis_size("exp")
    expert_count = lax.axis_size("ctx") * exp_count
    token_block, model_width = residual_in.shape[1:]
    token_count = requests * token_block

    gate_ups = near_parts(expert_input)
    contexts, keeps, sends = [], [], []
    for r in range(requests):
        context, keep, send = attention(
            queries[r],
            pages[r],
            cached_lengths[r],
            out_weight,
            token_block,
        )
        contexts.append(context)
        keeps.append(keep)
        sends.extend(send)
    context = jnp.stack(contexts)

    by_block = lambda values: [value.reshape(-1, token_block, model_width) for value in values]
    parts = [jnp.stack(by_block(keeps), axis=1)]
    send = jnp.stack(by_block(sends), axis=1) if sends else None
    for stride in reversed(strides(exp_count)):
        arrived = swap(send, "exp", stride)
        if parts[0].shape[0] > 1:
            total = parts[0] + arrived.astype(jnp.float32)
            half = total.shape[0] // 2
            parts, send = [total[:half]], total[half:].astype(jnp.bfloat16)
        else:
            parts = [parts[0], arrived]
    downs = near_parts(lax.optimization_barrier((expert_output, parts[0]))[0])
    weights = [(offset, first, down) for (offset, first), (_, down) in zip(gate_ups, downs)]
    parts = [part.reshape(-1, model_width) for part in parts]
    residual, ids, scores = residual_in, expert_ids, route_scores
    if rep_count > 1:
        share_size = token_block // rep_count
        share = sum(part.astype(jnp.float32) for part in parts).astype(jnp.bfloat16)
        share = share.reshape(requests, token_block, model_width)
        share = lax.psum_scatter(share, "rep", scatter_dimension=1, tiled=True)
        parts = [share.reshape(-1, model_width)]
        residual, ids, scores = (
            lax.dynamic_slice_in_dim(whole, core_place * share_size, share_size, 1)
            for whole in (residual, ids, scores)
        )
    own_hidden, normed = finish(
        parts,
        [first for _, first in gate_ups[1:]],
        residual.reshape(-1, model_width),
        norm_gain,
        ids.reshape(-1, ids.shape[2]).T,
        scores.reshape(-1, ids.shape[2]).T,
        expert_count,
    )
    own_hidden = own_hidden.reshape(requests, -1, model_width)
    if rep_count > 1:
        normed = normed.reshape(requests, share_size, -1)
        normed = lax.all_gather(normed, "rep", axis=1, tiled=True)
        normed = normed.reshape(token_count, -1)

    mixture = mixture_of(normed, weights)
    mixture = mixture.reshape(requests, token_block, model_width)
    if rep_count > 1:
        mixture = lax.psum_scatter(
            mixture.astype(jnp.bfloat16), "rep", scatter_dimension=1, tiled=True
        ).astype(jnp.float32)
    layer_out = (own_hidden.astype(jnp.float32) + mixture).astype(jnp.bfloat16)
    return (context, layer_out)


def solution(mesh):
    in_specs = (
        P("groups", "ctx", ("exp", "rep")),
        P("groups", "ctx", None, "exp"),
        P("groups", None),
        P("groups", ("ctx", "exp"), None),
        P(("exp", "rep"), None),
        P(),
        P("groups", ("ctx", "exp"), None),
        P("groups", ("ctx", "exp"), None),
        P(("ctx", "exp"), None, None, "rep"),
        P(("ctx", "exp"), "rep", None),
    )
    out_specs = (P("groups", "ctx", ("exp", "rep")), P("groups", ("ctx", "exp", "rep"), None))
    return jax.shard_map(
        per_device, mesh=mesh, in_specs=in_specs, out_specs=out_specs, check_vma=False
    )
```

```python
import functools

import jax
import jax.numpy as jnp
from jax import lax
from jax.experimental import pallas as pl
from jax.experimental.pallas import tpu as pltpu
from jax.sharding import PartitionSpec as P

HEAD = 128

floor_value = -1e30
norm_epsilon = 1e-06


def normalize(hidden, norm_gain):
    widened = hidden.astype(jnp.float32)
    mean_square = jnp.mean(widened * widened, axis=-1, keepdims=True)
    return (widened * lax.rsqrt(mean_square + norm_epsilon) * norm_gain).astype(jnp.bfloat16)


def strides(count):
    assert count & (count - 1) == 0
    return [1 << bit for bit in reversed(range(count.bit_length() - 1))]


def sum_order(held):
    offsets = [0]
    for stride in held:
        offsets = offsets + [offset ^ stride for offset in offsets]
    return offsets


def swap(value, axis, stride):
    return lax.ppermute(value, axis, [(i, i ^ stride) for i in range(lax.axis_size(axis))])


def shift(value, axis, step):
    count = lax.axis_size(axis)
    return lax.ppermute(value, axis, [(i, (i + step) % count) for i in range(count)])


def whole_specs(count):
    return [pl.BlockSpec(memory_space=pltpu.VMEM)] * count


SMEM_SPEC = pl.BlockSpec(memory_space=pltpu.SMEM)
LIMIT = pltpu.CompilerParams(vmem_limit_bytes=12 * 1024 * 1024)


def stack_heads(queries):
    heads = queries.shape[1] // HEAD
    return jnp.concatenate(
        [queries[:, h * HEAD : (h + 1) * HEAD] for h in range(heads)], axis=0
    )


def page_weights(stacked, keys, page, length, place, fresh_block):
    rows, page_size = stacked.shape[0], keys.shape[0]
    slab_size = page_size - fresh_block
    scores = lax.dot_general(
        keys, stacked, (((1,), (1,)), ((), ())), preferred_element_type=jnp.float32
    )
    lanes = HEAD if HEAD % fresh_block == 0 and rows % HEAD == 0 else rows
    offset = lax.broadcasted_iota(jnp.int32, (slab_size, lanes), 0)
    fresh = page * fresh_block + lax.broadcasted_iota(jnp.int32, (fresh_block, lanes), 0)
    lane = lax.broadcasted_iota(jnp.int32, (fresh_block, lanes), 1)
    position = place * fresh_block + lax.rem(lane, fresh_block)
    bias = jnp.concatenate(
        [
            jnp.where(offset < length, 0.0, floor_value),
            jnp.where(fresh <= position, 0.0, floor_value),
        ],
        axis=0,
    )
    masked = scores + jnp.concatenate([bias] * (rows // lanes), axis=1)
    peak = jnp.max(masked, axis=0, keepdims=True)
    weights = jnp.exp((masked - peak) * (HEAD**-0.5))
    total = jnp.sum(weights, axis=0, keepdims=True)
    return peak, total, weights.astype(jnp.bfloat16)


def weighted(values, weights):
    return lax.dot_general(
        values, weights, (((0,), (0,)), ((), ())), preferred_element_type=jnp.float32
    )


def page_partial(stacked, keys, values, page, length, place, fresh_block):
    peak, total, weights = page_weights(stacked, keys, page, length, place, fresh_block)
    return peak, total, weighted(values, weights)


def merge(first, second):
    peak = jnp.maximum(first[0], second[0])
    scale_first = jnp.exp((first[0] - peak) * (HEAD**-0.5))
    scale_second = jnp.exp((second[0] - peak) * (HEAD**-0.5))
    return (
        peak,
        first[1] * scale_first + second[1] * scale_second,
        first[2] * scale_first + second[2] * scale_second,
    )


def page_at(offset):
    count = lax.axis_size("ctx")
    return lax.rem(lax.axis_index("ctx") + offset + count, count)


def first_kernel(fresh_block, count, lengths, queries, keys, values, *refs):
    peak_out, total_out, summed_out, lengths_out = refs[-4:]
    for offset in range(count):
        lengths_out[offset : offset + 1, :] = jnp.full(
            (1, lengths_out.shape[1]), lengths[page_at(offset)], jnp.int32
        )
    place = lax.axis_index("ctx")
    peak_out[...], total_out[...], summed_out[...] = page_partial(
        stack_heads(queries[...]),
        keys[...],
        values[...],
        place,
        lengths[place],
        place,
        fresh_block,
    )


def middle_kernel(offsets, fresh_block, queries, lengths, *refs):
    count = len(offsets)
    pages, (peak, total, summed) = refs[: 2 * count], refs[2 * count : 2 * count + 3]
    outs = refs[2 * count + 3 :]
    stacked = stack_heads(queries[...])
    state = (peak[...], total[...], summed[...])
    for number, offset in enumerate(offsets):
        part = page_partial(
            stacked,
            pages[2 * number][...],
            pages[2 * number + 1][...],
            page_at(offset),
            lengths[offset : offset + 1, :],
            lax.axis_index("ctx"),
            fresh_block,
        )
        state = merge(state, part)
    for out, value in zip(outs, state):
        out[...] = value


def weights_kernel(offset, fresh_block, queries, keys, lengths, peak_out, total_out, weights_out):
    peak_out[...], total_out[...], weights_out[...] = page_weights(
        stack_heads(queries[...]),
        keys[...],
        page_at(offset),
        lengths[offset : offset + 1, :],
        lax.axis_index("ctx"),
        fresh_block,
    )


def late_kernel(
    fresh_block,
    values,
    last_peak,
    last_total,
    weights,
    peak,
    total,
    summed,
    weight,
    context_out,
    keep_out,
    *rest,
):
    send_out, blocks = rest[:-1], rest[-1]
    part = (last_peak[...], last_total[...], weighted(values[...], weights[...]))
    state = merge((peak[...], total[...], summed[...]), part)
    result = jnp.transpose(state[2] / state[1])
    context = jnp.concatenate(
        [
            result[h * fresh_block : (h + 1) * fresh_block]
            for h in range(result.shape[0] // fresh_block)
        ],
        axis=1,
    ).astype(jnp.bfloat16)
    context_out[...] = context
    blocks[...] = jnp.dot(context, weight[...], preferred_element_type=jnp.float32)
    place = lax.axis_index("exp")
    offsets = sum_order(strides(lax.axis_size("exp")))
    size = blocks.shape[0] // len(offsets)
    half = keep_out.shape[0] // size
    for number, offset in enumerate(offsets):
        index = place ^ offset
        value = blocks[pl.ds(pl.multiple_of(index * size, size), size), :]
        if number < half:
            keep_out[number * size : (number + 1) * size, :] = value
        else:
            low = (number - half) * size
            send_out[0][low : low + size, :] = value.astype(jnp.bfloat16)


def attention(queries, pages, lengths, out_weight, token_block):
    fresh_block, width = queries.shape
    rows = width // HEAD * fresh_block
    count = lax.axis_size("ctx")
    exp_count = lax.axis_size("exp")
    model_width = out_weight.shape[1]
    own_keys, own_values = pages[:, 0], pages[:, 1]
    held = []
    left_keys, left_values = own_keys, own_values
    right_keys, right_values = own_keys, own_values
    for step in range(1, (count - 1) // 2 + 1):
        left_keys = shift(left_keys, "ctx", 1)
        right_values = shift(right_values, "ctx", -1)
        left_values = shift(left_values, "ctx", 1)
        right_keys, _ = lax.optimization_barrier((right_keys, left_keys))
        right_keys = shift(right_keys, "ctx", -1)
        held.append((count - step, left_keys, left_values))
        held.append((step, right_keys, right_values))
    if count % 2 == 0:
        last = (count // 2, shift(left_keys, "ctx", 1), shift(right_values, "ctx", -1))
    else:
        last = held.pop()
    page_flops = 4 * rows * pages.shape[0] * HEAD
    line = jax.ShapeDtypeStruct((1, rows), jnp.float32)
    partial_shape = (line, line, jax.ShapeDtypeStruct((HEAD, rows), jnp.float32))
    *state, page_lengths = pl.pallas_call(
        functools.partial(first_kernel, fresh_block, count),
        out_shape=partial_shape + (jax.ShapeDtypeStruct((count, HEAD), jnp.int32),),
        in_specs=[SMEM_SPEC]
        + whole_specs(3)
        + [pl.BlockSpec(memory_space=pl.ANY)],
        out_specs=tuple(whole_specs(4)),
        compiler_params=LIMIT,
        cost_estimate=pl.CostEstimate(
            flops=16 * page_flops, bytes_accessed=8 << 20, transcendentals=0
        ),
    )(lengths, queries, own_keys, own_values, out_weight)
    for start in range(0, len(held), 2):
        group = held[start : start + 2]
        operands = [part for _, keys, values in group for part in (keys, values)]
        state = pl.pallas_call(
            functools.partial(middle_kernel, [offset for offset, _, _ in group], fresh_block),
            out_shape=partial_shape,
            in_specs=whole_specs(5 + len(operands)),
            out_specs=tuple(whole_specs(3)),
            compiler_params=LIMIT,
            cost_estimate=pl.CostEstimate(
                flops=len(group) * page_flops, bytes_accessed=2 << 20, transcendentals=0
            ),
        )(queries, page_lengths, *operands, *state)
    half = (max(1, exp_count // 2) * token_block, model_width)
    shapes = [
        jax.ShapeDtypeStruct(queries.shape, jnp.bfloat16),
        jax.ShapeDtypeStruct(half, jnp.float32),
    ]
    if exp_count > 1:
        shapes.append(jax.ShapeDtypeStruct(half, jnp.bfloat16))
    last_weights = pl.pallas_call(
        functools.partial(weights_kernel, last[0], fresh_block),
        out_shape=(line, line, jax.ShapeDtypeStruct((pages.shape[0], rows), jnp.bfloat16)),
        in_specs=whole_specs(3),
        out_specs=tuple(whole_specs(3)),
        compiler_params=LIMIT,
        cost_estimate=pl.CostEstimate(
            flops=page_flops, bytes_accessed=1 << 20, transcendentals=0
        ),
    )(queries, last[1], page_lengths)
    outs = pl.pallas_call(
        functools.partial(late_kernel, fresh_block),
        out_shape=shapes,
        in_specs=whole_specs(8),
        out_specs=whole_specs(len(shapes)),
        scratch_shapes=[pltpu.VMEM((fresh_block, model_width), jnp.float32)],
        compiler_params=LIMIT,
        cost_estimate=pl.CostEstimate(
            flops=page_flops + 2 * fresh_block * width * model_width,
            bytes_accessed=6 << 20,
            transcendentals=0,
        ),
    )(last[2], *last_weights, *state, out_weight)
    return outs[0], outs[1], outs[2:]


def finish_kernel(count, *refs):
    parts, (residual, gain, ids, scores), (hidden_out, sent_out) = (
        refs[:count],
        refs[count : count + 4],
        refs[-2:],
    )
    total = residual[...].astype(jnp.float32)
    for part in parts:
        total = total + part[...].astype(jnp.float32)
    hidden = total.astype(jnp.bfloat16)
    hidden_out[...] = hidden
    width = hidden.shape[1]
    sent_out[:, :width] = normalize(hidden, gain[...])
    chosen = jnp.transpose(scores[...])
    ids = jnp.transpose(ids[...])
    combine = (chosen / jnp.sum(chosen, axis=1, keepdims=True)).astype(jnp.bfloat16)
    combine = combine.astype(jnp.float32)
    tokens, choices = chosen.shape
    expert = lax.broadcasted_iota(jnp.int32, (tokens, sent_out.shape[1] - width), 1)
    dense = jnp.zeros(expert.shape, jnp.float32)
    for k in range(choices):
        dense = dense + jnp.where(ids[:, k : k + 1] == expert, combine[:, k : k + 1], 0.0)
    sent_out[:, width:] = dense.astype(jnp.bfloat16)


def finish(parts, swapped, residual, norm_gain, ids, scores, expert_count):
    tokens, width = residual.shape
    lanes = -(-expert_count // 128) * 128
    return pl.pallas_call(
        functools.partial(finish_kernel, len(parts)),
        out_shape=(
            jax.ShapeDtypeStruct((tokens, width), jnp.bfloat16),
            jax.ShapeDtypeStruct((tokens, width + lanes), jnp.bfloat16),
        ),
        in_specs=whole_specs(len(parts) + 4)
        + [pl.BlockSpec(memory_space=pl.ANY)] * len(swapped),
        out_specs=tuple(whole_specs(2)),
        compiler_params=LIMIT,
        cost_estimate=pl.CostEstimate(
            flops=8 * residual.size, bytes_accessed=1 << 19, transcendentals=0
        ),
    )(*parts, residual, norm_gain[None], ids, scores, *swapped)


def down_kernel(offsets, rows, *refs):
    count = len(offsets)
    inners, downs, outs = refs[:count], refs[count : 2 * count], refs[2 * count :]
    dense = rows[:, outs[0].shape[1] :].astype(jnp.float32)
    lane = lax.broadcasted_iota(jnp.int32, dense.shape, 1)
    base = lax.axis_index("ctx") * lax.axis_size("exp")
    total = 0.0
    for offset, inner, down in zip(offsets, inners, downs):
        gate = inner[0]
        activated = (gate / (1.0 + jnp.exp(-gate)) * inner[1]).astype(jnp.bfloat16)
        piece = jnp.dot(activated, down[0], preferred_element_type=jnp.float32)
        expert = base + (lax.axis_index("exp") ^ offset)
        scale = jnp.sum(jnp.where(lane == expert, dense, 0.0), axis=1, keepdims=True)
        total = total + piece.astype(jnp.bfloat16).astype(jnp.float32) * scale
    start = 0
    for out in outs:
        out[...] = total[start : start + out.shape[0]].astype(out.dtype)
        start += out.shape[0]


def expert_apply(groups, kinds, weights):
    count = len(weights)
    rows = jnp.concatenate(groups, axis=0)
    _, hidden, width = weights[0][2].shape
    inners = [
        jnp.einsum("nd,dgh->gnh", rows[:, :width], gate_up[0], preferred_element_type=jnp.float32)
        for _, gate_up, _ in weights
    ]

    return pl.pallas_call(
        functools.partial(down_kernel, [offset for offset, _, _ in weights]),
        out_shape=[
            jax.ShapeDtypeStruct((group.shape[0], width), kind)
            for group, kind in zip(groups, kinds)
        ],
        in_specs=whole_specs(1 + 2 * count),
        out_specs=whole_specs(len(groups)),
        compiler_params=LIMIT,
        cost_estimate=pl.CostEstimate(
            flops=2 * count * rows.shape[0] * width * hidden,
            bytes_accessed=2 << 20,
            transcendentals=0,
        ),
    )(rows, *inners, *[down for _, _, down in weights])


def near_parts(part):
    held = [(0, part)]
    for stride in strides(lax.axis_size("exp"))[1:]:
        held = held + [(offset ^ stride, swap(first, "exp", stride)) for offset, first in held]
    return held


def chunks_of(count):
    chunks = [range((count + 1) // 2, count), range((count + 1) // 2)]
    return [list(chunk) for chunk in chunks if len(chunk)]


def mixture_of(rows, weights):
    tokens = rows.shape[0]
    far = strides(lax.axis_size("exp"))[:1]
    chunks = chunks_of(lax.axis_size("ctx"))

    joined = [
        jnp.concatenate(
            [rows if offset == 0 else swap(rows, "ctx", offset) for offset in chunk], axis=0
        )
        for chunk in chunks
    ]
    crossed = []
    for piece in joined if far else []:
        crossed.append(swap(piece, "exp", far[0]))
    *homes, first = expert_apply(
        joined + (crossed or joined)[:1], [jnp.float32] * len(joined) + [jnp.bfloat16], weights
    )
    total, arrived = None, []
    for number, (chunk, value) in enumerate(zip(chunks, homes)):
        if far:
            other = first
            if number:
                (other,) = expert_apply(crossed[number : number + 1], [jnp.bfloat16], weights)
            value = value + swap(other, "exp", far[0]).astype(jnp.float32)
        for position, offset in enumerate(chunk):
            block = value[position * tokens : (position + 1) * tokens]
            if offset == 0:
                total = block
            else:
                arrived.append(swap(block.astype(jnp.bfloat16), "ctx", offset))
    for block in arrived:
        total = total + block.astype(jnp.float32)
    return total


def per_device(
    queries,
    pages,
    cached_lengths,
    residual_in,
    out_weight,
    norm_gain,
    expert_ids,
    route_scores,
    expert_input,
    expert_output,
):
    requests = queries.shape[0]
    core_place = lax.axis_index("rep")
    rep_count = lax.axis_size("rep")
    exp_count = lax.axis_size("exp")
    expert_count = lax.axis_size("ctx") * exp_count
    token_block, model_width = residual_in.shape[1:]
    token_count = requests * token_block

    gate_ups = near_parts(expert_input)
    contexts, keeps, sends = [], [], []
    for r in range(requests):
        context, keep, send = attention(
            queries[r],
            pages[r],
            cached_lengths[r],
            out_weight,
            token_block,
        )
        contexts.append(context)
        keeps.append(keep)
        sends.extend(send)
    context = jnp.stack(contexts)

    by_block = lambda values: [value.reshape(-1, token_block, model_width) for value in values]
    parts = [jnp.stack(by_block(keeps), axis=1)]
    send = jnp.stack(by_block(sends), axis=1) if sends else None
    for stride in reversed(strides(exp_count)):
        arrived = swap(send, "exp", stride)
        if parts[0].shape[0] > 1:
            total = parts[0] + arrived.astype(jnp.float32)
            half = total.shape[0] // 2
            parts, send = [total[:half]], total[half:].astype(jnp.bfloat16)
        else:
            parts = [parts[0], arrived]
    downs = near_parts(lax.optimization_barrier((expert_output, parts[0]))[0])
    weights = [(offset, first, down) for (offset, first), (_, down) in zip(gate_ups, downs)]
    parts = [part.reshape(-1, model_width) for part in parts]
    residual, ids, scores = residual_in, expert_ids, route_scores
    if rep_count > 1:
        share_size = token_block // rep_count
        share = sum(part.astype(jnp.float32) for part in parts).astype(jnp.bfloat16)
        share = share.reshape(requests, token_block, model_width)
        share = lax.psum_scatter(share, "rep", scatter_dimension=1, tiled=True)
        parts = [share.reshape(-1, model_width)]
        residual, ids, scores = (
            lax.dynamic_slice_in_dim(whole, core_place * share_size, share_size, 1)
            for whole in (residual, ids, scores)
        )
    own_hidden, normed = finish(
        parts,
        [first for _, first in gate_ups[1:]],
        residual.reshape(-1, model_width),
        norm_gain,
        ids.reshape(-1, ids.shape[2]).T,
        scores.reshape(-1, ids.shape[2]).T,
        expert_count,
    )
    own_hidden = own_hidden.reshape(requests, -1, model_width)
    if rep_count > 1:
        normed = normed.reshape(requests, share_size, -1)
        normed = lax.all_gather(normed, "rep", axis=1, tiled=True)
        normed = normed.reshape(token_count, -1)

    mixture = mixture_of(normed, weights)
    mixture = mixture.reshape(requests, token_block, model_width)
    if rep_count > 1:
        mixture = lax.psum_scatter(
            mixture.astype(jnp.bfloat16), "rep", scatter_dimension=1, tiled=True
        ).astype(jnp.float32)
    layer_out = (own_hidden.astype(jnp.float32) + mixture).astype(jnp.bfloat16)
    return (context, layer_out)


def solution(mesh):
    in_specs = (
        P("groups", "ctx", ("exp", "rep")),
        P("groups", "ctx", None, "exp"),
        P("groups", None),
        P("groups", ("ctx", "exp"), None),
        P(("exp", "rep"), None),
        P(),
        P("groups", ("ctx", "exp"), None),
        P("groups", ("ctx", "exp"), None),
        P(("ctx", "exp"), None, None, "rep"),
        P(("ctx", "exp"), "rep", None),
    )
    out_specs = (P("groups", "ctx", ("exp", "rep")), P("groups", ("ctx", "exp", "rep"), None))
    return jax.shard_map(
        per_device, mesh=mesh, in_specs=in_specs, out_specs=out_specs, check_vma=False
    )
```

```python
import functools

import jax
import jax.numpy as jnp
from jax import lax
from jax.experimental import pallas as pl
from jax.experimental.pallas import tpu as pltpu
from jax.sharding import PartitionSpec as P

HEAD = 128

floor_value = -1e30
norm_epsilon = 1e-06


def normalize(hidden, norm_gain):
    widened = hidden.astype(jnp.float32)
    mean_square = jnp.mean(widened * widened, axis=-1, keepdims=True)
    return (widened * lax.rsqrt(mean_square + norm_epsilon) * norm_gain).astype(jnp.bfloat16)


def strides(count):
    assert count & (count - 1) == 0
    return [1 << bit for bit in reversed(range(count.bit_length() - 1))]


def sum_order(held):
    offsets = [0]
    for stride in held:
        offsets = offsets + [offset ^ stride for offset in offsets]
    return offsets


def swap(value, axis, stride):
    return lax.ppermute(value, axis, [(i, i ^ stride) for i in range(lax.axis_size(axis))])


def shift(value, axis, step):
    count = lax.axis_size(axis)
    return lax.ppermute(value, axis, [(i, (i + step) % count) for i in range(count)])


def whole_specs(count):
    return [pl.BlockSpec(memory_space=pltpu.VMEM)] * count


SMEM_SPEC = pl.BlockSpec(memory_space=pltpu.SMEM)
LIMIT = pltpu.CompilerParams(vmem_limit_bytes=12 * 1024 * 1024)


def stack_heads(queries):
    heads = queries.shape[1] // HEAD
    return jnp.concatenate(
        [queries[:, h * HEAD : (h + 1) * HEAD] for h in range(heads)], axis=0
    )


def page_weights(stacked, keys, page, length, place, fresh_block):
    rows, page_size = stacked.shape[0], keys.shape[0]
    slab_size = page_size - fresh_block
    scores = lax.dot_general(
        keys, stacked, (((1,), (1,)), ((), ())), preferred_element_type=jnp.float32
    )
    lanes = HEAD if HEAD % fresh_block == 0 and rows % HEAD == 0 else rows
    offset = lax.broadcasted_iota(jnp.int32, (slab_size, lanes), 0)
    fresh = page * fresh_block + lax.broadcasted_iota(jnp.int32, (fresh_block, lanes), 0)
    lane = lax.broadcasted_iota(jnp.int32, (fresh_block, lanes), 1)
    position = place * fresh_block + lax.rem(lane, fresh_block)
    bias = jnp.concatenate(
        [
            jnp.where(offset < length, 0.0, floor_value),
            jnp.where(fresh <= position, 0.0, floor_value),
        ],
        axis=0,
    )
    masked = scores + jnp.concatenate([bias] * (rows // lanes), axis=1)
    peak = jnp.max(masked, axis=0, keepdims=True)
    weights = jnp.exp((masked - peak) * (HEAD**-0.5))
    total = jnp.sum(weights, axis=0, keepdims=True)
    return peak, total, weights.astype(jnp.bfloat16)


def weighted(values, weights):
    return lax.dot_general(
        values, weights, (((0,), (0,)), ((), ())), preferred_element_type=jnp.float32
    )


def page_partial(stacked, keys, values, page, length, place, fresh_block):
    peak, total, weights = page_weights(stacked, keys, page, length, place, fresh_block)
    return peak, total, weighted(values, weights)


def merge(first, second):
    peak = jnp.maximum(first[0], second[0])
    scale_first = jnp.exp((first[0] - peak) * (HEAD**-0.5))
    scale_second = jnp.exp((second[0] - peak) * (HEAD**-0.5))
    return (
        peak,
        first[1] * scale_first + second[1] * scale_second,
        first[2] * scale_first + second[2] * scale_second,
    )


def page_at(offset):
    count = lax.axis_size("ctx")
    return lax.rem(lax.axis_index("ctx") + offset + count, count)


def hold_kernel(weight, out):
    out[...] = jnp.zeros(out.shape, out.dtype)


def first_kernel(fresh_block, count, lengths, queries, keys, values, *refs):
    peak_out, total_out, summed_out, lengths_out = refs[-4:]
    for offset in range(count):
        lengths_out[offset : offset + 1, :] = jnp.full(
            (1, lengths_out.shape[1]), lengths[page_at(offset)], jnp.int32
        )
    place = lax.axis_index("ctx")
    peak_out[...], total_out[...], summed_out[...] = page_partial(
        stack_heads(queries[...]),
        keys[...],
        values[...],
        place,
        lengths[place],
        place,
        fresh_block,
    )


def middle_kernel(offsets, fresh_block, queries, lengths, *refs):
    count = len(offsets)
    pages, (peak, total, summed) = refs[: 2 * count], refs[2 * count : 2 * count + 3]
    outs = refs[2 * count + 3 :]
    stacked = stack_heads(queries[...])
    state = (peak[...], total[...], summed[...])
    for number, offset in enumerate(offsets):
        part = page_partial(
            stacked,
            pages[2 * number][...],
            pages[2 * number + 1][...],
            page_at(offset),
            lengths[offset : offset + 1, :],
            lax.axis_index("ctx"),
            fresh_block,
        )
        state = merge(state, part)
    for out, value in zip(outs, state):
        out[...] = value


def weights_kernel(offset, fresh_block, queries, keys, lengths, peak_out, total_out, weights_out):
    peak_out[...], total_out[...], weights_out[...] = page_weights(
        stack_heads(queries[...]),
        keys[...],
        page_at(offset),
        lengths[offset : offset + 1, :],
        lax.axis_index("ctx"),
        fresh_block,
    )


def late_kernel(
    fresh_block,
    values,
    last_peak,
    last_total,
    weights,
    peak,
    total,
    summed,
    weight,
    context_out,
    keep_out,
    *rest,
):
    send_out, blocks = rest[:-1], rest[-1]
    part = (last_peak[...], last_total[...], weighted(values[...], weights[...]))
    state = merge((peak[...], total[...], summed[...]), part)
    result = jnp.transpose(state[2] / state[1])
    context = jnp.concatenate(
        [
            result[h * fresh_block : (h + 1) * fresh_block]
            for h in range(result.shape[0] // fresh_block)
        ],
        axis=1,
    ).astype(jnp.bfloat16)
    context_out[...] = context
    blocks[...] = jnp.dot(context, weight[...], preferred_element_type=jnp.float32)
    place = lax.axis_index("exp")
    offsets = sum_order(strides(lax.axis_size("exp")))
    size = blocks.shape[0] // len(offsets)
    half = keep_out.shape[0] // size
    for number, offset in enumerate(offsets):
        index = place ^ offset
        value = blocks[pl.ds(pl.multiple_of(index * size, size), size), :]
        if number < half:
            keep_out[number * size : (number + 1) * size, :] = value
        else:
            low = (number - half) * size
            send_out[0][low : low + size, :] = value.astype(jnp.bfloat16)


def attention(queries, pages, lengths, out_weight, token_block):
    fresh_block, width = queries.shape
    rows = width // HEAD * fresh_block
    count = lax.axis_size("ctx")
    exp_count = lax.axis_size("exp")
    model_width = out_weight.shape[1]
    own_keys, own_values = pages[:, 0], pages[:, 1]
    weight_held = pl.pallas_call(
        hold_kernel,
        out_shape=jax.ShapeDtypeStruct((8, HEAD), jnp.float32),
        in_specs=[pl.BlockSpec(memory_space=pl.ANY)],
        out_specs=whole_specs(1)[0],
        compiler_params=LIMIT,
        cost_estimate=pl.CostEstimate(flops=4 << 30, bytes_accessed=4 << 20, transcendentals=0),
    )(out_weight)
    held = []
    left_keys, left_values = own_keys, own_values
    right_keys, right_values = own_keys, own_values
    for step in range(1, (count - 1) // 2 + 1):
        left_keys = shift(left_keys, "ctx", 1)
        right_values = shift(right_values, "ctx", -1)
        left_values, _ = lax.optimization_barrier((left_values, weight_held))
        left_values = shift(left_values, "ctx", 1)
        right_keys, _ = lax.optimization_barrier((right_keys, (left_keys, weight_held)))
        right_keys = shift(right_keys, "ctx", -1)
        held.append((count - step, left_keys, left_values))
        held.append((step, right_keys, right_values))
    if count % 2 == 0:
        last = (count // 2, shift(left_keys, "ctx", 1), shift(right_values, "ctx", -1))
    else:
        last = held.pop()
    page_flops = 4 * rows * pages.shape[0] * HEAD
    line = jax.ShapeDtypeStruct((1, rows), jnp.float32)
    partial_shape = (line, line, jax.ShapeDtypeStruct((HEAD, rows), jnp.float32))
    *state, page_lengths = pl.pallas_call(
        functools.partial(first_kernel, fresh_block, count),
        out_shape=partial_shape + (jax.ShapeDtypeStruct((count, HEAD), jnp.int32),),
        in_specs=[SMEM_SPEC]
        + whole_specs(3)
        + [pl.BlockSpec(memory_space=pl.ANY)],
        out_specs=tuple(whole_specs(4)),
        compiler_params=LIMIT,
        cost_estimate=pl.CostEstimate(
            flops=16 * page_flops, bytes_accessed=8 << 20, transcendentals=0
        ),
    )(lengths, queries, own_keys, own_values, weight_held)
    for start in range(0, len(held), 2):
        group = held[start : start + 2]
        operands = [part for _, keys, values in group for part in (keys, values)]
        state = pl.pallas_call(
            functools.partial(middle_kernel, [offset for offset, _, _ in group], fresh_block),
            out_shape=partial_shape,
            in_specs=whole_specs(5 + len(operands)),
            out_specs=tuple(whole_specs(3)),
            compiler_params=LIMIT,
            cost_estimate=pl.CostEstimate(
                flops=len(group) * page_flops, bytes_accessed=2 << 20, transcendentals=0
            ),
        )(queries, page_lengths, *operands, *state)
    half = (max(1, exp_count // 2) * token_block, model_width)
    shapes = [
        jax.ShapeDtypeStruct(queries.shape, jnp.bfloat16),
        jax.ShapeDtypeStruct(half, jnp.float32),
    ]
    if exp_count > 1:
        shapes.append(jax.ShapeDtypeStruct(half, jnp.bfloat16))
    last_weights = pl.pallas_call(
        functools.partial(weights_kernel, last[0], fresh_block),
        out_shape=(line, line, jax.ShapeDtypeStruct((pages.shape[0], rows), jnp.bfloat16)),
        in_specs=whole_specs(3),
        out_specs=tuple(whole_specs(3)),
        compiler_params=LIMIT,
        cost_estimate=pl.CostEstimate(
            flops=page_flops, bytes_accessed=1 << 20, transcendentals=0
        ),
    )(queries, last[1], page_lengths)
    outs = pl.pallas_call(
        functools.partial(late_kernel, fresh_block),
        out_shape=shapes,
        in_specs=whole_specs(8),
        out_specs=whole_specs(len(shapes)),
        scratch_shapes=[pltpu.VMEM((fresh_block, model_width), jnp.float32)],
        compiler_params=LIMIT,
        cost_estimate=pl.CostEstimate(
            flops=page_flops + 2 * fresh_block * width * model_width,
            bytes_accessed=6 << 20,
            transcendentals=0,
        ),
    )(last[2], *last_weights, *state, out_weight)
    return outs[0], outs[1], outs[2:]


def finish_kernel(count, *refs):
    parts, (residual, gain, ids, scores), (hidden_out, sent_out) = (
        refs[:count],
        refs[count : count + 4],
        refs[-2:],
    )
    total = residual[...].astype(jnp.float32)
    for part in parts:
        total = total + part[...].astype(jnp.float32)
    hidden = total.astype(jnp.bfloat16)
    hidden_out[...] = hidden
    width = hidden.shape[1]
    sent_out[:, :width] = normalize(hidden, gain[...])
    chosen = jnp.transpose(scores[...])
    ids = jnp.transpose(ids[...])
    combine = (chosen / jnp.sum(chosen, axis=1, keepdims=True)).astype(jnp.bfloat16)
    combine = combine.astype(jnp.float32)
    tokens, choices = chosen.shape
    expert = lax.broadcasted_iota(jnp.int32, (tokens, sent_out.shape[1] - width), 1)
    dense = jnp.zeros(expert.shape, jnp.float32)
    for k in range(choices):
        dense = dense + jnp.where(ids[:, k : k + 1] == expert, combine[:, k : k + 1], 0.0)
    sent_out[:, width:] = dense.astype(jnp.bfloat16)


def finish(parts, swapped, residual, norm_gain, ids, scores, expert_count):
    tokens, width = residual.shape
    lanes = -(-expert_count // 128) * 128
    return pl.pallas_call(
        functools.partial(finish_kernel, len(parts)),
        out_shape=(
            jax.ShapeDtypeStruct((tokens, width), jnp.bfloat16),
            jax.ShapeDtypeStruct((tokens, width + lanes), jnp.bfloat16),
        ),
        in_specs=whole_specs(len(parts) + 4)
        + [pl.BlockSpec(memory_space=pl.ANY)] * len(swapped),
        out_specs=tuple(whole_specs(2)),
        compiler_params=LIMIT,
        cost_estimate=pl.CostEstimate(
            flops=8 * residual.size, bytes_accessed=1 << 19, transcendentals=0
        ),
    )(*parts, residual, norm_gain[None], ids, scores, *swapped)


def down_kernel(offsets, rows, *refs):
    count = len(offsets)
    inners, downs, outs = refs[:count], refs[count : 2 * count], refs[2 * count :]
    dense = rows[:, outs[0].shape[1] :].astype(jnp.float32)
    lane = lax.broadcasted_iota(jnp.int32, dense.shape, 1)
    base = lax.axis_index("ctx") * lax.axis_size("exp")
    total = 0.0
    for offset, inner, down in zip(offsets, inners, downs):
        gate = inner[0]
        activated = (gate / (1.0 + jnp.exp(-gate)) * inner[1]).astype(jnp.bfloat16)
        piece = jnp.dot(activated, down[0], preferred_element_type=jnp.float32)
        expert = base + (lax.axis_index("exp") ^ offset)
        scale = jnp.sum(jnp.where(lane == expert, dense, 0.0), axis=1, keepdims=True)
        total = total + piece.astype(jnp.bfloat16).astype(jnp.float32) * scale
    start = 0
    for out in outs:
        out[...] = total[start : start + out.shape[0]].astype(out.dtype)
        start += out.shape[0]


def expert_apply(groups, kinds, weights):
    count = len(weights)
    rows = jnp.concatenate(groups, axis=0)
    _, hidden, width = weights[0][2].shape
    inners = [
        jnp.einsum("nd,dgh->gnh", rows[:, :width], gate_up[0], preferred_element_type=jnp.float32)
        for _, gate_up, _ in weights
    ]

    return pl.pallas_call(
        functools.partial(down_kernel, [offset for offset, _, _ in weights]),
        out_shape=[
            jax.ShapeDtypeStruct((group.shape[0], width), kind)
            for group, kind in zip(groups, kinds)
        ],
        in_specs=whole_specs(1 + 2 * count),
        out_specs=whole_specs(len(groups)),
        compiler_params=LIMIT,
        cost_estimate=pl.CostEstimate(
            flops=2 * count * rows.shape[0] * width * hidden,
            bytes_accessed=2 << 20,
            transcendentals=0,
        ),
    )(rows, *inners, *[down for _, _, down in weights])


def near_parts(part):
    held = [(0, part)]
    for stride in strides(lax.axis_size("exp"))[1:]:
        held = held + [(offset ^ stride, swap(first, "exp", stride)) for offset, first in held]
    return held


def chunks_of(count):
    chunks = [range((count + 1) // 2, count), range((count + 1) // 2)]
    return [list(chunk) for chunk in chunks if len(chunk)]


def mixture_of(rows, weights):
    tokens = rows.shape[0]
    far = strides(lax.axis_size("exp"))[:1]
    chunks = chunks_of(lax.axis_size("ctx"))

    joined = [
        jnp.concatenate(
            [rows if offset == 0 else swap(rows, "ctx", offset) for offset in chunk], axis=0
        )
        for chunk in chunks
    ]
    crossed = []
    for piece in joined if far else []:
        crossed.append(swap(piece, "exp", far[0]))
    *homes, first = expert_apply(
        joined + (crossed or joined)[:1], [jnp.float32] * len(joined) + [jnp.bfloat16], weights
    )
    total, arrived = None, []
    for number, (chunk, value) in enumerate(zip(chunks, homes)):
        if far:
            other = first
            if number:
                (other,) = expert_apply(crossed[number : number + 1], [jnp.bfloat16], weights)
            value = value + swap(other, "exp", far[0]).astype(jnp.float32)
        for position, offset in enumerate(chunk):
            block = value[position * tokens : (position + 1) * tokens]
            if offset == 0:
                total = block
            else:
                arrived.append(swap(block.astype(jnp.bfloat16), "ctx", offset))
    for block in arrived:
        total = total + block.astype(jnp.float32)
    return total


def per_device(
    queries,
    pages,
    cached_lengths,
    residual_in,
    out_weight,
    norm_gain,
    expert_ids,
    route_scores,
    expert_input,
    expert_output,
):
    requests = queries.shape[0]
    core_place = lax.axis_index("rep")
    rep_count = lax.axis_size("rep")
    exp_count = lax.axis_size("exp")
    expert_count = lax.axis_size("ctx") * exp_count
    token_block, model_width = residual_in.shape[1:]
    token_count = requests * token_block

    gate_ups = near_parts(expert_input)
    contexts, keeps, sends = [], [], []
    for r in range(requests):
        context, keep, send = attention(
            queries[r],
            pages[r],
            cached_lengths[r],
            out_weight,
            token_block,
        )
        contexts.append(context)
        keeps.append(keep)
        sends.extend(send)
    context = jnp.stack(contexts)

    by_block = lambda values: [value.reshape(-1, token_block, model_width) for value in values]
    parts = [jnp.stack(by_block(keeps), axis=1)]
    send = jnp.stack(by_block(sends), axis=1) if sends else None
    for stride in reversed(strides(exp_count)):
        arrived = swap(send, "exp", stride)
        if parts[0].shape[0] > 1:
            total = parts[0] + arrived.astype(jnp.float32)
            half = total.shape[0] // 2
            parts, send = [total[:half]], total[half:].astype(jnp.bfloat16)
        else:
            parts = [parts[0], arrived]
    downs = near_parts(lax.optimization_barrier((expert_output, parts[0]))[0])
    weights = [(offset, first, down) for (offset, first), (_, down) in zip(gate_ups, downs)]
    parts = [part.reshape(-1, model_width) for part in parts]
    residual, ids, scores = residual_in, expert_ids, route_scores
    if rep_count > 1:
        share_size = token_block // rep_count
        share = sum(part.astype(jnp.float32) for part in parts).astype(jnp.bfloat16)
        share = share.reshape(requests, token_block, model_width)
        share = lax.psum_scatter(share, "rep", scatter_dimension=1, tiled=True)
        parts = [share.reshape(-1, model_width)]
        residual, ids, scores = (
            lax.dynamic_slice_in_dim(whole, core_place * share_size, share_size, 1)
            for whole in (residual, ids, scores)
        )
    own_hidden, normed = finish(
        parts,
        [first for _, first in gate_ups[1:]],
        residual.reshape(-1, model_width),
        norm_gain,
        ids.reshape(-1, ids.shape[2]).T,
        scores.reshape(-1, ids.shape[2]).T,
        expert_count,
    )
    own_hidden = own_hidden.reshape(requests, -1, model_width)
    if rep_count > 1:
        normed = normed.reshape(requests, share_size, -1)
        normed = lax.all_gather(normed, "rep", axis=1, tiled=True)
        normed = normed.reshape(token_count, -1)

    mixture = mixture_of(normed, weights)
    mixture = mixture.reshape(requests, token_block, model_width)
    if rep_count > 1:
        mixture = lax.psum_scatter(
            mixture.astype(jnp.bfloat16), "rep", scatter_dimension=1, tiled=True
        ).astype(jnp.float32)
    layer_out = (own_hidden.astype(jnp.float32) + mixture).astype(jnp.bfloat16)
    return (context, layer_out)


def solution(mesh):
    in_specs = (
        P("groups", "ctx", ("exp", "rep")),
        P("groups", "ctx", None, "exp"),
        P("groups", None),
        P("groups", ("ctx", "exp"), None),
        P(("exp", "rep"), None),
        P(),
        P("groups", ("ctx", "exp"), None),
        P("groups", ("ctx", "exp"), None),
        P(("ctx", "exp"), None, None, "rep"),
        P(("ctx", "exp"), "rep", None),
    )
    out_specs = (P("groups", "ctx", ("exp", "rep")), P("groups", ("ctx", "exp", "rep"), None))
    return jax.shard_map(
        per_device, mesh=mesh, in_specs=in_specs, out_specs=out_specs, check_vma=False
    )
```

```python
import functools

import jax
import jax.numpy as jnp
from jax import lax
from jax.experimental import pallas as pl
from jax.experimental.pallas import tpu as pltpu
from jax.sharding import PartitionSpec as P

HEAD = 128

floor_value = -1e30
norm_epsilon = 1e-06


def normalize(hidden, norm_gain):
    widened = hidden.astype(jnp.float32)
    mean_square = jnp.mean(widened * widened, axis=-1, keepdims=True)
    return (widened * lax.rsqrt(mean_square + norm_epsilon) * norm_gain).astype(jnp.bfloat16)


def strides(count):
    assert count & (count - 1) == 0
    return [1 << bit for bit in reversed(range(count.bit_length() - 1))]


def sum_order(held):
    offsets = [0]
    for stride in held:
        offsets = offsets + [offset ^ stride for offset in offsets]
    return offsets


def swap(value, axis, stride):
    return lax.ppermute(value, axis, [(i, i ^ stride) for i in range(lax.axis_size(axis))])


def shift(value, axis, step):
    count = lax.axis_size(axis)
    return lax.ppermute(value, axis, [(i, (i + step) % count) for i in range(count)])


def whole_specs(count):
    return [pl.BlockSpec(memory_space=pltpu.VMEM)] * count


SMEM_SPEC = pl.BlockSpec(memory_space=pltpu.SMEM)
LIMIT = pltpu.CompilerParams(vmem_limit_bytes=12 * 1024 * 1024)


def stack_heads(queries):
    heads = queries.shape[1] // HEAD
    return jnp.concatenate(
        [queries[:, h * HEAD : (h + 1) * HEAD] for h in range(heads)], axis=0
    )


def page_weights(stacked, keys, page, length, place, fresh_block):
    rows, page_size = stacked.shape[0], keys.shape[0]
    slab_size = page_size - fresh_block
    scores = lax.dot_general(
        keys, stacked, (((1,), (1,)), ((), ())), preferred_element_type=jnp.float32
    )
    lanes = HEAD if HEAD % fresh_block == 0 and rows % HEAD == 0 else rows
    offset = lax.broadcasted_iota(jnp.int32, (slab_size, lanes), 0)
    fresh = page * fresh_block + lax.broadcasted_iota(jnp.int32, (fresh_block, lanes), 0)
    lane = lax.broadcasted_iota(jnp.int32, (fresh_block, lanes), 1)
    position = place * fresh_block + lax.rem(lane, fresh_block)
    bias = jnp.concatenate(
        [
            jnp.where(offset < length, 0.0, floor_value),
            jnp.where(fresh <= position, 0.0, floor_value),
        ],
        axis=0,
    )
    masked = scores + jnp.concatenate([bias] * (rows // lanes), axis=1)
    peak = jnp.max(masked, axis=0, keepdims=True)
    weights = jnp.exp((masked - peak) * (HEAD**-0.5))
    total = jnp.sum(weights, axis=0, keepdims=True)
    return peak, total, weights.astype(jnp.bfloat16)


def weighted(values, weights):
    return lax.dot_general(
        values, weights, (((0,), (0,)), ((), ())), preferred_element_type=jnp.float32
    )


def page_partial(stacked, keys, values, page, length, place, fresh_block):
    peak, total, weights = page_weights(stacked, keys, page, length, place, fresh_block)
    return peak, total, weighted(values, weights)


def merge(first, second):
    peak = jnp.maximum(first[0], second[0])
    scale_first = jnp.exp((first[0] - peak) * (HEAD**-0.5))
    scale_second = jnp.exp((second[0] - peak) * (HEAD**-0.5))
    return (
        peak,
        first[1] * scale_first + second[1] * scale_second,
        first[2] * scale_first + second[2] * scale_second,
    )


def page_at(offset):
    count = lax.axis_size("ctx")
    return lax.rem(lax.axis_index("ctx") + offset + count, count)


def hold_kernel(weight, out):
    out[...] = jnp.zeros(out.shape, out.dtype)


def first_kernel(fresh_block, count, lengths, queries, keys, values, *refs):
    peak_out, total_out, summed_out, lengths_out = refs[-4:]
    for offset in range(count):
        lengths_out[offset : offset + 1, :] = jnp.full(
            (1, lengths_out.shape[1]), lengths[page_at(offset)], jnp.int32
        )
    place = lax.axis_index("ctx")
    peak_out[...], total_out[...], summed_out[...] = page_partial(
        stack_heads(queries[...]),
        keys[...],
        values[...],
        place,
        lengths[place],
        place,
        fresh_block,
    )


def middle_kernel(offsets, fresh_block, queries, lengths, *refs):
    count = len(offsets)
    pages, (peak, total, summed) = refs[: 2 * count], refs[2 * count : 2 * count + 3]
    outs = refs[2 * count + 3 :]
    stacked = stack_heads(queries[...])
    state = (peak[...], total[...], summed[...])
    for number, offset in enumerate(offsets):
        part = page_partial(
            stacked,
            pages[2 * number][...],
            pages[2 * number + 1][...],
            page_at(offset),
            lengths[offset : offset + 1, :],
            lax.axis_index("ctx"),
            fresh_block,
        )
        state = merge(state, part)
    for out, value in zip(outs, state):
        out[...] = value


def weights_kernel(offset, fresh_block, queries, keys, lengths, peak_out, total_out, weights_out):
    peak_out[...], total_out[...], weights_out[...] = page_weights(
        stack_heads(queries[...]),
        keys[...],
        page_at(offset),
        lengths[offset : offset + 1, :],
        lax.axis_index("ctx"),
        fresh_block,
    )


def late_kernel(
    fresh_block,
    values,
    last_peak,
    last_total,
    weights,
    peak,
    total,
    summed,
    weight,
    context_out,
    keep_out,
    *rest,
):
    send_out, blocks = rest[:-1], rest[-1]
    part = (last_peak[...], last_total[...], weighted(values[...], weights[...]))
    state = merge((peak[...], total[...], summed[...]), part)
    result = jnp.transpose(state[2] / state[1])
    context = jnp.concatenate(
        [
            result[h * fresh_block : (h + 1) * fresh_block]
            for h in range(result.shape[0] // fresh_block)
        ],
        axis=1,
    ).astype(jnp.bfloat16)
    context_out[...] = context
    blocks[...] = jnp.dot(context, weight[...], preferred_element_type=jnp.float32)
    place = lax.axis_index("exp")
    offsets = sum_order(strides(lax.axis_size("exp")))
    size = blocks.shape[0] // len(offsets)
    half = keep_out.shape[0] // size
    for number, offset in enumerate(offsets):
        index = place ^ offset
        value = blocks[pl.ds(pl.multiple_of(index * size, size), size), :]
        if number < half:
            keep_out[number * size : (number + 1) * size, :] = value
        else:
            low = (number - half) * size
            send_out[0][low : low + size, :] = value.astype(jnp.bfloat16)


def attention(queries, pages, lengths, out_weight, token_block):
    fresh_block, width = queries.shape
    rows = width // HEAD * fresh_block
    count = lax.axis_size("ctx")
    exp_count = lax.axis_size("exp")
    model_width = out_weight.shape[1]
    own_keys, own_values = pages[:, 0], pages[:, 1]
    weight_held = pl.pallas_call(
        hold_kernel,
        out_shape=jax.ShapeDtypeStruct((8, HEAD), jnp.float32),
        in_specs=[pl.BlockSpec(memory_space=pl.ANY)],
        out_specs=whole_specs(1)[0],
        compiler_params=LIMIT,
        cost_estimate=pl.CostEstimate(flops=4 << 30, bytes_accessed=4 << 20, transcendentals=0),
    )(out_weight)
    held = []
    left_keys, left_values = own_keys, own_values
    right_keys, right_values = own_keys, own_values
    for step in range(1, (count - 1) // 2 + 1):
        left_keys = shift(left_keys, "ctx", 1)
        right_values = shift(right_values, "ctx", -1)
        left_values, _ = lax.optimization_barrier((left_values, weight_held))
        left_values = shift(left_values, "ctx", 1)
        right_keys, _ = lax.optimization_barrier((right_keys, (left_keys, weight_held)))
        right_keys = shift(right_keys, "ctx", -1)
        held.append((count - step, left_keys, left_values))
        held.append((step, right_keys, right_values))
    if count % 2 == 0:
        last = (count // 2, shift(left_keys, "ctx", 1), shift(right_values, "ctx", -1))
    else:
        last = held.pop()
    page_flops = 4 * rows * pages.shape[0] * HEAD
    line = jax.ShapeDtypeStruct((1, rows), jnp.float32)
    partial_shape = (line, line, jax.ShapeDtypeStruct((HEAD, rows), jnp.float32))
    *state, page_lengths = pl.pallas_call(
        functools.partial(first_kernel, fresh_block, count),
        out_shape=partial_shape + (jax.ShapeDtypeStruct((count, HEAD), jnp.int32),),
        in_specs=[SMEM_SPEC]
        + whole_specs(3)
        + [pl.BlockSpec(memory_space=pl.ANY)],
        out_specs=tuple(whole_specs(4)),
        compiler_params=LIMIT,
        cost_estimate=pl.CostEstimate(
            flops=16 * page_flops, bytes_accessed=8 << 20, transcendentals=0
        ),
    )(lengths, queries, own_keys, own_values, weight_held)
    for start in range(0, len(held), 2):
        group = held[start : start + 2]
        operands = [part for _, keys, values in group for part in (keys, values)]
        state = pl.pallas_call(
            functools.partial(middle_kernel, [offset for offset, _, _ in group], fresh_block),
            out_shape=partial_shape,
            in_specs=whole_specs(5 + len(operands)),
            out_specs=tuple(whole_specs(3)),
            compiler_params=LIMIT,
            cost_estimate=pl.CostEstimate(
                flops=len(group) * page_flops, bytes_accessed=2 << 20, transcendentals=0
            ),
        )(queries, page_lengths, *operands, *state)
    half = (max(1, exp_count // 2) * token_block, model_width)
    shapes = [
        jax.ShapeDtypeStruct(queries.shape, jnp.bfloat16),
        jax.ShapeDtypeStruct(half, jnp.float32),
    ]
    if exp_count > 1:
        shapes.append(jax.ShapeDtypeStruct(half, jnp.bfloat16))
    last_keys, _ = lax.optimization_barrier((last[1], state))
    last_weights = pl.pallas_call(
        functools.partial(weights_kernel, last[0], fresh_block),
        out_shape=(line, line, jax.ShapeDtypeStruct((pages.shape[0], rows), jnp.bfloat16)),
        in_specs=whole_specs(3),
        out_specs=tuple(whole_specs(3)),
        compiler_params=LIMIT,
        cost_estimate=pl.CostEstimate(
            flops=page_flops, bytes_accessed=1 << 20, transcendentals=0
        ),
    )(queries, last_keys, page_lengths)
    outs = pl.pallas_call(
        functools.partial(late_kernel, fresh_block),
        out_shape=shapes,
        in_specs=whole_specs(8),
        out_specs=whole_specs(len(shapes)),
        scratch_shapes=[pltpu.VMEM((fresh_block, model_width), jnp.float32)],
        compiler_params=LIMIT,
        cost_estimate=pl.CostEstimate(
            flops=page_flops + 2 * fresh_block * width * model_width,
            bytes_accessed=6 << 20,
            transcendentals=0,
        ),
    )(last[2], *last_weights, *state, out_weight)
    return outs[0], outs[1], outs[2:]


def finish_kernel(count, *refs):
    parts, (residual, gain, ids, scores), (hidden_out, sent_out) = (
        refs[:count],
        refs[count : count + 4],
        refs[-2:],
    )
    total = residual[...].astype(jnp.float32)
    for part in parts:
        total = total + part[...].astype(jnp.float32)
    hidden = total.astype(jnp.bfloat16)
    hidden_out[...] = hidden
    width = hidden.shape[1]
    sent_out[:, :width] = normalize(hidden, gain[...])
    chosen = jnp.transpose(scores[...])
    ids = jnp.transpose(ids[...])
    combine = (chosen / jnp.sum(chosen, axis=1, keepdims=True)).astype(jnp.bfloat16)
    combine = combine.astype(jnp.float32)
    tokens, choices = chosen.shape
    expert = lax.broadcasted_iota(jnp.int32, (tokens, sent_out.shape[1] - width), 1)
    dense = jnp.zeros(expert.shape, jnp.float32)
    for k in range(choices):
        dense = dense + jnp.where(ids[:, k : k + 1] == expert, combine[:, k : k + 1], 0.0)
    sent_out[:, width:] = dense.astype(jnp.bfloat16)


def finish(parts, swapped, residual, norm_gain, ids, scores, expert_count):
    tokens, width = residual.shape
    lanes = -(-expert_count // 128) * 128
    return pl.pallas_call(
        functools.partial(finish_kernel, len(parts)),
        out_shape=(
            jax.ShapeDtypeStruct((tokens, width), jnp.bfloat16),
            jax.ShapeDtypeStruct((tokens, width + lanes), jnp.bfloat16),
        ),
        in_specs=whole_specs(len(parts) + 4)
        + [pl.BlockSpec(memory_space=pl.ANY)] * len(swapped),
        out_specs=tuple(whole_specs(2)),
        compiler_params=LIMIT,
        cost_estimate=pl.CostEstimate(
            flops=8 * residual.size, bytes_accessed=1 << 19, transcendentals=0
        ),
    )(*parts, residual, norm_gain[None], ids, scores, *swapped)


def down_kernel(offsets, rows, *refs):
    count = len(offsets)
    inners, downs, outs = refs[:count], refs[count : 2 * count], refs[2 * count :]
    dense = rows[:, outs[0].shape[1] :].astype(jnp.float32)
    lane = lax.broadcasted_iota(jnp.int32, dense.shape, 1)
    base = lax.axis_index("ctx") * lax.axis_size("exp")
    total = 0.0
    for offset, inner, down in zip(offsets, inners, downs):
        gate = inner[0]
        activated = (gate / (1.0 + jnp.exp(-gate)) * inner[1]).astype(jnp.bfloat16)
        piece = jnp.dot(activated, down[0], preferred_element_type=jnp.float32)
        expert = base + (lax.axis_index("exp") ^ offset)
        scale = jnp.sum(jnp.where(lane == expert, dense, 0.0), axis=1, keepdims=True)
        total = total + piece.astype(jnp.bfloat16).astype(jnp.float32) * scale
    start = 0
    for out in outs:
        out[...] = total[start : start + out.shape[0]].astype(out.dtype)
        start += out.shape[0]


def expert_apply(groups, kinds, weights):
    count = len(weights)
    rows = jnp.concatenate(groups, axis=0)
    _, hidden, width = weights[0][2].shape
    inners = [
        jnp.einsum("nd,dgh->gnh", rows[:, :width], gate_up[0], preferred_element_type=jnp.float32)
        for _, gate_up, _ in weights
    ]

    return pl.pallas_call(
        functools.partial(down_kernel, [offset for offset, _, _ in weights]),
        out_shape=[
            jax.ShapeDtypeStruct((group.shape[0], width), kind)
            for group, kind in zip(groups, kinds)
        ],
        in_specs=whole_specs(1 + 2 * count),
        out_specs=whole_specs(len(groups)),
        compiler_params=LIMIT,
        cost_estimate=pl.CostEstimate(
            flops=2 * count * rows.shape[0] * width * hidden,
            bytes_accessed=2 << 20,
            transcendentals=0,
        ),
    )(rows, *inners, *[down for _, _, down in weights])


def near_parts(part):
    held = [(0, part)]
    for stride in strides(lax.axis_size("exp"))[1:]:
        held = held + [(offset ^ stride, swap(first, "exp", stride)) for offset, first in held]
    return held


def chunks_of(count):
    chunks = [range((count + 1) // 2, count), range((count + 1) // 2)]
    return [list(chunk) for chunk in chunks if len(chunk)]


def mixture_of(rows, weights):
    tokens = rows.shape[0]
    far = strides(lax.axis_size("exp"))[:1]
    chunks = chunks_of(lax.axis_size("ctx"))

    joined = [
        jnp.concatenate(
            [rows if offset == 0 else swap(rows, "ctx", offset) for offset in chunk], axis=0
        )
        for chunk in chunks
    ]
    crossed = []
    for piece in joined if far else []:
        crossed.append(swap(piece, "exp", far[0]))
    *homes, first = expert_apply(
        joined + (crossed or joined)[:1], [jnp.float32] * len(joined) + [jnp.bfloat16], weights
    )
    total, arrived = None, []
    for number, (chunk, value) in enumerate(zip(chunks, homes)):
        if far:
            other = first
            if number:
                (other,) = expert_apply(crossed[number : number + 1], [jnp.bfloat16], weights)
            value = value + swap(other, "exp", far[0]).astype(jnp.float32)
        for position, offset in enumerate(chunk):
            block = value[position * tokens : (position + 1) * tokens]
            if offset == 0:
                total = block
            else:
                arrived.append(swap(block.astype(jnp.bfloat16), "ctx", offset))
    for block in arrived:
        total = total + block.astype(jnp.float32)
    return total


def per_device(
    queries,
    pages,
    cached_lengths,
    residual_in,
    out_weight,
    norm_gain,
    expert_ids,
    route_scores,
    expert_input,
    expert_output,
):
    requests = queries.shape[0]
    core_place = lax.axis_index("rep")
    rep_count = lax.axis_size("rep")
    exp_count = lax.axis_size("exp")
    expert_count = lax.axis_size("ctx") * exp_count
    token_block, model_width = residual_in.shape[1:]
    token_count = requests * token_block

    gate_ups = near_parts(expert_input)
    contexts, keeps, sends = [], [], []
    for r in range(requests):
        context, keep, send = attention(
            queries[r],
            pages[r],
            cached_lengths[r],
            out_weight,
            token_block,
        )
        contexts.append(context)
        keeps.append(keep)
        sends.extend(send)
    context = jnp.stack(contexts)

    by_block = lambda values: [value.reshape(-1, token_block, model_width) for value in values]
    parts = [jnp.stack(by_block(keeps), axis=1)]
    send = jnp.stack(by_block(sends), axis=1) if sends else None
    for stride in reversed(strides(exp_count)):
        arrived = swap(send, "exp", stride)
        if parts[0].shape[0] > 1:
            total = parts[0] + arrived.astype(jnp.float32)
            half = total.shape[0] // 2
            parts, send = [total[:half]], total[half:].astype(jnp.bfloat16)
        else:
            parts = [parts[0], arrived]
    downs = near_parts(lax.optimization_barrier((expert_output, parts[0]))[0])
    weights = [(offset, first, down) for (offset, first), (_, down) in zip(gate_ups, downs)]
    parts = [part.reshape(-1, model_width) for part in parts]
    residual, ids, scores = residual_in, expert_ids, route_scores
    if rep_count > 1:
        share_size = token_block // rep_count
        share = sum(part.astype(jnp.float32) for part in parts).astype(jnp.bfloat16)
        share = share.reshape(requests, token_block, model_width)
        share = lax.psum_scatter(share, "rep", scatter_dimension=1, tiled=True)
        parts = [share.reshape(-1, model_width)]
        residual, ids, scores = (
            lax.dynamic_slice_in_dim(whole, core_place * share_size, share_size, 1)
            for whole in (residual, ids, scores)
        )
    own_hidden, normed = finish(
        parts,
        [first for _, first in gate_ups[1:]],
        residual.reshape(-1, model_width),
        norm_gain,
        ids.reshape(-1, ids.shape[2]).T,
        scores.reshape(-1, ids.shape[2]).T,
        expert_count,
    )
    own_hidden = own_hidden.reshape(requests, -1, model_width)
    if rep_count > 1:
        normed = normed.reshape(requests, share_size, -1)
        normed = lax.all_gather(normed, "rep", axis=1, tiled=True)
        normed = normed.reshape(token_count, -1)

    mixture = mixture_of(normed, weights)
    mixture = mixture.reshape(requests, token_block, model_width)
    if rep_count > 1:
        mixture = lax.psum_scatter(
            mixture.astype(jnp.bfloat16), "rep", scatter_dimension=1, tiled=True
        ).astype(jnp.float32)
    layer_out = (own_hidden.astype(jnp.float32) + mixture).astype(jnp.bfloat16)
    return (context, layer_out)


def solution(mesh):
    in_specs = (
        P("groups", "ctx", ("exp", "rep")),
        P("groups", "ctx", None, "exp"),
        P("groups", None),
        P("groups", ("ctx", "exp"), None),
        P(("exp", "rep"), None),
        P(),
        P("groups", ("ctx", "exp"), None),
        P("groups", ("ctx", "exp"), None),
        P(("ctx", "exp"), None, None, "rep"),
        P(("ctx", "exp"), "rep", None),
    )
    out_specs = (P("groups", "ctx", ("exp", "rep")), P("groups", ("ctx", "exp", "rep"), None))
    return jax.shard_map(
        per_device, mesh=mesh, in_specs=in_specs, out_specs=out_specs, check_vma=False
    )
```

```python
import functools

import jax
import jax.numpy as jnp
from jax import lax
from jax.experimental import pallas as pl
from jax.experimental.pallas import tpu as pltpu
from jax.sharding import PartitionSpec as P

HEAD = 128

floor_value = -1e30
norm_epsilon = 1e-06


def normalize(hidden, norm_gain):
    widened = hidden.astype(jnp.float32)
    mean_square = jnp.mean(widened * widened, axis=-1, keepdims=True)
    return (widened * lax.rsqrt(mean_square + norm_epsilon) * norm_gain).astype(jnp.bfloat16)


def strides(count):
    assert count & (count - 1) == 0
    return [1 << bit for bit in reversed(range(count.bit_length() - 1))]


def sum_order(held):
    offsets = [0]
    for stride in held:
        offsets = offsets + [offset ^ stride for offset in offsets]
    return offsets


def swap(value, axis, stride):
    return lax.ppermute(value, axis, [(i, i ^ stride) for i in range(lax.axis_size(axis))])


def shift(value, axis, step):
    count = lax.axis_size(axis)
    return lax.ppermute(value, axis, [(i, (i + step) % count) for i in range(count)])


def whole_specs(count):
    return [pl.BlockSpec(memory_space=pltpu.VMEM)] * count


SMEM_SPEC = pl.BlockSpec(memory_space=pltpu.SMEM)
LIMIT = pltpu.CompilerParams(vmem_limit_bytes=12 * 1024 * 1024)


def stack_heads(queries):
    heads = queries.shape[1] // HEAD
    return jnp.concatenate(
        [queries[:, h * HEAD : (h + 1) * HEAD] for h in range(heads)], axis=0
    )


def page_weights(stacked, keys, page, length, place, fresh_block):
    rows, page_size = stacked.shape[0], keys.shape[0]
    slab_size = page_size - fresh_block
    scores = lax.dot_general(
        keys, stacked, (((1,), (1,)), ((), ())), preferred_element_type=jnp.float32
    )
    lanes = HEAD if HEAD % fresh_block == 0 and rows % HEAD == 0 else rows
    offset = lax.broadcasted_iota(jnp.int32, (slab_size, lanes), 0)
    fresh = page * fresh_block + lax.broadcasted_iota(jnp.int32, (fresh_block, lanes), 0)
    lane = lax.broadcasted_iota(jnp.int32, (fresh_block, lanes), 1)
    position = place * fresh_block + lax.rem(lane, fresh_block)
    bias = jnp.concatenate(
        [
            jnp.where(offset < length, 0.0, floor_value),
            jnp.where(fresh <= position, 0.0, floor_value),
        ],
        axis=0,
    )
    masked = scores + jnp.concatenate([bias] * (rows // lanes), axis=1)
    peak = jnp.max(masked, axis=0, keepdims=True)
    weights = jnp.exp((masked - peak) * (HEAD**-0.5))
    total = jnp.sum(weights, axis=0, keepdims=True)
    return peak, total, weights.astype(jnp.bfloat16)


def weighted(values, weights):
    return lax.dot_general(
        values, weights, (((0,), (0,)), ((), ())), preferred_element_type=jnp.float32
    )


def page_partial(stacked, keys, values, page, length, place, fresh_block):
    peak, total, weights = page_weights(stacked, keys, page, length, place, fresh_block)
    return peak, total, weighted(values, weights)


def merge(first, second):
    peak = jnp.maximum(first[0], second[0])
    scale_first = jnp.exp((first[0] - peak) * (HEAD**-0.5))
    scale_second = jnp.exp((second[0] - peak) * (HEAD**-0.5))
    return (
        peak,
        first[1] * scale_first + second[1] * scale_second,
        first[2] * scale_first + second[2] * scale_second,
    )


def page_at(offset):
    count = lax.axis_size("ctx")
    return lax.rem(lax.axis_index("ctx") + offset + count, count)


def hold_kernel(weight, out):
    out[...] = jnp.zeros(out.shape, out.dtype)


def first_kernel(fresh_block, count, lengths, queries, keys, values, *refs):
    peak_out, total_out, summed_out, lengths_out = refs[-4:]
    for offset in range(count):
        lengths_out[offset : offset + 1, :] = jnp.full(
            (1, lengths_out.shape[1]), lengths[page_at(offset)], jnp.int32
        )
    place = lax.axis_index("ctx")
    peak_out[...], total_out[...], summed_out[...] = page_partial(
        stack_heads(queries[...]),
        keys[...],
        values[...],
        place,
        lengths[place],
        place,
        fresh_block,
    )


def middle_kernel(offsets, fresh_block, queries, lengths, *refs):
    count = len(offsets)
    pages, (peak, total, summed) = refs[: 2 * count], refs[2 * count : 2 * count + 3]
    outs = refs[2 * count + 3 :]
    stacked = stack_heads(queries[...])
    state = (peak[...], total[...], summed[...])
    for number, offset in enumerate(offsets):
        part = page_partial(
            stacked,
            pages[2 * number][...],
            pages[2 * number + 1][...],
            page_at(offset),
            lengths[offset : offset + 1, :],
            lax.axis_index("ctx"),
            fresh_block,
        )
        state = merge(state, part)
    for out, value in zip(outs, state):
        out[...] = value


def weights_kernel(offset, fresh_block, queries, keys, lengths, peak_out, total_out, weights_out):
    peak_out[...], total_out[...], weights_out[...] = page_weights(
        stack_heads(queries[...]),
        keys[...],
        page_at(offset),
        lengths[offset : offset + 1, :],
        lax.axis_index("ctx"),
        fresh_block,
    )


def late_kernel(
    fresh_block,
    values,
    last_peak,
    last_total,
    weights,
    peak,
    total,
    summed,
    weight,
    context_out,
    keep_out,
    *rest,
):
    send_out, blocks = rest[:-1], rest[-1]
    part = (last_peak[...], last_total[...], weighted(values[...], weights[...]))
    state = merge((peak[...], total[...], summed[...]), part)
    result = jnp.transpose(state[2] / state[1])
    context = jnp.concatenate(
        [
            result[h * fresh_block : (h + 1) * fresh_block]
            for h in range(result.shape[0] // fresh_block)
        ],
        axis=1,
    ).astype(jnp.bfloat16)
    context_out[...] = context
    blocks[...] = jnp.dot(context, weight[...], preferred_element_type=jnp.float32)
    place = lax.axis_index("exp")
    offsets = sum_order(strides(lax.axis_size("exp")))
    size = blocks.shape[0] // len(offsets)
    half = keep_out.shape[0] // size
    for number, offset in enumerate(offsets):
        index = place ^ offset
        value = blocks[pl.ds(pl.multiple_of(index * size, size), size), :]
        if number < half:
            keep_out[number * size : (number + 1) * size, :] = value
        else:
            low = (number - half) * size
            send_out[0][low : low + size, :] = value.astype(jnp.bfloat16)


def attention(queries, pages, lengths, out_weight, token_block):
    fresh_block, width = queries.shape
    rows = width // HEAD * fresh_block
    count = lax.axis_size("ctx")
    exp_count = lax.axis_size("exp")
    model_width = out_weight.shape[1]
    own_keys, own_values = pages[:, 0], pages[:, 1]
    weight_held = pl.pallas_call(
        hold_kernel,
        out_shape=jax.ShapeDtypeStruct((8, HEAD), jnp.float32),
        in_specs=[pl.BlockSpec(memory_space=pl.ANY)],
        out_specs=whole_specs(1)[0],
        compiler_params=LIMIT,
        cost_estimate=pl.CostEstimate(flops=4 << 30, bytes_accessed=4 << 20, transcendentals=0),
    )(out_weight)
    held = []
    left_keys, left_values = own_keys, own_values
    right_keys, right_values = own_keys, own_values
    for step in range(1, (count - 1) // 2 + 1):
        left_keys = shift(left_keys, "ctx", 1)
        right_values = shift(right_values, "ctx", -1)
        left_values, _ = lax.optimization_barrier((left_values, weight_held))
        left_values = shift(left_values, "ctx", 1)
        right_keys, _ = lax.optimization_barrier((right_keys, (left_keys, weight_held)))
        right_keys = shift(right_keys, "ctx", -1)
        held.append((count - step, left_keys, left_values))
        held.append((step, right_keys, right_values))
    if count % 2 == 0:
        last = (count // 2, shift(left_keys, "ctx", 1), shift(right_values, "ctx", -1))
    else:
        last = held.pop()
    page_flops = 4 * rows * pages.shape[0] * HEAD
    line = jax.ShapeDtypeStruct((1, rows), jnp.float32)
    partial_shape = (line, line, jax.ShapeDtypeStruct((HEAD, rows), jnp.float32))
    *state, page_lengths = pl.pallas_call(
        functools.partial(first_kernel, fresh_block, count),
        out_shape=partial_shape + (jax.ShapeDtypeStruct((count, HEAD), jnp.int32),),
        in_specs=[SMEM_SPEC]
        + whole_specs(3)
        + [pl.BlockSpec(memory_space=pl.ANY)],
        out_specs=tuple(whole_specs(4)),
        compiler_params=LIMIT,
        cost_estimate=pl.CostEstimate(
            flops=16 * page_flops, bytes_accessed=8 << 20, transcendentals=0
        ),
    )(lengths, queries, own_keys, own_values, weight_held)
    for start in range(0, len(held), 2):
        group = held[start : start + 2]
        operands = [part for _, keys, values in group for part in (keys, values)]
        state = pl.pallas_call(
            functools.partial(middle_kernel, [offset for offset, _, _ in group], fresh_block),
            out_shape=partial_shape,
            in_specs=whole_specs(5 + len(operands)),
            out_specs=tuple(whole_specs(3)),
            compiler_params=LIMIT,
            cost_estimate=pl.CostEstimate(
                flops=len(group) * page_flops, bytes_accessed=2 << 20, transcendentals=0
            ),
        )(queries, page_lengths, *operands, *state)
    half = (max(1, exp_count // 2) * token_block, model_width)
    shapes = [
        jax.ShapeDtypeStruct(queries.shape, jnp.bfloat16),
        jax.ShapeDtypeStruct(half, jnp.float32),
    ]
    if exp_count > 1:
        shapes.append(jax.ShapeDtypeStruct(half, jnp.bfloat16))
    last_keys, _ = lax.optimization_barrier((last[1], state))
    last_weights = pl.pallas_call(
        functools.partial(weights_kernel, last[0], fresh_block),
        out_shape=(line, line, jax.ShapeDtypeStruct((pages.shape[0], rows), jnp.bfloat16)),
        in_specs=whole_specs(3),
        out_specs=tuple(whole_specs(3)),
        compiler_params=LIMIT,
        cost_estimate=pl.CostEstimate(
            flops=page_flops, bytes_accessed=1 << 20, transcendentals=0
        ),
    )(queries, last_keys, page_lengths)
    outs = pl.pallas_call(
        functools.partial(late_kernel, fresh_block),
        out_shape=shapes,
        in_specs=whole_specs(8),
        out_specs=whole_specs(len(shapes)),
        scratch_shapes=[pltpu.VMEM((fresh_block, model_width), jnp.float32)],
        compiler_params=LIMIT,
        cost_estimate=pl.CostEstimate(
            flops=page_flops + 2 * fresh_block * width * model_width,
            bytes_accessed=6 << 20,
            transcendentals=0,
        ),
    )(last[2], *last_weights, *state, out_weight)
    return outs[0], outs[1], outs[2:]


def finish_kernel(count, *refs):
    parts, (residual, gain, ids, scores), (hidden_out, sent_out) = (
        refs[:count],
        refs[count : count + 4],
        refs[-2:],
    )
    total = residual[...].astype(jnp.float32)
    for part in parts:
        total = total + part[...].astype(jnp.float32)
    hidden = total.astype(jnp.bfloat16)
    hidden_out[...] = hidden
    width = hidden.shape[1]
    sent_out[:, :width] = normalize(hidden, gain[...])
    chosen = jnp.transpose(scores[...])
    ids = jnp.transpose(ids[...])
    combine = (chosen / jnp.sum(chosen, axis=1, keepdims=True)).astype(jnp.bfloat16)
    combine = combine.astype(jnp.float32)
    tokens, choices = chosen.shape
    expert = lax.broadcasted_iota(jnp.int32, (tokens, sent_out.shape[1] - width), 1)
    dense = jnp.zeros(expert.shape, jnp.float32)
    for k in range(choices):
        dense = dense + jnp.where(ids[:, k : k + 1] == expert, combine[:, k : k + 1], 0.0)
    sent_out[:, width:] = dense.astype(jnp.bfloat16)


def finish(parts, swapped, residual, norm_gain, ids, scores, expert_count):
    tokens, width = residual.shape
    lanes = -(-expert_count // 128) * 128
    return pl.pallas_call(
        functools.partial(finish_kernel, len(parts)),
        out_shape=(
            jax.ShapeDtypeStruct((tokens, width), jnp.bfloat16),
            jax.ShapeDtypeStruct((tokens, width + lanes), jnp.bfloat16),
        ),
        in_specs=whole_specs(len(parts) + 4)
        + [pl.BlockSpec(memory_space=pl.ANY)] * len(swapped),
        out_specs=tuple(whole_specs(2)),
        compiler_params=LIMIT,
        cost_estimate=pl.CostEstimate(
            flops=8 * residual.size, bytes_accessed=1 << 19, transcendentals=0
        ),
    )(*parts, residual, norm_gain[None], ids, scores, *swapped)


def down_kernel(offsets, rows, *refs):
    count = len(offsets)
    inners, downs, outs = refs[:count], refs[count : 2 * count], refs[2 * count :]
    dense = rows[:, outs[0].shape[1] :].astype(jnp.float32)
    lane = lax.broadcasted_iota(jnp.int32, dense.shape, 1)
    base = lax.axis_index("ctx") * lax.axis_size("exp")
    total = 0.0
    for offset, inner, down in zip(offsets, inners, downs):
        gate = inner[0]
        activated = (gate / (1.0 + jnp.exp(-gate)) * inner[1]).astype(jnp.bfloat16)
        piece = jnp.dot(activated, down[0], preferred_element_type=jnp.float32)
        expert = base + (lax.axis_index("exp") ^ offset)
        scale = jnp.sum(jnp.where(lane == expert, dense, 0.0), axis=1, keepdims=True)
        total = total + piece.astype(jnp.bfloat16).astype(jnp.float32) * scale
    start = 0
    for out in outs:
        out[...] = total[start : start + out.shape[0]].astype(out.dtype)
        start += out.shape[0]


def expert_apply(groups, kinds, weights):
    count = len(weights)
    rows = jnp.concatenate(groups, axis=0)
    _, hidden, width = weights[0][2].shape
    inners = [
        jnp.einsum("nd,dgh->gnh", rows[:, :width], gate_up[0], preferred_element_type=jnp.float32)
        for _, gate_up, _ in weights
    ]

    return pl.pallas_call(
        functools.partial(down_kernel, [offset for offset, _, _ in weights]),
        out_shape=[
            jax.ShapeDtypeStruct((group.shape[0], width), kind)
            for group, kind in zip(groups, kinds)
        ],
        in_specs=whole_specs(1 + 2 * count),
        out_specs=whole_specs(len(groups)),
        compiler_params=LIMIT,
        cost_estimate=pl.CostEstimate(
            flops=2 * count * rows.shape[0] * width * hidden,
            bytes_accessed=2 << 20,
            transcendentals=0,
        ),
    )(rows, *inners, *[down for _, _, down in weights])


def near_parts(part):
    held = [(0, part)]
    for stride in strides(lax.axis_size("exp"))[1:]:
        held = held + [(offset ^ stride, swap(first, "exp", stride)) for offset, first in held]
    return held


def chunks_of(count):
    chunks = [range((count + 1) // 2, count), range((count + 1) // 2)]
    return [list(chunk) for chunk in chunks if len(chunk)]


def mixture_of(rows, weights):
    tokens = rows.shape[0]
    far = strides(lax.axis_size("exp"))[:1]
    chunks = chunks_of(lax.axis_size("ctx"))

    blocks = [
        [rows if offset == 0 else swap(rows, "ctx", offset) for offset in chunk]
        for chunk in chunks
    ]
    joined = [jnp.concatenate(parts, axis=0) for parts in blocks]
    crossed = []
    if far:
        near = swap(joined[-1], "exp", far[0])
        for parts in blocks[:-1]:
            parts[0], _ = lax.optimization_barrier((parts[0], near))
            crossed.append(jnp.concatenate([swap(part, "exp", far[0]) for part in parts], axis=0))
        crossed.append(near)
    *homes, first = expert_apply(
        joined + (crossed or joined)[:1], [jnp.float32] * len(joined) + [jnp.bfloat16], weights
    )
    total, arrived = None, []
    for number, (chunk, value) in enumerate(zip(chunks, homes)):
        if far:
            other = first
            if number:
                (other,) = expert_apply(crossed[number : number + 1], [jnp.bfloat16], weights)
            value = value + swap(other, "exp", far[0]).astype(jnp.float32)
        for position, offset in enumerate(chunk):
            block = value[position * tokens : (position + 1) * tokens]
            if offset == 0:
                total = block
            else:
                arrived.append(swap(block.astype(jnp.bfloat16), "ctx", offset))
    for block in arrived:
        total = total + block.astype(jnp.float32)
    return total


def per_device(
    queries,
    pages,
    cached_lengths,
    residual_in,
    out_weight,
    norm_gain,
    expert_ids,
    route_scores,
    expert_input,
    expert_output,
):
    requests = queries.shape[0]
    core_place = lax.axis_index("rep")
    rep_count = lax.axis_size("rep")
    exp_count = lax.axis_size("exp")
    expert_count = lax.axis_size("ctx") * exp_count
    token_block, model_width = residual_in.shape[1:]
    token_count = requests * token_block

    gate_ups = near_parts(expert_input)
    contexts, keeps, sends = [], [], []
    for r in range(requests):
        context, keep, send = attention(
            queries[r],
            pages[r],
            cached_lengths[r],
            out_weight,
            token_block,
        )
        contexts.append(context)
        keeps.append(keep)
        sends.extend(send)
    context = jnp.stack(contexts)

    by_block = lambda values: [value.reshape(-1, token_block, model_width) for value in values]
    parts = [jnp.stack(by_block(keeps), axis=1)]
    send = jnp.stack(by_block(sends), axis=1) if sends else None
    for stride in reversed(strides(exp_count)):
        arrived = swap(send, "exp", stride)
        if parts[0].shape[0] > 1:
            total = parts[0] + arrived.astype(jnp.float32)
            half = total.shape[0] // 2
            parts, send = [total[:half]], total[half:].astype(jnp.bfloat16)
        else:
            parts = [parts[0], arrived]
    downs = near_parts(lax.optimization_barrier((expert_output, parts[0]))[0])
    weights = [(offset, first, down) for (offset, first), (_, down) in zip(gate_ups, downs)]
    parts = [part.reshape(-1, model_width) for part in parts]
    residual, ids, scores = residual_in, expert_ids, route_scores
    if rep_count > 1:
        share_size = token_block // rep_count
        share = sum(part.astype(jnp.float32) for part in parts).astype(jnp.bfloat16)
        share = share.reshape(requests, token_block, model_width)
        share = lax.psum_scatter(share, "rep", scatter_dimension=1, tiled=True)
        parts = [share.reshape(-1, model_width)]
        residual, ids, scores = (
            lax.dynamic_slice_in_dim(whole, core_place * share_size, share_size, 1)
            for whole in (residual, ids, scores)
        )
    own_hidden, normed = finish(
        parts,
        [first for _, first in gate_ups[1:]],
        residual.reshape(-1, model_width),
        norm_gain,
        ids.reshape(-1, ids.shape[2]).T,
        scores.reshape(-1, ids.shape[2]).T,
        expert_count,
    )
    own_hidden = own_hidden.reshape(requests, -1, model_width)
    if rep_count > 1:
        normed = normed.reshape(requests, share_size, -1)
        normed = lax.all_gather(normed, "rep", axis=1, tiled=True)
        normed = normed.reshape(token_count, -1)

    mixture = mixture_of(normed, weights)
    mixture = mixture.reshape(requests, token_block, model_width)
    if rep_count > 1:
        mixture = lax.psum_scatter(
            mixture.astype(jnp.bfloat16), "rep", scatter_dimension=1, tiled=True
        ).astype(jnp.float32)
    layer_out = (own_hidden.astype(jnp.float32) + mixture).astype(jnp.bfloat16)
    return (context, layer_out)


def solution(mesh):
    in_specs = (
        P("groups", "ctx", ("exp", "rep")),
        P("groups", "ctx", None, "exp"),
        P("groups", None),
        P("groups", ("ctx", "exp"), None),
        P(("exp", "rep"), None),
        P(),
        P("groups", ("ctx", "exp"), None),
        P("groups", ("ctx", "exp"), None),
        P(("ctx", "exp"), None, None, "rep"),
        P(("ctx", "exp"), "rep", None),
    )
    out_specs = (P("groups", "ctx", ("exp", "rep")), P("groups", ("ctx", "exp", "rep"), None))
    return jax.shard_map(
        per_device, mesh=mesh, in_specs=in_specs, out_specs=out_specs, check_vma=False
    )
```
